32 devices in a mesh: wide: 8 (over y, x, core), narrow: 4 (over z).
Axes of the slice: x: 2, y: 2, z: 4, core: 2. Of those that a mesh axis runs over, the one named last changes fastest.
Arguments:
- tokens: bfloat16 [32, 2048, 768], P(('wide', 'narrow')), may hold values from -6 to 6
- cotangent: bfloat16 [32, 2048, 768], P(('wide', 'narrow')), may hold values from -6 to 6
- lengths: int32 [32], P(('wide', 'narrow')), may hold values from 256 to 1024
- levels: int32 [32, 64], P(('wide', 'narrow')), may hold values from 0 to 7
- owners: int32 [4], replicated, may hold values from 0 to 7, as said below
- master_slots: float32 [8, 3072, 768], P('wide', 'narrow')
- moment_slots: float32 [8, 3072, 768], P('wide', 'narrow'), may hold values from -0.001953125 to 0.001953125
- square_slots: float32 [8, 3072, 768], P('wide', 'narrow'), may hold values from 7.052775e-08 to 1.128444e-06
- vec_master: float32 [15, 768], replicated
- vec_moment: float32 [15, 768], replicated, may hold values from -0.001953125 to 0.001953125
- vec_square: float32 [15, 768], replicated, may hold values from 7.052775e-08 to 1.128444e-06
Outputs:
- output: bfloat16 [32, 2048, 768], P(('wide', 'narrow'))
- input_grad: float32 [32, 2048, 768], P(('wide', 'narrow'))
- master_new_slots: float32 [8, 3072, 768], P('wide', 'narrow')
- moment_new_slots: float32 [8, 3072, 768], P('wide', 'narrow')
- square_new_slots: float32 [8, 3072, 768], P('wide', 'narrow')
- vec_grad: float32 [15, 768], replicated
- vec_moment_new: float32 [15, 768], replicated
- vec_square_new: float32 [15, 768], replicated
- vec_master_new: float32 [15, 768], replicated
- grad_norm: float32 [1], replicated
The draws below stay inside these ranges and needn't reach their ends.
Inputs may be any that keep to these rules, and one draw needn't show every extreme that they name: Four different indices of wide, the owners of the query-key-value, output, up and down projections in this order.
All inputs are finite; a program needn't handle non-finite values.
Results may differ from the reference program's by a relative error of at most 0.014.
The reference program's roundings to bfloat16 on the way count: a program that leaves them out, or rounds other values in their place, can miss the bound.
Values may be sent and summed in bfloat16 or wider, within the bound.
No kernel may reach another device: no remote copies, remote signals or barrier semaphores. Data moves between devices by JAX's collectives and lax.ppermute only.
A program may use at most 320 MiB of HBM per device.

```python
import math
import jax
import jax.numpy as jnp
from jax import lax

D = 768
HEADS = 12
HEAD_DIM = 64
FF = 3072
BLOCK = 16
SEQ = 1024
LEVELS = 8
STEP = 10
SEQS = 32
VROWS = 15
PARAMS = 7089408
N_WIDE = 8
N_NARROW = 4


def owner_list(key):
    subkeys = jax.random.split(jax.random.fold_in(key, 11), 2)
    inner = jax.random.permutation(subkeys[0], N_WIDE - 2)[:2].astype(jnp.int32) + 1
    values = jnp.concatenate([jnp.array([0, N_WIDE - 1], jnp.int32), inner])
    order = jax.random.permutation(subkeys[1], 4)
    return values[order]


def draw_owners(key, part):
    return owner_list(key)


def draw_master_slots(key, part):
    owners = owner_list(key)
    slot_index = jnp.arange(N_WIDE, dtype=jnp.int32)
    scale = jnp.full((N_WIDE,), D ** (-0.5), jnp.float32)
    scale = jnp.where(slot_index == owners[0], (D // 2) ** (-0.5), scale)
    scale = jnp.where(slot_index == owners[1], (D // 32) ** (-0.5), scale)
    scale = jnp.where(slot_index == owners[2], D ** (-0.5), scale)
    scale = jnp.where(slot_index == owners[3], FF ** (-0.5), scale)
    base = jax.random.normal(jax.random.fold_in(key, 12), (N_WIDE, FF, D), jnp.float32)
    return (base * scale[:, None, None]).astype(jnp.float32)


def draw_vec_master(key, part):
    subkeys = jax.random.split(jax.random.fold_in(key, 7), 3)
    ramp_up = jnp.exp(jnp.log(3.0) * (jnp.arange(D, dtype=jnp.float32) / D - 0.5))
    factors = jax.random.uniform(subkeys[0], (2, D), jnp.float32, 0.75, 1.33)
    gains = ramp_up[None, :] * factors
    biases = 0.3 * jax.random.normal(subkeys[1], (1 + FF // D, D), jnp.float32)
    table_rows = 0.5 * jax.random.normal(subkeys[2], (LEVELS, D), jnp.float32)
    return jnp.concatenate([gains, biases, table_rows], axis=0).astype(jnp.float32)


def plant(values, key, smallest, high):
    dims = values.shape
    index_at = [jax.random.randint(jax.random.fold_in(key, axis), (), 0, dims[axis]) for axis in range(len(dims))]
    values = values.at[tuple(index_at)].set(smallest)
    longest = dims.index(max(dims))
    index_at[longest] = (index_at[longest] + 1) % dims[longest]
    return values.at[tuple(index_at)].set(high)


def level_of(rng, dims, cuts, smallest, high):
    level, own = 1.0, jax.random.fold_in(rng, 6)
    for dim, shards_of in cuts:
        draws = jnp.exp(jax.random.uniform(jax.random.fold_in(own, dim), (shards_of,), jnp.float32, smallest / len(cuts), high / len(cuts)))
        level = level * jnp.repeat(draws, dims[dim] // shards_of).reshape([-1 if axis == dim else 1 for axis in range(len(dims))])
    return level


def noise(key, dims, scale, reach, cuts=(), kind=jnp.bfloat16):
    drawn = scale * jax.random.normal(key, dims, jnp.float32)
    if cuts:
        drawn = drawn * level_of(key, dims, cuts, -0.22, 0.18)
    return jnp.clip(drawn, -reach, reach).astype(kind)


def setup_inputs(seed: int = 0) -> dict:
    seeds = jax.random.split(jax.random.key(seed), 12)
    tokens = noise(seeds[0], (SEQS, 2 * SEQ, D), 1.0, 6.0, ((0, 32),))
    cotangent = noise(seeds[1], (SEQS, 2 * SEQ, D), 1.0, 6.0, ((0, 32),))
    lengths = plant(jax.random.randint(seeds[2], (SEQS,), SEQ // 4, SEQ + 1), jax.random.fold_in(seeds[2], 1), SEQ // 4, SEQ).astype(jnp.int32)
    levels = plant(jax.random.randint(seeds[3], (SEQS, SEQ // BLOCK), 0, LEVELS), jax.random.fold_in(seeds[3], 1), 0, LEVELS - 1).astype(jnp.int32)
    owners = draw_owners(jax.random.fold_in(seeds[11], 71), 0)
    master_slots = draw_master_slots(jax.random.fold_in(seeds[11], 71), 0)
    moment_slots = noise(seeds[6], (N_WIDE, FF, D), (PARAMS ** -0.5), 0.001953125, ((0, 8), (1, 4)), jnp.float32)
    square_slots = jnp.clip(jnp.exp(math.log(1.1284439551673131e-06) - 2.7725887 * jax.random.uniform(seeds[7], (N_WIDE, FF, D), jnp.float32) ** level_of(seeds[7], (N_WIDE, FF, D), ((0, 8), (1, 4)), -0.2, 0.2)), 7.052774719795707e-08, 1.1284439551673131e-06)
    vec_master = draw_vec_master(jax.random.fold_in(seeds[11], 71), 0)
    vec_moment = noise(seeds[9], (VROWS, D), (PARAMS ** -0.5), 0.001953125, (), jnp.float32)
    vec_square = jnp.clip(jnp.exp(jax.random.uniform(seeds[10], (VROWS, D), jnp.float32, math.log(7.052774719795707e-08), math.log(1.1284439551673131e-06))), 7.052774719795707e-08, 1.1284439551673131e-06)
    return {"tokens": tokens, "cotangent": cotangent, "lengths": lengths, "levels": levels, "owners": owners, "master_slots": master_slots, "moment_slots": moment_slots, "square_slots": square_slots, "vec_master": vec_master, "vec_moment": vec_moment, "vec_square": vec_square}


ln_eps = 1e-05
learn_rate = 0.05
vector_rate = 0.5
decay_rate = 0.1
moment_decay = 0.5
adam_eps = 1e-08
masked_score = -1e+30
rope_base = 10000.0
highest = lax.Precision.HIGHEST

@jax.custom_vjp
def low(v):
    return lax.optimization_barrier(v.astype(jnp.bfloat16)).astype(jnp.float32)

@jax.custom_vjp
def low_back(v):
    return v

def low_keep(v):
    return (low(v), None)

def low_pass(kept, grad):
    return (grad,)

def back_keep(v):
    return (v, None)

def back_low(kept, grad):
    return (low(grad),)
low.defvjp(low_keep, low_pass)
low_back.defvjp(back_keep, back_low)

def matrix_shapes():
    return ((D, 3 * D), (D, D), (D, FF), (FF, D))

def unpack(slots, owner, shape):
    rows, cols = shape
    slot = slots[owner]
    slot_rows = FF // N_NARROW
    count = rows * cols // (N_NARROW * D)
    pieces = [slot[index_n * slot_rows:index_n * slot_rows + count].reshape(rows // N_NARROW, cols) for index_n in range(N_NARROW)]
    return jnp.concatenate(pieces, axis=0)

def pack(total, owner, matrix):
    rows, cols = matrix.shape
    slot_rows = FF // N_NARROW
    count = rows * cols // (N_NARROW * D)
    pieces = []
    for index_n in range(N_NARROW):
        share = matrix[index_n * (rows // N_NARROW):(index_n + 1) * (rows // N_NARROW)].reshape(count, D)
        pieces.append(jnp.concatenate([share, jnp.zeros((slot_rows - count, D), matrix.dtype)], axis=0))
    return total.at[owner].set(jnp.concatenate(pieces, axis=0))

def layer_norm(entries, gain):
    centred = entries - lax.optimization_barrier(jnp.mean(entries, axis=-1, keepdims=True))
    scaling = lax.rsqrt(lax.optimization_barrier(jnp.mean(centred * centred, axis=-1, keepdims=True)) + ln_eps)
    return centred * scaling * gain

def rope_tables(row_count, head_dim):
    positions = (jnp.arange(row_count, dtype=jnp.int32) % SEQ).astype(jnp.float32)
    exponents = jnp.arange(head_dim // 2, dtype=jnp.float32) * (2.0 / head_dim)
    angles = positions[:, None] * (rope_base ** (-exponents))[None, :]
    return (jnp.cos(angles)[:, None, :], jnp.sin(angles)[:, None, :])

def rotate(entries, cos_table, sin_table):
    half_dim = entries.shape[-1] // 2
    front_half = entries[..., :half_dim]
    back_half = entries[..., half_dim:]
    return jnp.concatenate([front_half * cos_table - back_half * sin_table, back_half * cos_table + front_half * sin_table], axis=-1)

def attention(query_heads, key_heads, value_heads, length):
    row_count = 2 * SEQ
    block_rows = min(512, SEQ // 2)
    key_index = jnp.arange(row_count, dtype=jnp.int32)
    key_noised = key_index < SEQ
    key_block = key_index % SEQ // BLOCK
    key_kept = key_index % SEQ < length
    scaling = HEAD_DIM ** (-0.5)

    def one_block(block_index):
        row_start = block_index * block_rows
        queries = lax.dynamic_slice_in_dim(query_heads, row_start, block_rows, 0)
        query_index = row_start + jnp.arange(block_rows, dtype=jnp.int32)
        query_noised = (query_index < SEQ)[:, None]
        query_block = (query_index % SEQ // BLOCK)[:, None]
        same = query_noised & key_noised[None, :] & (query_block == key_block[None, :])
        earlier = query_noised & (~key_noised)[None, :] & (key_block[None, :] < query_block)
        causal = ~query_noised & (~key_noised)[None, :] & (key_block[None, :] <= query_block)
        visible = (same | earlier | causal) & (key_kept[None, :] | (query_index[:, None] == key_index[None, :]))
        scores = low_back(jnp.einsum('qhd,khd->hqk', queries, key_heads, precision=highest) * scaling)
        scores = jnp.where(visible[None], scores, masked_score)
        row_max = lax.optimization_barrier(jnp.max(scores, axis=-1, keepdims=True))
        expo = jnp.exp(scores - row_max)
        probs = low(expo / lax.optimization_barrier(jnp.sum(expo, axis=-1, keepdims=True)))
        return jnp.einsum('hqk,khd->qhd', probs, value_heads, precision=highest)
    blocks = lax.map(jax.checkpoint(one_block), jnp.arange(row_count // block_rows, dtype=jnp.int32))
    return blocks.reshape(row_count, HEADS * HEAD_DIM)

def layer(inputs, w_qkv, w_out, w_up, w_down, vectors, length, level_ids):
    gain_one = vectors[0]
    gain_two = vectors[1]
    down_bias = vectors[2]
    up_bias = vectors[3:3 + FF // D].reshape(FF)
    table_rows = vectors[3 + FF // D:]
    level_rows = jnp.repeat(table_rows[level_ids], BLOCK, axis=0)
    hidden = inputs + jnp.concatenate([level_rows, jnp.zeros_like(level_rows)], axis=0)
    attn_in = low(layer_norm(hidden, gain_one))
    projected = low_back(jnp.dot(attn_in, low(w_qkv), precision=highest)).reshape(2 * SEQ, 3, HEADS, HEAD_DIM)
    cos_table, sin_table = rope_tables(2 * SEQ, HEAD_DIM)
    query_heads = low(rotate(projected[:, 0], cos_table, sin_table))
    key_heads = low(rotate(projected[:, 1], cos_table, sin_table))
    value_heads = low(projected[:, 2])
    attended = low(low_back(attention(query_heads, key_heads, value_heads, length)))
    attn_out = low_back(jnp.dot(attended, low(w_out), precision=highest))
    resid = hidden + attn_out
    mlp_in = low(layer_norm(resid, gain_two))
    pre_act = low_back(jnp.dot(mlp_in, low(w_up), precision=highest)) + up_bias
    activated = low(jax.nn.gelu(pre_act, approximate=True))
    mlp_out = low_back(jnp.dot(activated, low(w_down), precision=highest))
    return resid + mlp_out + down_bias

def adam(grad, moment, square, master, decay, rate):
    moment_new = moment_decay * moment + (1.0 - moment_decay) * grad
    square_new = moment_decay * square + (1.0 - moment_decay) * grad * grad
    correction = 1.0 - moment_decay ** STEP
    master_new = master * (1.0 - rate * decay) - rate * (moment_new / correction) / (jnp.sqrt(square_new / correction) + adam_eps)
    return (moment_new, square_new, master_new)

def reference(tokens, cotangent, lengths, levels, owners, master_slots, moment_slots, square_slots, vec_master, vec_moment, vec_square):
    shapes = matrix_shapes()
    matrices = tuple((unpack(master_slots, owners[index_k], shapes[index_k]) for index_k in range(4)))
    masters = matrices + (vec_master,)

    def one_sequence(carry, item):
        inputs, grad_out, length, level_ids = item

        def forward(entries, w_qkv, w_out, w_up, w_down, vectors):
            return layer(entries, w_qkv, w_out, w_up, w_down, vectors, length, level_ids)
        result, backward = jax.vjp(forward, inputs.astype(jnp.float32), *masters)
        grads = backward(grad_out.astype(jnp.float32))
        carry = tuple((total + grad for total, grad in zip(carry, grads[1:])))
        return (carry, (result.astype(jnp.bfloat16), grads[0]))
    start = tuple((jnp.zeros_like(master) for master in masters))
    sums, (output, input_grad) = lax.scan(one_sequence, start, (tokens, cotangent, lengths, levels))
    row_scale = 1.0 / (2 * SEQ)
    scaled = tuple((total * row_scale for total in sums))
    norm_value = jnp.sqrt(sum((jnp.sum(grad * grad) for grad in scaled)))
    clip_factor = jnp.minimum(1.0, 1.0 / (norm_value + 1e-06))
    clipped = tuple((grad * clip_factor for grad in scaled))
    master_out = jnp.zeros_like(master_slots)
    moment_out = jnp.zeros_like(moment_slots)
    square_out = jnp.zeros_like(square_slots)
    for index_k in range(4):
        moment_old = unpack(moment_slots, owners[index_k], shapes[index_k])
        square_old = unpack(square_slots, owners[index_k], shapes[index_k])
        moment_new, square_new, master_new = adam(clipped[index_k], moment_old, square_old, matrices[index_k], decay_rate, learn_rate)
        master_out = pack(master_out, owners[index_k], master_new)
        moment_out = pack(moment_out, owners[index_k], moment_new)
        square_out = pack(square_out, owners[index_k], square_new)
    vec_moment_new, vec_square_new, vec_master_new = adam(clipped[4], vec_moment, vec_square, vec_master, 0.0, vector_rate)
    return (output, input_grad, master_out, moment_out, square_out, clipped[4], vec_moment_new, vec_square_new, vec_master_new, norm_value.reshape(1))
```

```python
from functools import partial

import jax
import jax.numpy as jnp
from jax import lax
from jax.experimental import pallas as pl
from jax.experimental.pallas import tpu as pltpu
from jax.sharding import PartitionSpec as P

D = 768
HEADS = 12
HEAD_DIM = 64
FF = 3072
BLOCK = 16
SEQ = 1024
LEVELS = 8
STEP = 10
ROWS = 2 * SEQ

ln_eps = 1e-05
learn_rate = 0.05
vector_rate = 0.5
decay_rate = 0.1
moment_decay = 0.5
adam_eps = 1e-08
masked_score = -1e30
rope_base = 10000.0
row_scale = 1.0 / (2 * SEQ)

TILE = 256
PAIR = 2 * HEAD_DIM
GROUPS = HEADS // 2
UP_ROWS = FF // D
VROWS = 3 + UP_ROWS + LEVELS
low = jnp.bfloat16
full = jnp.float32


def dot(a, b, dim_a=1, dim_b=0):
    return lax.dot_general(
        a, b, (((dim_a,), (dim_b,)), ((), ())), preferred_element_type=full
    )


def params(limit=56):
    return pltpu.CompilerParams(vmem_limit_bytes=limit * 2**20)


def whole(shape):
    zeros = (0,) * len(shape)
    return pl.BlockSpec(shape, lambda *_: zeros, pipeline_mode=pl.Buffered(1))


def rows_of(width):
    return pl.BlockSpec((TILE, width), lambda i, *_: (i, 0))


def hidden_tile(levels_ref, tokens_ref, vec_ref):
    step = pl.program_id(0)
    per_tile = TILE // BLOCK
    first = lax.rem(step, SEQ // TILE) * per_tile
    rows = []
    for block in range(per_tile):
        level = levels_ref[first + block]
        row = vec_ref[pl.ds(3 + UP_ROWS + level, 1), :]
        rows.append(jnp.broadcast_to(row, (BLOCK, D)))
    embedding = jnp.concatenate(rows, axis=0)
    noised = step < SEQ // TILE
    return tokens_ref[...].astype(full) + jnp.where(noised, embedding, 0.0)


def normalised(entries):
    centred = entries - jnp.mean(entries, axis=-1, keepdims=True)
    scaling = lax.rsqrt(jnp.mean(centred * centred, axis=-1, keepdims=True) + ln_eps)
    return centred * scaling, scaling


def norm_back(normed, scaling, gain, grad):
    inner = grad * gain
    return (
        inner
        - jnp.mean(inner, axis=-1, keepdims=True)
        - normed * jnp.mean(inner * normed, axis=-1, keepdims=True)
    ) * scaling


def eight_rows(entries):
    return entries.reshape(-1, 8, entries.shape[-1]).sum(axis=0)


def norm_one_kernel(levels_ref, tokens_ref, vec_ref, out_ref):
    normed, _ = normalised(hidden_tile(levels_ref, tokens_ref, vec_ref))
    out_ref[...] = (normed * vec_ref[0:1, :]).astype(low)


def norm_one(levels, tokens, vec_master):
    return pl.pallas_call(
        norm_one_kernel,
        grid_spec=pltpu.PrefetchScalarGridSpec(
            num_scalar_prefetch=1,
            grid=(ROWS // TILE,),
            in_specs=[rows_of(D), whole((VROWS, D))],
            out_specs=rows_of(D),
        ),
        out_shape=jax.ShapeDtypeStruct((ROWS, D), low),
        cost_estimate=pl.CostEstimate(
            flops=10 * ROWS * D, bytes_accessed=4 * ROWS * D, transcendentals=0
        ),
        compiler_params=params(),
        name="norm_one",
    )(levels, tokens, vec_master)


def turn(entries, cos, sin):
    return entries * cos + pltpu.roll(entries, HEAD_DIM, 1) * sin


def project_kernel(a_ref, w_ref, cos_ref, sin_ref, out_ref):
    a = a_ref[...]
    cos = cos_ref[...]
    sin = sin_ref[...]
    for part in range(3):
        projected = dot(a, w_ref[:, part * D : (part + 1) * D])
        if part < 2:
            for group in range(GROUPS):
                columns = slice(group * PAIR, (group + 1) * PAIR)
                turned = turn(projected[:, columns], cos, sin).astype(low)
                if part == 0:
                    turned = (turned.astype(full) * HEAD_DIM**-0.5).astype(low)
                out_ref[:, part * D + group * PAIR : part * D + (group + 1) * PAIR] = turned
        else:
            out_ref[:, 2 * D :] = projected.astype(low)


def project(attn_in, w_qkv, cos, sin):
    table = pl.BlockSpec((TILE, PAIR), lambda i: (lax.rem(i, SEQ // TILE), 0))
    return pl.pallas_call(
        project_kernel,
        grid=(ROWS // TILE,),
        in_specs=[rows_of(D), whole((D, 3 * D)), table, table],
        out_specs=rows_of(3 * D),
        out_shape=jax.ShapeDtypeStruct((ROWS, 3 * D), low),
        cost_estimate=pl.CostEstimate(
            flops=6 * ROWS * D * D, bytes_accessed=8 * ROWS * D, transcendentals=0
        ),
        compiler_params=params(),
        name="project",
    )(attn_in, w_qkv, cos, sin)


QT = 256
TILES = SEQ // QT


def fill_bias(length, same_ref, earlier_ref, causal_ref, length_ref):
    key = lax.broadcasted_iota(jnp.int32, (QT, QT), 0)
    query = lax.broadcasted_iota(jnp.int32, (QT, QT), 1)
    key_block = key // BLOCK
    query_block = query // BLOCK
    for tile in range(TILES):
        kept = key + tile * QT < length
        own = kept | (key == query)
        same_ref[tile] = jnp.where((key_block == query_block) & own, 0.0, masked_score)
        earlier_ref[tile] = jnp.where((key_block < query_block) & kept, 0.0, masked_score)
        causal_ref[tile] = jnp.where((key_block <= query_block) & own, 0.0, masked_score)
    position = lax.broadcasted_iota(jnp.int32, (SEQ, QT), 0)
    length_ref[...] = jnp.where(position < length, 0.0, masked_score)


bias_scratch = [
    pltpu.VMEM((TILES, QT, QT), full),
    pltpu.VMEM((TILES, QT, QT), full),
    pltpu.VMEM((TILES, QT, QT), full),
    pltpu.VMEM((SEQ, QT), full),
]


def segments(tile, noised):
    found = []
    if noised:
        found.append((tile * QT, QT, "same"))
        found.append((SEQ + tile * QT, QT, "earlier"))
    else:
        found.append((SEQ + tile * QT, QT, "causal"))
    if tile > 1:
        found.append((SEQ + QT, (tile - 1) * QT, "length"))
    if tile > 0:
        found.append((SEQ, QT, None))
    return found


def masked(scores, kind, tile, start, count, biases):
    same_ref, earlier_ref, causal_ref, length_ref = biases
    if kind == "same":
        return scores + same_ref[tile]
    if kind == "earlier":
        return scores + earlier_ref[tile]
    if kind == "causal":
        return scores + causal_ref[tile]
    if kind == "length":
        return scores + length_ref[start - SEQ : start - SEQ + count, :]
    return scores


def lane_masks(head, rows):
    lane = lax.broadcasted_iota(jnp.int32, (rows, PAIR), 1)
    halves = (lane // (HEAD_DIM // 2)) % 2 == head
    plain = lane // HEAD_DIM == head
    return halves, plain


def attend_kernel(length_ref, q_ref, k_ref, v_ref, o_ref, log_ref, *biases):
    @pl.when(pl.program_id(0) == 0)
    def _():
        fill_bias(length_ref[0], *biases)

    def one_head(head, carry):
        halves, plain = lane_masks(head, QT)
        for tile in range(TILES):
            for noised in (True, False):
                row = tile * QT + (0 if noised else SEQ)
                query = jnp.where(halves, q_ref[row : row + QT, :], jnp.zeros((), low))
                parts = []
                row_max = None
                for start, count, kind in segments(tile, noised):
                    scores = dot(k_ref[start : start + count, :], query, 1, 1)
                    scores = masked(scores, kind, tile, start, count, biases)
                    parts.append((start, count, scores))
                    top = jnp.max(scores, axis=0, keepdims=True)
                    row_max = top if row_max is None else jnp.maximum(row_max, top)
                total = None
                attended = None
                for start, count, scores in parts:
                    expo = jnp.exp(scores - row_max)
                    part_total = jnp.sum(expo, axis=0, keepdims=True)
                    product = dot(expo.astype(low), v_ref[start : start + count, :], 0, 0)
                    total = part_total if total is None else total + part_total
                    attended = product if attended is None else attended + product
                inverse = jnp.transpose(jnp.broadcast_to(1.0 / total, (PAIR, QT)))
                result = (attended * inverse).astype(low)
                o_ref[row : row + QT, :] = jnp.where(plain, result, o_ref[row : row + QT, :])
                log_ref[0, pl.ds(head, 1), row : row + QT] = row_max + jnp.log(total)
        return carry

    lax.fori_loop(0, 2, one_head, 0)


def column_spec(offset):
    return pl.BlockSpec((ROWS, PAIR), lambda g, *_: (0, offset + g))


log_spec = pl.BlockSpec((1, 2, ROWS), lambda g, *_: (g, 0, 0))
PAIRS_SEEN = 1572864


def attend(length, qkv):
    return pl.pallas_call(
        attend_kernel,
        grid_spec=pltpu.PrefetchScalarGridSpec(
            num_scalar_prefetch=1,
            grid=(GROUPS,),
            in_specs=[column_spec(0), column_spec(GROUPS), column_spec(2 * GROUPS)],
            out_specs=[column_spec(0), log_spec],
            scratch_shapes=bias_scratch,
        ),
        out_shape=[
            jax.ShapeDtypeStruct((ROWS, D), low),
            jax.ShapeDtypeStruct((GROUPS, 2, ROWS), full),
        ],
        cost_estimate=pl.CostEstimate(
            flops=16 * PAIRS_SEEN * D, bytes_accessed=8 * ROWS * D, transcendentals=0
        ),
        compiler_params=params(),
        name="attend",
    )(length, qkv, qkv, qkv)


def attend_back_kernel(
    length_ref, q_ref, k_ref, v_ref, o_ref, grad_ref, log_ref, cos_ref, sin_ref,
    dq_ref, dk_ref, dv_ref, q_acc, k_acc, v_acc, delta_acc, *biases
):
    @pl.when(pl.program_id(0) == 0)
    def _():
        fill_bias(length_ref[0], *biases)

    k_acc[...] = jnp.zeros_like(k_acc)
    v_acc[...] = jnp.zeros_like(v_acc)
    for row in range(0, ROWS, QT):
        product = o_ref[row : row + QT, :].astype(full) * grad_ref[row : row + QT, :].astype(full)
        turned = jnp.transpose(product)
        delta_acc[0:1, row : row + QT] = jnp.sum(turned[:HEAD_DIM], axis=0, keepdims=True)
        delta_acc[1:2, row : row + QT] = jnp.sum(turned[HEAD_DIM:], axis=0, keepdims=True)

    def one_head(head, carry):
        halves, plain = lane_masks(head, QT)
        for tile in range(TILES):
            for noised in (True, False):
                row = tile * QT + (0 if noised else SEQ)
                zero = jnp.zeros((), low)
                query = jnp.where(halves, q_ref[row : row + QT, :], zero)
                grad = jnp.where(plain, grad_ref[row : row + QT, :], zero)
                log_total = log_ref[0, pl.ds(head, 1), row : row + QT]
                delta = delta_acc[pl.ds(head, 1), row : row + QT]
                query_grad = None
                for start, count, kind in segments(tile, noised):
                    keys = k_ref[start : start + count, :]
                    scores = dot(keys, query, 1, 1)
                    scores = masked(scores, kind, tile, start, count, biases)
                    probs = jnp.exp(scores - log_total)
                    prob_grad = dot(v_ref[start : start + count, :], grad, 1, 1)
                    score_grad = (probs * (prob_grad - delta)).astype(low)
                    v_acc[start : start + count, :] += dot(probs.astype(low), grad)
                    k_acc[start : start + count, :] += dot(score_grad, query)
                    part = dot(score_grad, keys, 0, 0)
                    query_grad = part if query_grad is None else query_grad + part
                q_acc[row : row + QT, :] = jnp.where(
                    halves, query_grad, q_acc[row : row + QT, :]
                )
        return carry

    lax.fori_loop(0, 2, one_head, 0)
    for row in range(0, ROWS, QT):
        rows = slice(row, row + QT)
        cos = cos_ref[row % SEQ : row % SEQ + QT, :]
        sin = -sin_ref[row % SEQ : row % SEQ + QT, :]
        dq_ref[rows, :] = turn(q_acc[rows, :] * HEAD_DIM**-0.5, cos, sin).astype(low)
        dk_ref[rows, :] = turn(k_acc[rows, :], cos, sin).astype(low)
        dv_ref[rows, :] = v_acc[rows, :].astype(low)


def attend_back(length, qkv, attended, grad, logs, cos, sin):
    table = whole((SEQ, PAIR))
    out = jax.ShapeDtypeStruct((ROWS, D), low)
    return pl.pallas_call(
        attend_back_kernel,
        grid_spec=pltpu.PrefetchScalarGridSpec(
            num_scalar_prefetch=1,
            grid=(GROUPS,),
            in_specs=[
                column_spec(0), column_spec(GROUPS), column_spec(2 * GROUPS),
                column_spec(0), column_spec(0), log_spec, table, table,
            ],
            out_specs=[column_spec(0)] * 3,
            scratch_shapes=[
                pltpu.VMEM((ROWS, PAIR), full),
                pltpu.VMEM((ROWS, PAIR), full),
                pltpu.VMEM((ROWS, PAIR), full),
                pltpu.VMEM((8, ROWS), full),
                *bias_scratch,
            ],
        ),
        out_shape=[out, out, out],
        cost_estimate=pl.CostEstimate(
            flops=40 * PAIRS_SEEN * D, bytes_accessed=16 * ROWS * D, transcendentals=0
        ),
        compiler_params=params(),
        name="attend_back",
    )(length, qkv, qkv, qkv, attended, grad, logs, cos, sin)


root_two_pi = 0.7978845608028654
cubic = 0.044715


def feed_kernel(
    levels_ref, tokens_ref, o_ref, dy_ref, vec_ref, out_w, up_w, down_w,
    y_ref, b_ref, gl_ref, du_ref, dr_ref, drb_ref, do_ref, sums_ref, upsum_ref
):
    @pl.when(pl.program_id(0) == 0)
    def _():
        sums_ref[...] = jnp.zeros_like(sums_ref)
        upsum_ref[...] = jnp.zeros_like(upsum_ref)

    gain = vec_ref[1:2, :]
    resid = hidden_tile(levels_ref, tokens_ref, vec_ref) + dot(o_ref[...], out_w[...])
    normed, scaling = normalised(resid)
    mlp_in = (normed * gain).astype(low)
    b_ref[...] = mlp_in
    dy = dy_ref[...]
    result = resid + vec_ref[2:3, :]
    back = jnp.zeros((TILE, D), full)
    for part in range(UP_ROWS):
        columns = slice(part * D, (part + 1) * D)
        pre = dot(mlp_in, up_w[:, columns]) + vec_ref[3 + part : 4 + part, :]
        square = pre * pre
        bent = jnp.tanh(root_two_pi * (pre + cubic * (pre * square)))
        half = 0.5 * (1.0 + bent)
        act = (pre * half).astype(low)
        slope = half + 0.5 * pre * (1.0 - bent * bent) * (
            root_two_pi + (3.0 * cubic * root_two_pi) * square
        )
        gl_ref[:, columns] = act
        result = result + dot(act, down_w[columns, :])
        pre_grad = dot(dy, down_w[columns, :], 1, 1) * slope
        upsum_ref[:, columns] += eight_rows(pre_grad)
        pre_low = pre_grad.astype(low)
        du_ref[:, columns] = pre_low
        back = back + dot(pre_low, up_w[:, columns], 1, 1)
    y_ref[...] = result.astype(low)
    dy_full = dy.astype(full)
    sums_ref[0:8, :] += eight_rows(back * normed)
    sums_ref[8:16, :] += eight_rows(dy_full)
    resid_grad = dy_full + norm_back(normed, scaling, gain, back)
    dr_ref[...] = resid_grad
    resid_low = resid_grad.astype(low)
    drb_ref[...] = resid_low
    do_ref[...] = dot(resid_low, out_w[...], 1, 1).astype(low)


def feed(levels, tokens, attended, cotangent, vec_master, w_out, w_up, w_down):
    def out(width, kind=low):
        return jax.ShapeDtypeStruct((ROWS, width), kind)

    return pl.pallas_call(
        feed_kernel,
        grid_spec=pltpu.PrefetchScalarGridSpec(
            num_scalar_prefetch=1,
            grid=(ROWS // TILE,),
            in_specs=[
                rows_of(D), rows_of(D), rows_of(D), whole((VROWS, D)),
                whole((D, D)), whole((D, FF)), whole((FF, D)),
            ],
            out_specs=[
                rows_of(D), rows_of(D), rows_of(FF), rows_of(FF), rows_of(D), rows_of(D),
                rows_of(D),
                pl.BlockSpec((16, D), lambda i, *_: (0, 0)),
                pl.BlockSpec((8, FF), lambda i, *_: (0, 0)),
            ],
        ),
        out_shape=[
            out(D), out(D), out(FF), out(FF), out(D, full), out(D), out(D),
            jax.ShapeDtypeStruct((16, D), full), jax.ShapeDtypeStruct((8, FF), full),
        ],
        cost_estimate=pl.CostEstimate(
            flops=ROWS * D * (4 * D + 8 * FF), bytes_accessed=30 * ROWS * D, transcendentals=0
        ),
        compiler_params=params(),
        name="feed",
    )(levels, tokens, attended, cotangent, vec_master, w_out, w_up, w_down)


def weight_kernel(x_ref, y_ref, out_ref):
    out_ref[...] = (dot(x_ref[...], y_ref[...], 0, 0) * row_scale).astype(low)


def weight_grad(x, y, block_x, block_y):
    wide_x, wide_y = x.shape[1], y.shape[1]
    return pl.pallas_call(
        weight_kernel,
        grid=(wide_x // block_x, wide_y // block_y),
        in_specs=[
            pl.BlockSpec((ROWS, block_x), lambda i, j: (0, i)),
            pl.BlockSpec((ROWS, block_y), lambda i, j: (0, j)),
        ],
        out_specs=pl.BlockSpec((block_x, block_y), lambda i, j: (i, j)),
        out_shape=jax.ShapeDtypeStruct((wide_x, wide_y), low),
        cost_estimate=pl.CostEstimate(
            flops=2 * ROWS * wide_x * wide_y,
            bytes_accessed=2 * ROWS * (wide_x + wide_y),
            transcendentals=0,
        ),
        compiler_params=params(),
        name="weight_grad",
    )(x, y)


def entry_kernel(
    levels_ref, tokens_ref, dr_ref, dq_ref, dk_ref, dv_ref, vec_ref, w_ref,
    grad_ref, gain_ref, table_ref
):
    step = pl.program_id(0)

    @pl.when(step == 0)
    def _():
        gain_ref[...] = jnp.zeros_like(gain_ref)
        table_ref[...] = jnp.zeros_like(table_ref)

    normed, scaling = normalised(hidden_tile(levels_ref, tokens_ref, vec_ref))
    back = dot(dq_ref[...], w_ref[:, :D], 1, 1)
    back = back + dot(dk_ref[...], w_ref[:, D : 2 * D], 1, 1)
    back = back + dot(dv_ref[...], w_ref[:, 2 * D :], 1, 1)
    gain_ref[...] += eight_rows(back * normed)
    result = dr_ref[...] + norm_back(normed, scaling, vec_ref[0:1, :], back)
    grad_ref[...] = result

    @pl.when(step < SEQ // TILE)
    def _():
        per_tile = TILE // BLOCK
        sums = result.reshape(per_tile, BLOCK, D).sum(axis=1)
        for block in range(per_tile):
            level = levels_ref[step * per_tile + block]
            table_ref[pl.ds(level, 1), :] += sums[block : block + 1, :]


def entry(levels, tokens, resid_grad, dq, dk, dv, vec_master, w_qkv):
    return pl.pallas_call(
        entry_kernel,
        grid_spec=pltpu.PrefetchScalarGridSpec(
            num_scalar_prefetch=1,
            grid=(ROWS // TILE,),
            in_specs=[rows_of(D)] * 5 + [whole((VROWS, D)), whole((D, 3 * D))],
            out_specs=[
                rows_of(D),
                pl.BlockSpec((8, D), lambda i, *_: (0, 0)),
                pl.BlockSpec((LEVELS, D), lambda i, *_: (0, 0)),
            ],
        ),
        out_shape=[
            jax.ShapeDtypeStruct((ROWS, D), full),
            jax.ShapeDtypeStruct((8, D), full),
            jax.ShapeDtypeStruct((LEVELS, D), full),
        ],
        cost_estimate=pl.CostEstimate(
            flops=6 * ROWS * D * D, bytes_accessed=20 * ROWS * D, transcendentals=0
        ),
        compiler_params=params(),
        name="entry",
    )(levels, tokens, resid_grad, dq, dk, dv, vec_master, w_qkv)


def turn_tables():
    positions = jnp.arange(SEQ, dtype=jnp.int32).astype(full)
    exponents = jnp.arange(HEAD_DIM // 2, dtype=full) * (2.0 / HEAD_DIM)
    angles = positions[:, None] * (rope_base ** (-exponents))[None, :]
    cos = jnp.cos(angles)
    sin = jnp.sin(angles)
    return (
        jnp.concatenate([cos, cos, cos, cos], axis=1),
        jnp.concatenate([-sin, -sin, sin, sin], axis=1),
    )


def swap_halves(matrix):
    rows = matrix.shape[0]
    pairs = matrix.reshape(rows, -1, 2, 2, HEAD_DIM // 2)
    return jnp.swapaxes(pairs, 2, 3).reshape(rows, -1)


def adam(grad, moment, square, master, decay, rate):
    moment_new = moment_decay * moment + (1.0 - moment_decay) * grad
    square_new = moment_decay * square + (1.0 - moment_decay) * grad * grad
    correction = 1.0 - moment_decay**STEP
    master_new = master * (1.0 - rate * decay) - rate * (moment_new / correction) / (
        jnp.sqrt(square_new / correction) + adam_eps
    )
    return (moment_new, square_new, master_new)


def spread(value, axis, source):
    kept = jnp.where(lax.axis_index(axis) == source, value, 0).astype(value.dtype)
    return lax.psum(kept, axis)


def shortened(value):

    def short(part):
        return part.astype(jnp.bfloat16) if part.dtype == jnp.float32 else part

    return jax.tree.map(short, value)


def local(
    tokens,
    cotangent,
    lengths,
    levels,
    owners,
    master_slots,
    moment_slots,
    square_slots,
    vec_master,
    vec_moment,
    vec_square,
):
    narrow_count = lax.axis_size("narrow")
    wide_count = lax.axis_size("wide")
    position = lax.axis_index("wide")
    slot_rows = master_slots.shape[1]
    shapes = ((D, 3 * D), (D, D), (D, FF), (FF, D))

    def share_of(slots, index_k):
        rows, cols = shapes[index_k]
        count = rows * cols // (narrow_count * D)
        return slots[0, :count].reshape(rows // narrow_count, cols)

    def owner_share(index_k):
        share = share_of(master_slots, index_k).astype(jnp.bfloat16)
        if index_k == 0:
            share = jnp.concatenate([swap_halves(share[:, : 2 * D]), share[:, 2 * D :]], axis=1)
        return spread(share, "wide", owners[index_k])

    shards = tuple((owner_share(index_k) for index_k in range(4)))
    w_qkv, w_out, w_up, w_down = lax.all_gather(shards, "narrow", axis=0, tiled=True)
    tokens = tokens.reshape(ROWS, D)
    cotangent = cotangent.reshape(ROWS, D)
    levels = levels.reshape(-1)
    cos, sin = turn_tables()
    attn_in = norm_one(levels, tokens, vec_master)
    qkv = project(attn_in, w_qkv, cos, sin)
    attended, logs = attend(lengths, qkv)
    output, mlp_in, act, pre_grad, resid_grad, resid_low, attended_grad, sums, up_sums = feed(
        levels, tokens, attended, cotangent, vec_master, w_out, w_up, w_down
    )
    down_grad = weight_grad(act, cotangent, 768, 768)
    up_grad = weight_grad(mlp_in, pre_grad, 768, 768)
    out_grad = weight_grad(attended, resid_low, 768, 384)
    dq, dk, dv = attend_back(lengths, qkv, attended, attended_grad, logs, cos, sin)
    q_grad = weight_grad(attn_in, dq, 768, 384)
    k_grad = weight_grad(attn_in, dk, 768, 384)
    v_grad = weight_grad(attn_in, dv, 768, 384)
    qkv_grad = jnp.concatenate([swap_halves(q_grad), swap_halves(k_grad), v_grad], axis=1)
    input_grad, gain_sums, table_grad = entry(
        levels, tokens, resid_grad, dq, dk, dv, vec_master, w_qkv
    )
    vec_local = (
        jnp.concatenate(
            [
                gain_sums.sum(axis=0)[None],
                sums[:8].sum(axis=0)[None],
                sums[8:].sum(axis=0)[None],
                up_sums.sum(axis=0).reshape(UP_ROWS, D),
                table_grad,
            ],
            axis=0,
        )
        * row_scale
    )
    narrow_shares = tuple(
        lax.psum_scatter(grad, "narrow", scatter_dimension=0, tiled=True).astype(full)
        for grad in (qkv_grad, out_grad, up_grad, down_grad)
    )
    summed = lax.psum(
        (narrow_shares[0], narrow_shares[1], narrow_shares[2], narrow_shares[3]), "wide"
    )
    pieces = tuple(
        (
            lax.dynamic_slice_in_dim(
                total.reshape(-1),
                position * (total.size // wide_count),
                total.size // wide_count,
                0,
            )
            for total in summed
        )
    )
    square_local = sum((jnp.sum(piece * piece) for piece in pieces))
    vec_total, square_total = lax.psum((vec_local, square_local), ("narrow", "wide"))
    norm_value = jnp.sqrt(square_total + jnp.sum(vec_total * vec_total))
    clip_factor = jnp.minimum(1.0, 1.0 / (norm_value + 1e-06))
    master_out = jnp.zeros((slot_rows, D), jnp.float32)
    moment_out = jnp.zeros((slot_rows, D), jnp.float32)
    square_out = jnp.zeros((slot_rows, D), jnp.float32)
    for index_k in range(4):
        clipped = summed[index_k] * clip_factor
        moment_new, square_new, master_new = adam(
            clipped,
            share_of(moment_slots, index_k),
            share_of(square_slots, index_k),
            share_of(master_slots, index_k),
            decay_rate,
            learn_rate,
        )
        is_owner = position == owners[index_k]
        count = master_new.size // D
        filler = jnp.zeros((slot_rows - count, D), jnp.float32)
        master_out = master_out + jnp.where(
            is_owner, jnp.concatenate([master_new.reshape(count, D), filler], axis=0), 0.0
        )
        moment_out = moment_out + jnp.where(
            is_owner, jnp.concatenate([moment_new.reshape(count, D), filler], axis=0), 0.0
        )
        square_out = square_out + jnp.where(
            is_owner, jnp.concatenate([square_new.reshape(count, D), filler], axis=0), 0.0
        )
    vec_clipped = vec_total * clip_factor
    vec_moment_new, vec_square_new, vec_master_new = adam(
        vec_clipped, vec_moment, vec_square, vec_master, 0.0, vector_rate
    )
    return (
        output[None],
        input_grad[None],
        master_out[None],
        moment_out[None],
        square_out[None],
        vec_clipped,
        vec_moment_new,
        vec_square_new,
        vec_master_new,
        norm_value.reshape(1),
    )


def solution(mesh):
    placed = (
        P(("wide", "narrow"), None, None),
        P(("wide", "narrow"), None, None),
        P(("wide", "narrow")),
        P(("wide", "narrow"), None),
        P(),
        P("wide", "narrow", None),
        P("wide", "narrow", None),
        P("wide", "narrow", None),
        P(),
        P(),
        P(),
    )
    return jax.shard_map(
        local,
        mesh=mesh,
        in_specs=placed,
        out_specs=(
            P(("wide", "narrow"), None, None),
            P(("wide", "narrow"), None, None),
            P("wide", "narrow", None),
            P("wide", "narrow", None),
            P("wide", "narrow", None),
            P(),
            P(),
            P(),
            P(),
            P(),
        ),
        check_vma=False,
    )
```

```python
from functools import partial

import jax
import jax.numpy as jnp
from jax import lax
from jax.experimental import pallas as pl
from jax.experimental.pallas import tpu as pltpu
from jax.sharding import PartitionSpec as P

D = 768
HEADS = 12
HEAD_DIM = 64
FF = 3072
BLOCK = 16
SEQ = 1024
LEVELS = 8
STEP = 10
ROWS = 2 * SEQ

ln_eps = 1e-05
learn_rate = 0.05
vector_rate = 0.5
decay_rate = 0.1
moment_decay = 0.5
adam_eps = 1e-08
masked_score = -1e30
rope_base = 10000.0
row_scale = 1.0 / (2 * SEQ)

TILE = 256
PAIR = 2 * HEAD_DIM
GROUPS = HEADS // 2
UP_ROWS = FF // D
VROWS = 3 + UP_ROWS + LEVELS
low = jnp.bfloat16
full = jnp.float32


def dot(a, b, dim_a=1, dim_b=0):
    return lax.dot_general(
        a, b, (((dim_a,), (dim_b,)), ((), ())), preferred_element_type=full
    )


def came_from(here, place, narrow):
    return lax.rem(here - place + narrow, narrow) if narrow > 1 else 0


anywhere = pl.BlockSpec(memory_space=pl.ANY)


def copies_in_order(source, target, here, semaphores):
    planes, narrow, _, rows, _ = source.shape
    found = []
    for place in range(narrow):
        for plane in range(planes):
            found.append(
                pltpu.make_async_copy(
                    source.at[plane, came_from(here, place, narrow)],
                    target.at[:, pl.ds((place * planes + plane) * rows, rows), :],
                    semaphores.at[place * planes + plane],
                )
            )
    return found


def bring(sources, targets, here, semaphores):
    found = []
    for index, (source, target) in enumerate(zip(sources, targets)):
        found += copies_in_order(source, target, here, semaphores.at[index])
    for copy in found:
        copy.start()
    for copy in found:
        copy.wait()


def ordered_shape(weight):
    planes, narrow, parts, rows, columns = weight.shape
    return (parts, planes * narrow * rows, columns)


def ordered_scratch(weights):
    return [pltpu.VMEM(ordered_shape(weight), low) for weight in weights] + [
        pltpu.SemaphoreType.DMA((len(weights), 16))
    ]


def side_by_side(ref, parts):
    return jnp.concatenate([ref[part] for part in parts], axis=1)


def params(limit=56):
    return pltpu.CompilerParams(vmem_limit_bytes=limit * 2**20)


def whole(shape):
    zeros = (0,) * len(shape)
    return pl.BlockSpec(shape, lambda *_: zeros, pipeline_mode=pl.Buffered(1))


def rows_of(width, rows=TILE):
    return pl.BlockSpec((rows, width), lambda i, *_: (i, 0))


def hidden_tile(levels_ref, tokens, vec_ref, sub=0, subs=1):
    count = tokens.shape[0]
    step = pl.program_id(0) * subs + sub
    per_tile = count // BLOCK
    first = lax.rem(step, SEQ // count) * per_tile
    rows = []
    for block in range(per_tile):
        level = levels_ref[first + block]
        row = vec_ref[pl.ds(3 + UP_ROWS + level, 1), :]
        rows.append(jnp.broadcast_to(row, (BLOCK, D)))
    embedding = jnp.concatenate(rows, axis=0)
    noised = step < SEQ // count
    return tokens.astype(full) + jnp.where(noised, embedding, 0.0)


def normalised(entries):
    centred = entries - jnp.mean(entries, axis=-1, keepdims=True)
    scaling = lax.rsqrt(jnp.mean(centred * centred, axis=-1, keepdims=True) + ln_eps)
    return centred * scaling, scaling


def norm_back(normed, scaling, gain, grad):
    inner = grad * gain
    return (
        inner
        - jnp.mean(inner, axis=-1, keepdims=True)
        - normed * jnp.mean(inner * normed, axis=-1, keepdims=True)
    ) * scaling


def eight_rows(entries):
    return entries.reshape(-1, 8, entries.shape[-1]).sum(axis=0)


def norm_one_kernel(levels_ref, tokens_ref, vec_ref, out_ref):
    normed, _ = normalised(hidden_tile(levels_ref, tokens_ref[...], vec_ref))
    out_ref[...] = (normed * vec_ref[0:1, :]).astype(low)


def norm_one(levels, tokens, vec_master):
    return pl.pallas_call(
        norm_one_kernel,
        grid_spec=pltpu.PrefetchScalarGridSpec(
            num_scalar_prefetch=1,
            grid=(ROWS // TILE,),
            in_specs=[rows_of(D), whole((VROWS, D))],
            out_specs=rows_of(D),
        ),
        out_shape=jax.ShapeDtypeStruct((ROWS, D), low),
        cost_estimate=pl.CostEstimate(
            flops=10 * ROWS * D, bytes_accessed=4 * ROWS * D, transcendentals=0
        ),
        compiler_params=params(),
        name="norm_one",
    )(levels, tokens, vec_master)


def turn(entries, cos, sin):
    return entries * cos + pltpu.roll(entries, HEAD_DIM, 1) * sin


PROJECT_TILE = 512


def project_kernel(pairs, place_ref, a_ref, w_hbm, cos_ref, sin_ref, out_ref, w_ref, semaphores):
    @pl.when(pl.program_id(0) == 0)
    def _():
        bring([w_hbm], [w_ref], place_ref[1], semaphores)

    weights = side_by_side(w_ref, range(3))
    for sub in range(PROJECT_TILE // TILE):
        rows = slice(sub * TILE, (sub + 1) * TILE)
        cos = cos_ref[rows, :]
        sin = sin_ref[rows, :]
        projected = dot(a_ref[rows, :], weights)
        for part in range(3):
            for pair in range(pairs):
                start = (part * pairs + pair) * PAIR
                columns = slice(start, start + PAIR)
                result = projected[:, columns]
                if part < 2:
                    result = turn(result, cos, sin).astype(low)
                if part == 0:
                    result = result.astype(full) * HEAD_DIM**-0.5
                out_ref[rows, columns] = result.astype(low)


def project(places, attn_in, w_part, cos, sin):
    width = 3 * w_part.shape[4]
    table = pl.BlockSpec(
        (PROJECT_TILE, PAIR), lambda i, *_: (lax.rem(i, SEQ // PROJECT_TILE), 0)
    )
    return pl.pallas_call(
        partial(project_kernel, width // (3 * PAIR)),
        grid_spec=pltpu.PrefetchScalarGridSpec(
            num_scalar_prefetch=1,
            grid=(ROWS // PROJECT_TILE,),
            in_specs=[rows_of(D, PROJECT_TILE), anywhere, table, table],
            out_specs=rows_of(width, PROJECT_TILE),
            scratch_shapes=ordered_scratch([w_part]),
        ),
        out_shape=jax.ShapeDtypeStruct((ROWS, width), low),
        cost_estimate=pl.CostEstimate(
            flops=2 * ROWS * D * width, bytes_accessed=8 * ROWS * D, transcendentals=0
        ),
        compiler_params=params(),
        name="project",
    )(places, attn_in, w_part, cos, sin)


QT = 256
TILES = SEQ // QT
SHORTEST = 256


def fill_bias(length, same_ref, earlier_ref, causal_ref, length_ref):
    key = lax.broadcasted_iota(jnp.int32, (QT, QT), 0)
    query = lax.broadcasted_iota(jnp.int32, (QT, QT), 1)
    key_block = key // BLOCK
    query_block = query // BLOCK
    for tile in range(TILES):
        kept = key + tile * QT < length
        own = kept | (key == query)
        same_ref[tile] = jnp.where((key_block == query_block) & own, 0.0, masked_score)
        earlier_ref[tile] = jnp.where((key_block < query_block) & kept, 0.0, masked_score)
        causal_ref[tile] = jnp.where((key_block <= query_block) & own, 0.0, masked_score)
    position = lax.broadcasted_iota(jnp.int32, (SEQ, QT), 0)
    length_ref[...] = jnp.where(position < length, 0.0, masked_score)


bias_scratch = [
    pltpu.VMEM((TILES, QT, QT), full),
    pltpu.VMEM((TILES, QT, QT), full),
    pltpu.VMEM((TILES, QT, QT), full),
    pltpu.VMEM((SEQ, QT), full),
]


def segments(tile, noised):
    found = []
    if noised:
        found.append((tile * QT, QT, "same"))
        found.append((SEQ + tile * QT, QT, "earlier"))
    else:
        found.append((SEQ + tile * QT, QT, "causal"))
    before = tile * QT
    free = min(before, SHORTEST)
    if before > free:
        found.append((SEQ + free, before - free, "length"))
    if free > 0:
        found.append((SEQ, free, None))
    return found


def masked(scores, kind, tile, start, count, biases):
    same_ref, earlier_ref, causal_ref, length_ref = biases
    if kind == "same":
        return scores + same_ref[tile]
    if kind == "earlier":
        return scores + earlier_ref[tile]
    if kind == "causal":
        return scores + causal_ref[tile]
    if kind == "length":
        return scores + length_ref[start - SEQ : start - SEQ + count, :]
    return scores


def lane_masks(head, rows):
    lane = lax.broadcasted_iota(jnp.int32, (rows, PAIR), 1)
    halves = (lane // (HEAD_DIM // 2)) % 2 == head
    plain = lane // HEAD_DIM == head
    return halves, plain


def attend_kernel(aliased, scalar_ref, q_ref, k_ref, v_ref, *refs):
    o_ref, log_ref, *biases = refs[2:] if aliased else refs

    @pl.when(pl.program_id(0) == 0)
    def _():
        fill_bias(scalar_ref[0], *biases)

    units = [
        (head, tile, noised)
        for head in range(2)
        for tile in range(TILES)
        for noised in (True, False)
    ]

    def score(head, tile, noised):
        halves, _ = lane_masks(head, QT)
        row = tile * QT + (0 if noised else SEQ)
        query = jnp.where(halves, q_ref[row : row + QT, :], jnp.zeros((), low))
        parts = []
        for start, count, kind in segments(tile, noised):
            scores = dot(k_ref[start : start + count, :], query, 1, 1)
            parts.append((start, count, masked(scores, kind, tile, start, count, biases)))
        return parts

    def weigh(head, tile, noised, parts):
        row = tile * QT + (0 if noised else SEQ)
        row_max = None
        for start, count, scores in parts:
            top = jnp.max(scores, axis=0, keepdims=True)
            row_max = top if row_max is None else jnp.maximum(row_max, top)
        total = None
        weights = []
        for start, count, scores in parts:
            expo = jnp.exp(scores - row_max)
            part_total = jnp.sum(expo, axis=0, keepdims=True)
            total = part_total if total is None else total + part_total
            weights.append((start, count, expo.astype(low)))
        log_ref[0, head : head + 1, row : row + QT] = row_max + jnp.log(total)
        return weights, total

    def finish(head, tile, noised, weights, total):
        _, plain = lane_masks(head, QT)
        row = tile * QT + (0 if noised else SEQ)
        attended = None
        for start, count, expo in weights:
            product = dot(expo, v_ref[start : start + count, :], 0, 0)
            attended = product if attended is None else attended + product
        inverse = jnp.transpose(jnp.broadcast_to(1.0 / total, (PAIR, QT)))
        result = (attended * inverse).astype(low)
        o_ref[row : row + QT, :] = jnp.where(plain, result, o_ref[row : row + QT, :])

    parts = score(*units[0])
    held = None
    for index, unit in enumerate(units):
        following = score(*units[index + 1]) if index + 1 < len(units) else None
        weights = weigh(*unit, parts)
        if held is not None:
            finish(*held)
        held = (*unit, *weights)
        parts = following
    finish(*held)


def column_spec(offset):
    return pl.BlockSpec((ROWS, PAIR), lambda g, *_: (0, offset + g))


pair_spec = pl.BlockSpec((ROWS, PAIR), lambda g, scalars: (0, scalars[1] + g))
log_spec = pl.BlockSpec((1, 2, ROWS), lambda g, scalars: (scalars[1] + g, 0, 0))
PAIRS_SEEN = 1572864


def attend(scalars, qkv, before):
    pairs = qkv.shape[1] // (3 * PAIR)
    aliased = before is not None
    kept = [pl.BlockSpec(memory_space=pl.ANY)] * 2 if aliased else []
    return pl.pallas_call(
        partial(attend_kernel, aliased),
        grid_spec=pltpu.PrefetchScalarGridSpec(
            num_scalar_prefetch=1,
            grid=(pairs,),
            in_specs=[column_spec(0), column_spec(pairs), column_spec(2 * pairs), *kept],
            out_specs=[pair_spec, log_spec],
            scratch_shapes=bias_scratch,
        ),
        out_shape=[
            jax.ShapeDtypeStruct((ROWS, D), low),
            jax.ShapeDtypeStruct((GROUPS, 2, ROWS), full),
        ],
        input_output_aliases={4: 0, 5: 1} if aliased else {},
        cost_estimate=pl.CostEstimate(
            flops=16 * PAIRS_SEEN * PAIR * pairs,
            bytes_accessed=8 * ROWS * PAIR * pairs,
            transcendentals=0,
        ),
        compiler_params=params(),
        name="attend",
    )(scalars, qkv, qkv, qkv, *(before or ()))


def attend_back_kernel(
    scalar_ref, q_ref, k_ref, v_ref, o_ref, grad_ref, log_ref, cos_ref, sin_ref,
    grad_out_ref, q_acc, k_acc, v_acc, delta_acc, prob_ref, score_ref, own_prob_ref,
    own_score_ref, *biases
):
    @pl.when(pl.program_id(0) == 0)
    def _():
        fill_bias(scalar_ref[0], *biases)

    for row in range(0, ROWS, QT):
        product = o_ref[row : row + QT, :].astype(full) * grad_ref[row : row + QT, :].astype(full)
        turned = jnp.transpose(product)
        delta_acc[0:1, row : row + QT] = jnp.sum(turned[:HEAD_DIM], axis=0, keepdims=True)
        delta_acc[1:2, row : row + QT] = jnp.sum(turned[HEAD_DIM:], axis=0, keepdims=True)

    def products(head, tile, noised, start, count):
        halves, plain = lane_masks(head, QT)
        row = tile * QT + (0 if noised else SEQ)
        zero = jnp.zeros((), low)
        query = jnp.where(halves, q_ref[row : row + QT, :], zero)
        grad = jnp.where(plain, grad_ref[row : row + QT, :], zero)
        scores = dot(k_ref[start : start + count, :], query, 1, 1)
        return scores, dot(v_ref[start : start + count, :], grad, 1, 1)

    def keep(head, tile, noised, start, count, kind, pair):
        row = tile * QT + (0 if noised else SEQ)
        scores, prob_grad = pair
        scores = masked(scores, kind, tile, start, count, biases)
        probs = jnp.exp(scores - log_ref[0, head : head + 1, row : row + QT])
        delta = delta_acc[head : head + 1, row : row + QT]
        score_grad = (probs * (prob_grad - delta)).astype(low)
        if kind == "same":
            own_prob_ref[start : start + count, :] = probs.astype(low)
            own_score_ref[start : start + count, :] = score_grad
        else:
            key = start - SEQ
            prob_ref[key : key + count, row : row + QT] = probs.astype(low)
            score_ref[key : key + count, row : row + QT] = score_grad

    def put(ref, row, mask, value):
        ref[row : row + QT, :] = jnp.where(mask, value, ref[row : row + QT, :])

    def sums(head, tile):
        halves, plain = lane_masks(head, QT)
        row = tile * QT
        rows, clean_rows = slice(row, row + QT), slice(SEQ + row, SEQ + row + QT)
        seen = (slice(row, SEQ), slice(SEQ + row, ROWS))
        put(v_acc, row, plain, dot(own_prob_ref[rows, :], grad_ref[rows, :]))
        put(k_acc, row, halves, dot(own_score_ref[rows, :], q_ref[rows, :]))
        put(
            v_acc, SEQ + row, plain,
            dot(prob_ref[rows, seen[0]], grad_ref[seen[0], :])
            + dot(prob_ref[rows, seen[1]], grad_ref[seen[1], :]),
        )
        put(
            k_acc, SEQ + row, halves,
            dot(score_ref[rows, seen[0]], q_ref[seen[0], :])
            + dot(score_ref[rows, seen[1]], q_ref[seen[1], :]),
        )
        keys = k_ref[SEQ : SEQ + row + QT, :]
        put(
            q_acc, row, halves,
            dot(score_ref[: row + QT, rows], keys, 0, 0)
            + dot(own_score_ref[rows, :], k_ref[rows, :], 0, 0),
        )
        put(q_acc, SEQ + row, halves, dot(score_ref[: row + QT, clean_rows], keys, 0, 0))

    items = []
    for head in range(2):
        for tile in reversed(range(TILES)):
            for noised in (True, False):
                for start, count, kind in segments(tile, noised):
                    items.append((head, tile, noised, start, count, kind))
    waiting = []
    pair = products(*items[0][:5])
    for index, item in enumerate(items):
        following = None
        if index + 1 < len(items):
            following = products(*items[index + 1][:5])
        keep(*item, pair)
        pair = following
        if index + 1 == len(items) or items[index + 1][:2] != item[:2]:
            sums(*item[:2])
    for row in range(0, ROWS, QT):
        rows = slice(row, row + QT)
        cos = cos_ref[row % SEQ : row % SEQ + QT, :]
        sin = -sin_ref[row % SEQ : row % SEQ + QT, :]
        grad_out_ref[0, rows, :] = turn(q_acc[rows, :] * HEAD_DIM**-0.5, cos, sin).astype(low)
        grad_out_ref[1, rows, :] = turn(k_acc[rows, :], cos, sin).astype(low)
        grad_out_ref[2, rows, :] = v_acc[rows, :].astype(low)


def attend_back(scalars, qkv, attended, grad, logs, cos, sin):
    pairs = qkv.shape[1] // (3 * PAIR)
    table = whole((SEQ, PAIR))
    return pl.pallas_call(
        attend_back_kernel,
        grid_spec=pltpu.PrefetchScalarGridSpec(
            num_scalar_prefetch=1,
            grid=(pairs,),
            in_specs=[
                column_spec(0), column_spec(pairs), column_spec(2 * pairs),
                pair_spec, pair_spec, log_spec, table, table,
            ],
            out_specs=pl.BlockSpec((3, ROWS, PAIR), lambda g, *_: (0, 0, g)),
            scratch_shapes=[
                pltpu.VMEM((ROWS, PAIR), full),
                pltpu.VMEM((ROWS, PAIR), full),
                pltpu.VMEM((ROWS, PAIR), full),
                pltpu.VMEM((8, ROWS), full),
                pltpu.VMEM((SEQ, ROWS), low),
                pltpu.VMEM((SEQ, ROWS), low),
                pltpu.VMEM((SEQ, QT), low),
                pltpu.VMEM((SEQ, QT), low),
                *bias_scratch,
            ],
        ),
        out_shape=jax.ShapeDtypeStruct((3, ROWS, pairs * PAIR), low),
        cost_estimate=pl.CostEstimate(
            flops=40 * PAIRS_SEEN * PAIR * pairs,
            bytes_accessed=16 * ROWS * PAIR * pairs,
            transcendentals=0,
        ),
        compiler_params=params(),
        name="attend_back",
    )(scalars, qkv, qkv, qkv, attended, grad, logs, cos, sin)


root_two_pi = 0.7978845608028654
cubic = 0.044715


HALF = D // 2
FF_HALF = FF // 2


FEED_TILE = 512
SUB = 256


def feed_kernel(
    levels_ref, side_ref, tokens_ref, o_ref, dy_ref, vec_ref, bias_ref,
    wide_mine_hbm, wide_other_hbm, down_mine_hbm, down_other_hbm,
    y_ref, b_ref, gl_ref, du_ref, dr_ref, drb_ref, do_ref, sums_ref, upsum_ref,
    wide_mine, wide_other, down_mine, down_other, semaphores
):
    @pl.when(pl.program_id(0) == 0)
    def _():
        sums_ref[...] = jnp.zeros_like(sums_ref)
        upsum_ref[...] = jnp.zeros_like(upsum_ref)
        bring(
            [wide_mine_hbm, wide_other_hbm, down_mine_hbm, down_other_hbm],
            [wide_mine, wide_other, down_mine, down_other],
            side_ref[1],
            semaphores,
        )

    swapped = side_ref[0] == 1
    gain = vec_ref[1:2, :]
    subs = FEED_TILE // SUB

    def in_order(mine, other):
        return jnp.concatenate(
            [jnp.where(swapped, other, mine), jnp.where(swapped, mine, other)], axis=1
        )

    def weights(part):
        wide_ref, down_ref = (wide_mine, down_mine) if part < 2 else (wide_other, down_other)
        inner = part % 2
        up = side_by_side(wide_ref, (inner * 2, inner * 2 + 1))
        return up, down_ref[0, inner * D : (inner + 1) * D, :]

    def head(sub):
        rows = slice(sub * SUB, (sub + 1) * SUB)
        attended = o_ref[rows, :]
        hidden = hidden_tile(levels_ref, tokens_ref[rows, :], vec_ref, sub, subs)
        resid = hidden + in_order(
            dot(attended, wide_mine[UP_ROWS]), dot(attended, wide_other[UP_ROWS])
        )
        normed, scaling = normalised(resid)
        mlp_in = (normed * gain).astype(low)
        b_ref[rows, :] = mlp_in
        return normed, scaling, mlp_in, resid + vec_ref[2:3, :]

    def products(sub, part, mlp_in):
        up, down = weights(part)
        rows = slice(sub * SUB, (sub + 1) * SUB)
        columns = slice(part * D, (part + 1) * D)
        return dot(mlp_in, up) + bias_ref[:, columns], dot(dy_ref[rows, :], down, 1, 1)

    def bend(sub, part, pre, act_grad):
        rows = slice(sub * SUB, (sub + 1) * SUB)
        columns = slice(part * D, (part + 1) * D)
        square = pre * pre
        bent = jnp.tanh(pre * (root_two_pi + (cubic * root_two_pi) * square))
        half = 0.5 + 0.5 * bent
        act = (pre * half).astype(low)
        slope = half + (0.5 * pre) * (1.0 - bent * bent) * (
            root_two_pi + (3.0 * cubic * root_two_pi) * square
        )
        pre_grad = act_grad * slope
        pre_low = pre_grad.astype(low)
        gl_ref[rows, columns] = act
        du_ref[rows, columns] = pre_low
        upsum_ref[:, columns] += eight_rows(pre_grad)
        return act, pre_low

    def main(sub, mlp_in, result):
        back = None
        ahead = products(sub, 0, mlp_in)
        for part in range(UP_ROWS):
            pair = ahead
            if part + 1 < UP_ROWS:
                ahead = products(sub, part + 1, mlp_in)
            act, pre_low = bend(sub, part, *pair)
            up, down = weights(part)
            result = result + dot(act, down)
            term = dot(pre_low, up, 1, 1)
            back = term if back is None else back + term
        return result, back

    def tail(sub, normed, scaling, result, back):
        rows = slice(sub * SUB, (sub + 1) * SUB)
        y_ref[rows, :] = result.astype(low)
        dy_full = dy_ref[rows, :].astype(full)
        sums_ref[0:8, :] += eight_rows(back * normed)
        sums_ref[8:16, :] += eight_rows(dy_full)
        resid_grad = dy_full + norm_back(normed, scaling, gain, back)
        dr_ref[rows, :] = resid_grad
        drb_ref[rows, :] = resid_grad.astype(low)
        first, second = resid_grad[:, :HALF], resid_grad[:, HALF:]
        mine = jnp.where(swapped, second, first).astype(low)
        other = jnp.where(swapped, first, second).astype(low)
        do_ref[rows, :] = (
            dot(mine, wide_mine[UP_ROWS], 1, 1) + dot(other, wide_other[UP_ROWS], 1, 1)
        ).astype(low)

    state = head(0)
    for sub in range(subs):
        normed, scaling, mlp_in, result = state
        result, back = main(sub, mlp_in, result)
        if sub + 1 < subs:
            state = head(sub + 1)
        tail(sub, normed, scaling, result, back)


def feed(levels, side, tokens, attended, cotangent, vec_master, bias, weights):
    def out(width, kind=low):
        return jax.ShapeDtypeStruct((ROWS, width), kind)

    def rows(width):
        return rows_of(width, FEED_TILE)

    return pl.pallas_call(
        feed_kernel,
        grid_spec=pltpu.PrefetchScalarGridSpec(
            num_scalar_prefetch=2,
            grid=(ROWS // FEED_TILE,),
            in_specs=[
                rows(D), rows(D), rows(D), whole((VROWS, D)), whole((1, FF)), *[anywhere] * 4
            ],
            out_specs=[
                rows(D), rows(D), rows(FF), rows(FF), rows(D), rows(D), rows(D),
                pl.BlockSpec((16, D), lambda i, *_: (0, 0)),
                pl.BlockSpec((8, FF), lambda i, *_: (0, 0)),
            ],
            scratch_shapes=ordered_scratch(weights),
        ),
        out_shape=[
            out(D), out(D), out(FF), out(FF), out(D, full), out(D), out(D),
            jax.ShapeDtypeStruct((16, D), full), jax.ShapeDtypeStruct((8, FF), full),
        ],
        cost_estimate=pl.CostEstimate(
            flops=ROWS * D * (4 * D + 8 * FF), bytes_accessed=30 * ROWS * D, transcendentals=0
        ),
        compiler_params=params(),
        name="feed",
    )(levels, side, tokens, attended, cotangent, vec_master, bias, *weights)


def weight_kernel(added, scalar_ref, x_ref, y_ref, *refs):
    out_ref = refs[-1]
    result = dot(x_ref[...], y_ref[...], 0, 0) * row_scale
    planes, narrow, _, rows, _ = out_ref.shape
    for place in range(narrow):
        for plane in range(planes):
            start = (place * planes + plane) * rows
            block = result[start : start + rows]
            if added:
                block = block + refs[0][plane, place, 0].astype(full)
            out_ref[plane, place, 0] = block.astype(low)


def weight_call(name, count, x_spec, y_spec, out_spec, shape, first, x, y, added):
    return pl.pallas_call(
        partial(weight_kernel, added is not None),
        grid_spec=pltpu.PrefetchScalarGridSpec(
            num_scalar_prefetch=1,
            grid=(count,),
            in_specs=[x_spec, y_spec, *([out_spec] if added is not None else [])],
            out_specs=out_spec,
        ),
        out_shape=jax.ShapeDtypeStruct(shape, low),
        cost_estimate=pl.CostEstimate(
            flops=4 * ROWS * count * D * HALF, bytes_accessed=8 * ROWS * D, transcendentals=0
        ),
        compiler_params=params(),
        name=name,
    )(jnp.asarray(first, jnp.int32).reshape(1), x, y, *([added] if added is not None else []))


def grad_of_columns(blocks, x, y, first, count, added=None):
    planes, narrow = blocks
    rows = D // (planes * narrow)
    if y.ndim == 3:
        y_spec = pl.BlockSpec((None, ROWS, HALF), lambda j, s: (s[0] + j, 0, 0))
    else:
        y_spec = pl.BlockSpec((ROWS, HALF), lambda j, s: (0, s[0] + j))
    return weight_call(
        "grad_of_columns",
        count,
        pl.BlockSpec((ROWS, D), lambda j, s: (0, 0)),
        y_spec,
        pl.BlockSpec((planes, narrow, 1, rows, HALF), lambda j, s: (0, 0, j, 0, 0)),
        (planes, narrow, count, rows, HALF),
        first, x, y, added,
    )


def wide_kernel(added, side_ref, x_ref, y_ref, o_hbm, dr_hbm, *refs):
    out_ref, o_ref, dr_ref, semaphores = refs[-4:]
    step = pl.program_id(0)
    column = pl.multiple_of(side_ref[1] * HALF, HALF)
    copies = [
        pltpu.make_async_copy(o_hbm, o_ref, semaphores.at[0]),
        pltpu.make_async_copy(dr_hbm.at[:, pl.ds(column, HALF)], dr_ref, semaphores.at[1]),
    ]

    def store(result):
        planes, narrow, _, rows, _ = out_ref.shape
        for place in range(narrow):
            for plane in range(planes):
                start = (place * planes + plane) * rows
                block = result[start : start + rows] * row_scale
                if added:
                    block = block + refs[0][plane, place, 0].astype(full)
                out_ref[plane, place, 0] = block.astype(low)

    @pl.when(step == 0)
    def _():
        for copy in copies:
            copy.start()

    @pl.when(step < UP_ROWS)
    def _():
        store(dot(x_ref[...], y_ref[...], 0, 0))

    @pl.when(step == UP_ROWS)
    def _():
        for copy in copies:
            copy.wait()
        store(dot(o_ref[...], dr_ref[...], 0, 0))


def grad_of_wide(blocks, x, y, first, attended, resid_low, side, added=None):
    planes, narrow = blocks
    rows = D // (planes * narrow)
    count = UP_ROWS + 1
    out_spec = pl.BlockSpec((planes, narrow, 1, rows, HALF), lambda j, s: (0, 0, j, 0, 0))
    return pl.pallas_call(
        partial(wide_kernel, added is not None),
        grid_spec=pltpu.PrefetchScalarGridSpec(
            num_scalar_prefetch=1,
            grid=(count,),
            in_specs=[
                whole((ROWS, D)),
                pl.BlockSpec(
                    (ROWS, HALF), lambda j, s: (0, s[0] + jnp.minimum(j, UP_ROWS - 1))
                ),
                anywhere,
                anywhere,
                *([out_spec] if added is not None else []),
            ],
            out_specs=out_spec,
            scratch_shapes=[
                pltpu.VMEM((ROWS, D), low),
                pltpu.VMEM((ROWS, HALF), low),
                pltpu.SemaphoreType.DMA((2,)),
            ],
        ),
        out_shape=jax.ShapeDtypeStruct((planes, narrow, count, rows, HALF), low),
        cost_estimate=pl.CostEstimate(
            flops=4 * ROWS * count * D * HALF, bytes_accessed=8 * ROWS * D, transcendentals=0
        ),
        compiler_params=params(),
        name="grad_of_wide",
    )(
        jnp.stack([jnp.int32(first), side]), x, y, attended, resid_low,
        *([added] if added is not None else []),
    )


def grad_of_rows(blocks, x, y, first, count, added=None):
    planes, narrow = blocks
    if planes == 1:
        rows = HALF
        out_spec = pl.BlockSpec((1, 1, 1, rows, D), lambda i, s: (0, 0, 0, i, 0))
        shape = (1, 1, 1, count * HALF, D)
    else:
        rows = HALF // planes
        out_spec = pl.BlockSpec((planes, 1, 1, rows, D), lambda i, s: (0, i, 0, 0, 0))
        shape = (planes, count, 1, rows, D)
    return weight_call(
        "grad_of_rows",
        count,
        pl.BlockSpec((ROWS, HALF), lambda i, s: (0, s[0] + i)),
        pl.BlockSpec((ROWS, D), lambda i, s: (0, 0)),
        out_spec,
        shape,
        first, x, y, added,
    )


ENTRY_TILE = 512


def entry_kernel(count, levels_ref, place_ref, tokens_ref, dr_ref, vec_ref, *refs):
    step = pl.program_id(0)
    grads, sources = refs[:count], refs[count : 2 * count]
    grad_ref, gain_ref, table_ref = refs[2 * count : 2 * count + 3]
    weights, semaphores = refs[2 * count + 3 : -1], refs[-1]

    @pl.when(step == 0)
    def _():
        gain_ref[...] = jnp.zeros_like(gain_ref)
        table_ref[...] = jnp.zeros_like(table_ref)
        bring(sources, weights, place_ref[1], semaphores)

    matrices = [side_by_side(weight, range(3)) for weight in weights]
    per_tile = TILE // BLOCK
    subs = ENTRY_TILE // TILE
    for sub in range(subs):
        rows = slice(sub * TILE, (sub + 1) * TILE)
        back = None
        for grad, matrix in zip(grads, matrices):
            parts = jnp.concatenate([grad[part, rows, :] for part in range(3)], axis=1)
            term = dot(parts, matrix, 1, 1)
            back = term if back is None else back + term
        hidden = hidden_tile(levels_ref, tokens_ref[rows, :], vec_ref, sub, subs)
        normed, scaling = normalised(hidden)
        gain_ref[...] += eight_rows(back * normed)
        result = dr_ref[rows, :] + norm_back(normed, scaling, vec_ref[0:1, :], back)
        grad_ref[rows, :] = result

    @pl.when(step < SEQ // ENTRY_TILE)
    def _():
        for sub in range(subs):
            sums = grad_ref[sub * TILE : (sub + 1) * TILE, :]
            sums = sums.reshape(per_tile, BLOCK, D).sum(axis=1)
            for block in range(per_tile):
                level = levels_ref[(step * subs + sub) * per_tile + block]
                table_ref[pl.ds(level, 1), :] += sums[block : block + 1, :]


def entry(levels, places, tokens, resid_grad, vec_master, grads, weights):
    count = len(weights)
    return pl.pallas_call(
        partial(entry_kernel, count),
        grid_spec=pltpu.PrefetchScalarGridSpec(
            num_scalar_prefetch=2,
            grid=(ROWS // ENTRY_TILE,),
            in_specs=[rows_of(D, ENTRY_TILE), rows_of(D, ENTRY_TILE), whole((VROWS, D))]
            + [
                pl.BlockSpec((3, ENTRY_TILE, grad.shape[2]), lambda i, *_: (0, i, 0))
                for grad in grads
            ]
            + [anywhere] * count,
            out_specs=[
                rows_of(D, ENTRY_TILE),
                pl.BlockSpec((8, D), lambda i, *_: (0, 0)),
                pl.BlockSpec((LEVELS, D), lambda i, *_: (0, 0)),
            ],
            scratch_shapes=ordered_scratch(weights),
        ),
        out_shape=[
            jax.ShapeDtypeStruct((ROWS, D), full),
            jax.ShapeDtypeStruct((8, D), full),
            jax.ShapeDtypeStruct((LEVELS, D), full),
        ],
        cost_estimate=pl.CostEstimate(
            flops=6 * ROWS * D * D, bytes_accessed=20 * ROWS * D, transcendentals=0
        ),
        compiler_params=params(),
        name="entry",
    )(levels, places, tokens, resid_grad, vec_master, *grads, *weights)


PARTS = (3, 1, 4)


def swapped_halves(entries):
    lane = lax.broadcasted_iota(jnp.int32, entries.shape, 1) % PAIR
    quarter = HEAD_DIM // 2
    width = entries.shape[1]
    ahead = pltpu.roll(entries, width - quarter, 1)
    behind = pltpu.roll(entries, quarter, 1)
    second = (lane >= quarter) & (lane < 2 * quarter)
    third = (lane >= 2 * quarter) & (lane < 3 * quarter)
    return jnp.where(second, ahead, jnp.where(third, behind, entries))


def slot_pieces(kind, wide):
    planes = wide // 2
    found = []
    for plane in range(planes):
        for half in range(2):
            place = 2 * plane + half
            if kind < 3:
                parts, rows = PARTS[kind], D // 4 // planes
                for part in range(parts):
                    where = pl.ds(plane * rows * parts + part, rows, stride=parts)
                    found.append((place, part, part * rows, rows, where, half * HALF))
            else:
                rows = HALF // planes
                for column in range(2):
                    where = pl.ds(half * HALF + plane * rows, rows)
                    found.append((place, 2, column * rows, rows, where, column * HALF))
    return found


LANES = 128


def pack_kernel(owners_ref, slot_ref, out_ref, stage_ref):
    place = lax.axis_index("wide")
    wide = out_ref.shape[0]
    for index in range(D // LANES):
        stage_ref[index] = slot_ref[:, index * LANES : (index + 1) * LANES]
    for kind in range(4):

        @pl.when(owners_ref[kind] == place)
        def _(kind=kind):
            for target, part, start, rows, where, column in slot_pieces(kind, wide):
                for index in range(HALF // LANES):
                    block = stage_ref[column // LANES + index, where, :]
                    if kind == 0 and part < 2:
                        block = swapped_halves(block)
                    columns = slice(index * LANES, (index + 1) * LANES)
                    out_ref[target, start : start + rows, columns] = block.astype(low)


def pack(owners, slot):
    wide = lax.axis_size("wide")
    shape = (wide, 2 * D // wide, HALF)
    return pl.pallas_call(
        pack_kernel,
        grid_spec=pltpu.PrefetchScalarGridSpec(
            num_scalar_prefetch=1,
            grid=(1,),
            in_specs=[whole(slot.shape)],
            out_specs=whole(shape),
            scratch_shapes=[pltpu.VMEM((D // LANES, slot.shape[0], LANES), full)],
        ),
        out_shape=jax.ShapeDtypeStruct(shape, low),
        cost_estimate=pl.CostEstimate(
            flops=D * D, bytes_accessed=6 * D * D, transcendentals=0
        ),
        compiler_params=params(),
        name="pack",
    )(owners, slot)


def settle_kernel(owners_ref, qkv_ref, wide_ref, down_ref, out_ref, square_ref):
    squares = jnp.zeros((8, HALF), full)

    def summed(ref, part):
        result = ref[0, part].astype(full)
        for index in range(1, ref.shape[0]):
            result = result + ref[index, part].astype(full)
        return result.astype(low)

    out_ref[...] = jnp.zeros_like(out_ref)
    for kind in range(4):
        target = owners_ref[kind]
        for part in range((3, 1, 4, 1)[kind]):
            if kind == 0:
                share = summed(qkv_ref, part)
            elif kind < 3:
                share = summed(wide_ref, UP_ROWS if kind == 1 else part)
            else:
                share = summed(down_ref, 0)
            rows = share.shape[0]
            for column in range(share.shape[1] // HALF):
                block = share[:, column * HALF : (column + 1) * HALF]
                start = (part + column) * rows
                out_ref[target, start : start + rows, :] = block
                entries = block.astype(full)
                squares = squares + eight_rows(entries * entries)
    square_ref[...] = jnp.broadcast_to(jnp.sum(squares, keepdims=True), square_ref.shape)


def settle(owners, qkv, wide_parts, down):
    wide = lax.axis_size("wide")
    shape = (wide, 2 * D // wide, HALF)
    return pl.pallas_call(
        settle_kernel,
        grid_spec=pltpu.PrefetchScalarGridSpec(
            num_scalar_prefetch=1,
            grid=(1,),
            in_specs=[whole(qkv.shape), whole(wide_parts.shape), whole(down.shape)],
            out_specs=[whole(shape), whole((8, 128))],
        ),
        out_shape=[jax.ShapeDtypeStruct(shape, low), jax.ShapeDtypeStruct((8, 128), full)],
        cost_estimate=pl.CostEstimate(
            flops=4 * D * D, bytes_accessed=6 * D * D, transcendentals=0
        ),
        compiler_params=params(),
        name="settle",
    )(owners, qkv, wide_parts, down)


FINISH_ROWS = 192


def finish_kernel(
    plain, owners_ref, came_ref, sums_ref, vec_moment_ref, vec_square_ref, vec_master_ref,
    moment_ref, square_ref, master_ref,
    master_out, moment_out, square_out, vec_grad_out, vec_moment_out, vec_square_out,
    vec_master_out, norm_out, grad_ref
):
    step = pl.program_id(0)
    place = lax.axis_index("wide")
    here = lax.axis_index("narrow")
    wide = came_ref.shape[0]
    narrow = sums_ref.shape[0]
    total = sums_ref[here]
    for index in range(1, narrow):
        total = total + sums_ref[lax.rem(here - index + narrow, narrow)]
    vec, total = total[:VROWS], total[VROWS:, 0:1]
    norm = jnp.sqrt(total + jnp.sum(vec * vec, keepdims=True))
    clip = jnp.minimum(1.0, 1.0 / (norm + 1e-06))

    @pl.when(step == 0)
    def _():
        if plain:
            grad_ref[...] = came_ref[...]
        for kind in range(0 if plain else 4):

            @pl.when(owners_ref[kind] == place)
            def _(kind=kind):
                for source, part, start, rows, where, column in slot_pieces(kind, wide):
                    block = came_ref[source, start : start + rows, :].astype(full)
                    for index in range(HALF // LANES):
                        piece = block[:, index * LANES : (index + 1) * LANES]
                        if kind == 0 and part < 2:
                            piece = swapped_halves(piece)
                        grad_ref[column // LANES + index, where, :] = piece

        norm_out[...] = norm
        vec_clipped = vec * clip
        vec_grad_out[...] = vec_clipped
        vec_moment_out[...], vec_square_out[...], vec_master_out[...] = adam(
            vec_clipped, vec_moment_ref[...], vec_square_ref[...], vec_master_ref[...],
            0.0, vector_rate,
        )

    used = jnp.int32(0)
    for kind in range(4):
        rows = D // 4 * (PARTS[kind] if kind < 3 else 4)
        used = jnp.where(owners_ref[kind] == place, rows, used)
    row = step * FINISH_ROWS + lax.broadcasted_iota(jnp.int32, (FINISH_ROWS, D), 0)
    start = pl.multiple_of(step * FINISH_ROWS, FINISH_ROWS)
    grad = jnp.concatenate(
        [grad_ref[index, pl.ds(start, FINISH_ROWS), :] for index in range(D // LANES)], axis=1
    )
    moment_new, square_new, master_new = adam(
        grad * clip,
        moment_ref[...], square_ref[...], master_ref[...], decay_rate, learn_rate,
    )
    kept = row < used
    master_out[...] = jnp.where(kept, master_new, 0.0)
    moment_out[...] = jnp.where(kept, moment_new, 0.0)
    square_out[...] = jnp.where(kept, square_new, 0.0)


def finish(plain, owners, came, sums, vec_states, states):
    rows = states[0].shape[0]
    state_spec = pl.BlockSpec((FINISH_ROWS, D), lambda i, *_: (i, 0))
    vec_spec = whole((VROWS, D))
    state = jax.ShapeDtypeStruct((rows, D), full)
    vec = jax.ShapeDtypeStruct((VROWS, D), full)
    return pl.pallas_call(
        partial(finish_kernel, plain),
        grid_spec=pltpu.PrefetchScalarGridSpec(
            num_scalar_prefetch=1,
            grid=(rows // FINISH_ROWS,),
            in_specs=[whole(came.shape), whole(sums.shape), *[vec_spec] * 3, *[state_spec] * 3],
            out_specs=[*[state_spec] * 3, *[vec_spec] * 4, whole((1, 1))],
            scratch_shapes=[pltpu.VMEM((D // LANES, rows, LANES), full)],
        ),
        out_shape=[state] * 3 + [vec] * 4 + [jax.ShapeDtypeStruct((1, 1), full)],
        cost_estimate=pl.CostEstimate(
            flops=20 * D * D, bytes_accessed=26 * D * D, transcendentals=0
        ),
        compiler_params=params(),
        name="finish",
    )(owners, came, sums, *vec_states, *states)


def turn_tables():
    positions = jnp.arange(SEQ, dtype=jnp.int32).astype(full)
    exponents = jnp.arange(HEAD_DIM // 2, dtype=full) * (2.0 / HEAD_DIM)
    angles = positions[:, None] * (rope_base ** (-exponents))[None, :]
    cos = jnp.cos(angles)
    sin = jnp.sin(angles)
    return (
        jnp.concatenate([cos, cos, cos, cos], axis=1),
        jnp.concatenate([-sin, -sin, sin, sin], axis=1),
    )


def adam(grad, moment, square, master, decay, rate):
    moment_new = moment_decay * moment + (1.0 - moment_decay) * grad
    square_new = moment_decay * square + (1.0 - moment_decay) * grad * grad
    correction = 1.0 - moment_decay**STEP
    master_new = master * (1.0 - rate * decay) - rate * (moment_new / correction) / (
        jnp.sqrt(square_new / correction) + adam_eps
    )
    return (moment_new, square_new, master_new)


def flip(value, axis, bits):
    count = lax.axis_size(axis)
    return lax.ppermute(value, axis, [(i, i ^ bits) for i in range(count)])


def planes_groups():
    count = lax.axis_size("wide")
    return [list(range(start, count, 2)) for start in range(2)]


def shift(value, step):
    count = lax.axis_size("narrow")
    return lax.ppermute(value, "narrow", [(i, (i + step) % count) for i in range(count)])


def swap_planes(blocks):
    return lax.all_to_all(blocks, "wide", 0, 0, axis_index_groups=planes_groups())


def copies(value, count):
    return jnp.broadcast_to(value[None], (count, *value.shape))


def after(value, *others):
    return lax.optimization_barrier((value, *others))[0]


def gather_narrow(share):
    return [share] + [shift(share, step) for step in range(1, lax.axis_size("narrow"))]


def gather_planes(held):
    held = swap_planes(copies(jnp.stack(held), lax.axis_size("wide") // 2))
    if held.shape[3] % 16 == 0:
        return held
    narrow, parts, columns = held.shape[1], held.shape[2], held.shape[4]
    order = (lax.axis_index("narrow") - jnp.arange(narrow)) % narrow
    held = jnp.take(held, order, axis=1)
    return held.transpose(2, 1, 0, 3, 4).reshape(1, 1, parts, -1, columns)


def total(blocks):
    return jnp.sum(blocks.astype(full), axis=0).astype(low)


def reduce_planes(matrix):
    planes, narrow = lax.axis_size("wide") // 2, lax.axis_size("narrow")
    if matrix.shape[0] != planes:
        parts, columns = matrix.shape[2], matrix.shape[4]
        matrix = matrix.reshape(parts, narrow, planes, -1, columns)
        matrix = matrix.transpose(2, 1, 0, 3, 4)
    return total(swap_planes(matrix))


def narrow_pieces(held):
    count = lax.axis_size("narrow")
    place = lax.axis_index("narrow")

    def part(step):
        return lax.dynamic_index_in_dim(held, (place + step) % count, 0, keepdims=False)

    return [part(0)] + [shift(part(step), step) for step in range(1, count)]


def swap_halves(matrix):
    pairs = matrix.reshape(*matrix.shape[:-1], -1, 2, 2, HEAD_DIM // 2)
    return jnp.swapaxes(pairs, -3, -2).reshape(matrix.shape)


def plain_layouts(slot_rows):
    wide = lax.axis_size("wide")
    planes, most = wide // 2, 2 * D // wide
    rows, deep = D // 4 // planes, HALF // planes

    def pack_columns(kind, slot):
        parts = PARTS[kind]
        blocks = slot[: rows * planes * parts].reshape(planes, rows, parts, 2, HALF)
        blocks = blocks.transpose(0, 3, 2, 1, 4)
        if kind == 0:
            blocks = jnp.concatenate([swap_halves(blocks[:, :, :2]), blocks[:, :, 2:]], axis=2)
        blocks = blocks.reshape(wide, parts * rows, HALF)
        return jnp.pad(blocks, ((0, 0), (0, most - parts * rows), (0, 0)))

    def unpack_columns(kind, blocks):
        parts = PARTS[kind]
        blocks = blocks[:, : parts * rows].reshape(planes, 2, parts, rows, HALF)
        if kind == 0:
            blocks = jnp.concatenate([swap_halves(blocks[:, :, :2]), blocks[:, :, 2:]], axis=2)
        flat = blocks.transpose(0, 3, 2, 1, 4).reshape(planes * rows * parts, D)
        return jnp.pad(flat, ((0, slot_rows - flat.shape[0]), (0, 0)))

    def pack_down(slot):
        blocks = slot.reshape(2, planes, deep, 2, HALF)
        return blocks.transpose(1, 0, 3, 2, 4).reshape(wide, 2 * deep, HALF)

    def unpack_down(blocks):
        blocks = blocks.reshape(planes, 2, 2, deep, HALF)
        return blocks.transpose(1, 0, 3, 2, 4).reshape(slot_rows, D)

    packs = [partial(pack_columns, kind) for kind in range(3)] + [pack_down]
    unpacks = [partial(unpack_columns, kind) for kind in range(3)] + [unpack_down]
    packs.append(lambda slot: jnp.zeros((wide, most, HALF), slot.dtype))
    unpacks.append(lambda blocks: jnp.zeros((slot_rows, D), blocks.dtype))
    return packs, unpacks


def plain_pack(kind, slot):
    return lax.switch(kind, plain_layouts(slot.shape[0])[0], slot.astype(low))


def plain_settle(owners, qkv, wide_parts, down):
    wide = lax.axis_size("wide")
    qkv, wide_parts, down = total(qkv), total(wide_parts), total(down)
    down = jnp.stack([down[0, :, :HALF], down[0, :, HALF:]])
    places = jnp.arange(wide, dtype=jnp.int32)[:, None, None]
    sent = jnp.zeros((wide, 2 * D // wide, HALF), low)
    squares = jnp.zeros((), full)
    shares = (qkv, wide_parts[UP_ROWS:], wide_parts[:UP_ROWS], down)
    for kind, share in enumerate(shares):
        share = share.reshape(-1, HALF)
        squares = squares + jnp.sum(jnp.square(share.astype(full)))
        block = jnp.pad(share, ((0, sent.shape[1] - share.shape[0]), (0, 0)))[None]
        sent = jnp.where(places == owners[kind], block, sent)
    return sent, jnp.broadcast_to(squares, (8, 128))


def plain_unpack(kind, slot_rows, came):
    slot = lax.switch(kind, plain_layouts(slot_rows)[1], came).astype(full)
    return jnp.swapaxes(slot.reshape(slot_rows, D // LANES, LANES), 0, 1)


def sum_over_wide(value):
    wide = lax.axis_size("wide")
    bit = 1
    while bit < wide:
        value = value + flip(value, "wide", bit)
        bit *= 2
    return value


def vectors_over_wide(value):
    return jnp.sum(lax.all_to_all(copies(value, lax.axis_size("wide")), "wide", 0, 0), axis=0)


def local(
    tokens,
    cotangent,
    lengths,
    levels,
    owners,
    master_slots,
    moment_slots,
    square_slots,
    vec_master,
    vec_moment,
    vec_square,
):
    narrow = lax.axis_size("narrow")
    wide = lax.axis_size("wide")
    side = lax.axis_index("wide") & 1
    planes = wide // 2
    rows = D // (narrow * planes)
    deep = FF // 2 // (narrow * planes)

    plain = rows % 16 != 0
    owned = owners == lax.axis_index("wide")
    kind = jnp.where(jnp.any(owned), jnp.argmax(owned), 4).astype(jnp.int32)
    if plain:
        packed = plain_pack(kind, master_slots[0])
    else:
        packed = pack(owners, master_slots[0])
    came = lax.all_to_all(packed, "wide", 0, 0)

    def share(kind, count):
        return lax.dynamic_index_in_dim(came, owners[kind], 0, keepdims=False)[:count]

    qkv_share = share(0, 3 * rows).reshape(3, rows, HALF)
    wide_share = jnp.concatenate([share(2, 4 * rows), share(1, rows)])
    wide_share = wide_share.reshape(UP_ROWS + 1, rows, HALF)
    down_share = share(3, 2 * deep)
    down_share = jnp.concatenate([down_share[:deep], down_share[deep:]], axis=1)[None]

    tokens = tokens.reshape(ROWS, D)
    cotangent = cotangent.reshape(ROWS, D)
    levels = levels.reshape(-1)
    here = jnp.stack([side, lax.axis_index("narrow")]).astype(jnp.int32)
    cos, sin = turn_tables()
    bias = vec_master[3 : 3 + UP_ROWS].reshape(UP_ROWS, 2, HALF)
    bias = jnp.stack([bias[:, 0], bias[:, 1]])
    bias = jnp.where(side == 1, bias[::-1], bias).reshape(1, FF)
    half_pairs = GROUPS // 2
    scalars = [
        jnp.stack([lengths[0], half_pairs * half]) for half in (side, 1 - side)
    ]
    attn_in = norm_one(levels, tokens, vec_master)

    qkv_plane = gather_narrow(after(qkv_share, attn_in, cos, sin, bias, *scalars))
    qkv_mine = gather_planes(qkv_plane)
    down_plane = gather_narrow(after(down_share, *qkv_plane))
    qkv_other = flip(qkv_mine, "wide", 1)
    heads_mine = project(here, attn_in, qkv_mine, cos, sin)
    down_mine = gather_planes(after(down_plane, qkv_mine))
    wide_plane = gather_narrow(after(wide_share, qkv_mine))
    before = attend(scalars[0], heads_mine, None)
    wide_mine = gather_planes(after(wide_plane, before[0], down_mine))
    down_other = flip(after(down_mine, before[0]), "wide", 1)
    heads_other = project(here, after(attn_in, before[0]), qkv_other, cos, sin)
    attended, logs = attend(scalars[1], heads_other, before)
    wide_other = flip(after(wide_mine, attended), "wide", 1)
    output, mlp_in, act, pre_grad, resid_grad, resid_low, attended_grad, sums, up_sums = feed(
        levels,
        here,
        tokens,
        attended,
        cotangent,
        vec_master,
        bias,
        (wide_mine, wide_other, down_mine, down_other),
    )

    blocks = (1, 1) if plain else (planes, narrow)
    down_theirs = flip(grad_of_rows(blocks, act, cotangent, 4, 4), "wide", 1)
    wide_theirs = grad_of_wide(
        blocks, mlp_in, pre_grad, 4, attended, resid_low, 1 - side
    )
    wide_came = flip(wide_theirs, "wide", 1)
    down_grad = grad_of_rows(blocks, act, after(cotangent, wide_theirs), 0, 4, down_theirs)
    down_planes = reduce_planes(down_grad)
    wide_grad = grad_of_wide(
        blocks, mlp_in, after(pre_grad, down_grad), 0, attended, resid_low, side, wide_came
    )
    grad_other = attend_back(
        scalars[1], heads_other, attended, after(attended_grad, wide_grad), logs, cos, sin
    )
    wide_planes = reduce_planes(after(wide_grad, down_planes))
    down_pieces = narrow_pieces(down_planes)
    qkv_theirs = grad_of_columns(blocks, attn_in, grad_other, 0, 3)
    grad_mine = attend_back(
        scalars[0], heads_mine, attended, after(attended_grad, qkv_theirs, down_planes), logs, cos, sin
    )
    qkv_grad = grad_of_columns(
        blocks, attn_in, grad_mine, 0, 3, flip(qkv_theirs, "wide", 1)
    )
    wide_pieces = narrow_pieces(after(wide_planes, qkv_grad, *down_pieces))
    qkv_planes = reduce_planes(after(qkv_grad, wide_planes))
    input_grad, gain_sums, table_grad = entry(
        levels, here, tokens, resid_grad, vec_master,
        (after(grad_mine, qkv_grad, wide_planes, *down_pieces), grad_other),
        (qkv_mine, qkv_other),
    )
    qkv_pieces = narrow_pieces(after(qkv_planes, input_grad, *wide_pieces))
    up_sums = up_sums.sum(axis=0).reshape(2, UP_ROWS, HALF)
    up_sums = jnp.where(side == 1, up_sums[::-1], up_sums)
    up_sums = jnp.swapaxes(up_sums, 0, 1).reshape(UP_ROWS, D)
    vec_local = (
        jnp.concatenate(
            [
                gain_sums.sum(axis=0)[None],
                sums[:8].sum(axis=0)[None],
                sums[8:].sum(axis=0)[None],
                up_sums,
                table_grad,
            ],
            axis=0,
        )
        * row_scale
    )
    vec_wide = vectors_over_wide(after(vec_local, qkv_planes))
    sent, squares = (plain_settle if plain else settle)(
        owners, jnp.stack(qkv_pieces), jnp.stack(wide_pieces), jnp.stack(down_pieces)
    )
    came = lax.all_to_all(after(sent, vec_wide), "wide", 0, 0)
    if plain:
        came = plain_unpack(kind, master_slots.shape[1], came)
    squares = jnp.tile(sum_over_wide(squares)[:1], (1, D // LANES))
    all_sums = jnp.stack(gather_narrow(jnp.concatenate([vec_wide, squares])))
    (
        master_new, moment_new, square_new,
        vec_grad, vec_moment_new, vec_square_new, vec_master_new, norm_value,
    ) = finish(
        plain, owners, came, all_sums, (vec_moment, vec_square, vec_master),
        (moment_slots[0], square_slots[0], master_slots[0]),
    )
    return (
        output[None],
        input_grad[None],
        master_new[None],
        moment_new[None],
        square_new[None],
        vec_grad,
        vec_moment_new,
        vec_square_new,
        vec_master_new,
        norm_value.reshape(1),
    )


def solution(mesh):
    placed = (
        P(("wide", "narrow"), None, None),
        P(("wide", "narrow"), None, None),
        P(("wide", "narrow")),
        P(("wide", "narrow"), None),
        P(),
        P("wide", "narrow", None),
        P("wide", "narrow", None),
        P("wide", "narrow", None),
        P(),
        P(),
        P(),
    )
    return jax.shard_map(
        local,
        mesh=mesh,
        in_specs=placed,
        out_specs=(
            P(("wide", "narrow"), None, None),
            P(("wide", "narrow"), None, None),
            P("wide", "narrow", None),
            P("wide", "narrow", None),
            P("wide", "narrow", None),
            P(),
            P(),
            P(),
            P(),
            P(),
        ),
        check_vma=False,
    )
```

```python
from functools import partial

import jax
import jax.numpy as jnp
from jax import lax
from jax.experimental import pallas as pl
from jax.experimental.pallas import tpu as pltpu
from jax.sharding import PartitionSpec as P

D = 768
HEADS = 12
HEAD_DIM = 64
FF = 3072
BLOCK = 16
SEQ = 1024
LEVELS = 8
STEP = 10
ROWS = 2 * SEQ

ln_eps = 1e-05
learn_rate = 0.05
vector_rate = 0.5
decay_rate = 0.1
moment_decay = 0.5
adam_eps = 1e-08
masked_score = -1e30
rope_base = 10000.0
row_scale = 1.0 / (2 * SEQ)

TILE = 256
PAIR = 2 * HEAD_DIM
GROUPS = HEADS // 2
UP_ROWS = FF // D
VROWS = 3 + UP_ROWS + LEVELS
low = jnp.bfloat16
full = jnp.float32


def dot(a, b, dim_a=1, dim_b=0):
    return lax.dot_general(
        a, b, (((dim_a,), (dim_b,)), ((), ())), preferred_element_type=full
    )


def came_from(here, place, narrow):
    return lax.rem(here - place + narrow, narrow) if narrow > 1 else 0


anywhere = pl.BlockSpec(memory_space=pltpu.HBM)


def copies_in_order(source, target, here, semaphores):
    planes, narrow, _, rows, _ = source.shape
    found = []
    for place in range(narrow):
        for plane in range(planes):
            found.append(
                pltpu.make_async_copy(
                    source.at[plane, came_from(here, place, narrow)],
                    target.at[:, pl.ds((place * planes + plane) * rows, rows), :],
                    semaphores.at[place * planes + plane],
                )
            )
    return found


def all_copies(sources, targets, here, semaphores):
    found = []
    for index, (source, target) in enumerate(zip(sources, targets)):
        found += copies_in_order(source, target, here, semaphores.at[index])
    return found


def bring(sources, targets, here, semaphores):
    found = all_copies(sources, targets, here, semaphores)
    for copy in found:
        copy.start()
    for copy in found:
        copy.wait()


def ordered_shape(weight):
    planes, narrow, parts, rows, columns = weight.shape
    return (parts, planes * narrow * rows, columns)


def ordered_scratch(weights):
    return [pltpu.VMEM(ordered_shape(weight), low) for weight in weights] + [
        pltpu.SemaphoreType.DMA((len(weights), 16))
    ]


def side_by_side(ref, parts):
    return jnp.concatenate([ref[part] for part in parts], axis=1)


def params(limit=62):
    return pltpu.CompilerParams(vmem_limit_bytes=limit * 2**20)


def whole(shape):
    zeros = (0,) * len(shape)
    return pl.BlockSpec(shape, lambda *_: zeros, pipeline_mode=pl.Buffered(1))


def rows_of(width, rows=TILE):
    return pl.BlockSpec((rows, width), lambda i, *_: (i, 0))


def hidden_tile(levels_ref, tokens, vec_ref, sub=0, subs=1):
    count = tokens.shape[0]
    step = pl.program_id(0) * subs + sub
    per_tile = count // BLOCK
    first = lax.rem(step, SEQ // count) * per_tile
    rows = []
    for block in range(per_tile):
        level = levels_ref[first + block]
        row = vec_ref[pl.ds(3 + UP_ROWS + level, 1), :]
        rows.append(jnp.broadcast_to(row, (BLOCK, D)))
    embedding = jnp.concatenate(rows, axis=0)
    noised = step < SEQ // count
    return tokens.astype(full) + jnp.where(noised, embedding, 0.0)


def normalised(entries):
    centred = entries - jnp.mean(entries, axis=-1, keepdims=True)
    scaling = lax.rsqrt(jnp.mean(centred * centred, axis=-1, keepdims=True) + ln_eps)
    return centred * scaling, scaling


def norm_back(normed, scaling, gain, grad):
    inner = grad * gain
    return (
        inner
        - jnp.mean(inner, axis=-1, keepdims=True)
        - normed * jnp.mean(inner * normed, axis=-1, keepdims=True)
    ) * scaling


def eight_rows(entries):
    return entries.reshape(-1, 8, entries.shape[-1]).sum(axis=0)


def norm_one_kernel(levels_ref, tokens_ref, vec_ref, out_ref):
    normed, _ = normalised(hidden_tile(levels_ref, tokens_ref[...], vec_ref))
    out_ref[...] = (normed * vec_ref[0:1, :]).astype(low)


def norm_one(levels, tokens, vec_master):
    return pl.pallas_call(
        norm_one_kernel,
        grid_spec=pltpu.PrefetchScalarGridSpec(
            num_scalar_prefetch=1,
            grid=(ROWS // TILE,),
            in_specs=[rows_of(D), whole((VROWS, D))],
            out_specs=rows_of(D),
        ),
        out_shape=jax.ShapeDtypeStruct((ROWS, D), low),
        cost_estimate=pl.CostEstimate(
            flops=10 * ROWS * D, bytes_accessed=4 * ROWS * D, transcendentals=0
        ),
        compiler_params=params(),
        name="norm_one",
    )(levels, tokens, vec_master)


def turn(entries, cos, sin):
    return entries * cos + pltpu.roll(entries, HEAD_DIM, 1) * sin


PROJECT_TILE = 512


def project_kernel(pairs, place_ref, a_ref, w_hbm, cos_ref, sin_ref, out_ref, w_ref, semaphores):
    @pl.when(pl.program_id(0) == 0)
    def _():
        bring([w_hbm], [w_ref], place_ref[1], semaphores)

    weights = side_by_side(w_ref, range(3))
    for sub in range(PROJECT_TILE // TILE):
        rows = slice(sub * TILE, (sub + 1) * TILE)
        cos = cos_ref[rows, :]
        sin = sin_ref[rows, :]
        projected = dot(a_ref[rows, :], weights)
        for part in range(3):
            for pair in range(pairs):
                start = (part * pairs + pair) * PAIR
                columns = slice(start, start + PAIR)
                result = projected[:, columns]
                if part < 2:
                    result = turn(result, cos, sin)
                if part == 0:
                    result = result * HEAD_DIM**-0.5
                out_ref[rows, columns] = result.astype(low)


def project(places, attn_in, w_part, cos, sin):
    width = 3 * w_part.shape[4]
    table = pl.BlockSpec(
        (PROJECT_TILE, PAIR), lambda i, *_: (lax.rem(i, SEQ // PROJECT_TILE), 0)
    )
    return pl.pallas_call(
        partial(project_kernel, width // (3 * PAIR)),
        grid_spec=pltpu.PrefetchScalarGridSpec(
            num_scalar_prefetch=1,
            grid=(ROWS // PROJECT_TILE,),
            in_specs=[rows_of(D, PROJECT_TILE), anywhere, table, table],
            out_specs=rows_of(width, PROJECT_TILE),
            scratch_shapes=ordered_scratch([w_part]),
        ),
        out_shape=jax.ShapeDtypeStruct((ROWS, width), low),
        cost_estimate=pl.CostEstimate(
            flops=2 * ROWS * D * width, bytes_accessed=8 * ROWS * D, transcendentals=0
        ),
        compiler_params=params(),
        name="project",
    )(places, attn_in, w_part, cos, sin)


QT = 256
TILES = SEQ // QT
SHORTEST = 256


def fill_bias(length, same_ref, earlier_ref, causal_ref, length_ref):
    key = lax.broadcasted_iota(jnp.int32, (QT, QT), 0)
    query = lax.broadcasted_iota(jnp.int32, (QT, QT), 1)
    key_block = key // BLOCK
    query_block = query // BLOCK
    for tile in range(TILES):
        kept = key + tile * QT < length
        own = kept | (key == query)
        same_ref[tile] = jnp.where((key_block == query_block) & own, 0.0, masked_score)
        earlier_ref[tile] = jnp.where((key_block < query_block) & kept, 0.0, masked_score)
        causal_ref[tile] = jnp.where((key_block <= query_block) & own, 0.0, masked_score)
    position = lax.broadcasted_iota(jnp.int32, (SEQ, QT), 0)
    length_ref[...] = jnp.where(position < length, 0.0, masked_score)


bias_scratch = [
    pltpu.VMEM((TILES, QT, QT), full),
    pltpu.VMEM((TILES, QT, QT), full),
    pltpu.VMEM((TILES, QT, QT), full),
    pltpu.VMEM((SEQ, QT), full),
]


def segments(tile, noised):
    found = []
    if noised:
        found.append((tile * QT, QT, "same"))
        found.append((SEQ + tile * QT, QT, "earlier"))
    else:
        found.append((SEQ + tile * QT, QT, "causal"))
    before = tile * QT
    free = min(before, SHORTEST)
    if before > free:
        found.append((SEQ + free, before - free, "length"))
    if free > 0:
        found.append((SEQ, free, None))
    return found


def masked(scores, kind, tile, start, count, biases):
    same_ref, earlier_ref, causal_ref, length_ref = biases
    if kind == "same":
        return scores + same_ref[tile]
    if kind == "earlier":
        return scores + earlier_ref[tile]
    if kind == "causal":
        return scores + causal_ref[tile]
    if kind == "length":
        return scores + length_ref[start - SEQ : start - SEQ + count, :]
    return scores


def lane_masks(head, rows):
    lane = lax.broadcasted_iota(jnp.int32, (rows, PAIR), 1)
    halves = (lane // (HEAD_DIM // 2)) % 2 == head
    plain = lane // HEAD_DIM == head
    return halves, plain


def attend_kernel(aliased, scalar_ref, q_ref, k_ref, v_ref, *refs):
    o_ref, log_ref, *biases = refs[2:] if aliased else refs

    @pl.when(pl.program_id(0) == 0)
    def _():
        fill_bias(scalar_ref[0], *biases)

    units = [
        (head, tile, noised)
        for head in range(2)
        for tile in range(TILES)
        for noised in (True, False)
    ]

    def score(head, tile, noised):
        halves, _ = lane_masks(head, QT)
        row = tile * QT + (0 if noised else SEQ)
        query = jnp.where(halves, q_ref[row : row + QT, :], jnp.zeros((), low))
        parts = []
        for start, count, kind in segments(tile, noised):
            scores = dot(k_ref[start : start + count, :], query, 1, 1)
            parts.append((start, count, masked(scores, kind, tile, start, count, biases)))
        return parts

    def weigh(head, tile, noised, parts):
        row = tile * QT + (0 if noised else SEQ)
        row_max = None
        for start, count, scores in parts:
            top = jnp.max(scores, axis=0, keepdims=True)
            row_max = top if row_max is None else jnp.maximum(row_max, top)
        total = None
        weights = []
        for start, count, scores in parts:
            expo = jnp.exp(scores - row_max)
            part_total = jnp.sum(expo, axis=0, keepdims=True)
            total = part_total if total is None else total + part_total
            weights.append((start, count, expo.astype(low)))
        log_ref[0, head : head + 1, row : row + QT] = row_max + jnp.log(total)
        return weights, total

    def finish(head, tile, noised, weights, total):
        _, plain = lane_masks(head, QT)
        row = tile * QT + (0 if noised else SEQ)
        attended = None
        for start, count, expo in weights:
            product = dot(expo, v_ref[start : start + count, :], 0, 0)
            attended = product if attended is None else attended + product
        inverse = jnp.transpose(jnp.broadcast_to(1.0 / total, (PAIR, QT)))
        result = (attended * inverse).astype(low)
        o_ref[row : row + QT, :] = jnp.where(plain, result, o_ref[row : row + QT, :])

    parts = score(*units[0])
    held = None
    for index, unit in enumerate(units):
        following = score(*units[index + 1]) if index + 1 < len(units) else None
        weights = weigh(*unit, parts)
        if held is not None:
            finish(*held)
        held = (*unit, *weights)
        parts = following
    finish(*held)


def column_spec(offset):
    return pl.BlockSpec((ROWS, PAIR), lambda g, *_: (0, offset + g))


def pair_spec_from(first):
    return pl.BlockSpec((ROWS, PAIR), lambda g, scalars: (0, scalars[1] + first + g))


def log_spec_from(first):
    return pl.BlockSpec((1, 2, ROWS), lambda g, scalars: (scalars[1] + first + g, 0, 0))


pair_spec = pair_spec_from(0)
log_spec = log_spec_from(0)
PAIRS_SEEN = 1572864


def attend(scalars, qkv, before, first=0, count=None):
    pairs = qkv.shape[1] // (3 * PAIR)
    count = count or pairs
    aliased = before is not None
    kept = [pl.BlockSpec(memory_space=pl.ANY)] * 2 if aliased else []
    return pl.pallas_call(
        partial(attend_kernel, aliased),
        grid_spec=pltpu.PrefetchScalarGridSpec(
            num_scalar_prefetch=1,
            grid=(count,),
            in_specs=[
                column_spec(first), column_spec(pairs + first), column_spec(2 * pairs + first), *kept
            ],
            out_specs=[pair_spec_from(first), log_spec_from(first)],
            scratch_shapes=bias_scratch,
        ),
        out_shape=[
            jax.ShapeDtypeStruct((ROWS, D), low),
            jax.ShapeDtypeStruct((GROUPS, 2, ROWS), full),
        ],
        input_output_aliases={4: 0, 5: 1} if aliased else {},
        cost_estimate=pl.CostEstimate(
            flops=16 * PAIRS_SEEN * PAIR * count,
            bytes_accessed=8 * ROWS * PAIR * count,
            transcendentals=0,
        ),
        compiler_params=params(),
        name="attend",
    )(scalars, qkv, qkv, qkv, *(before or ()))


def attend_back_kernel(
    weighted, scalar_ref, q_ref, k_ref, v_ref, o_ref, grad_ref, log_ref, cos_ref, sin_ref, *refs
):
    a_ref, weight_ref = None, None
    if weighted:
        a_ref, grad_out_ref, weight_ref, *refs = refs
    else:
        grad_out_ref, *refs = refs
    q_acc, k_acc, v_acc, delta_acc, prob_ref, score_ref, own_prob_ref, own_score_ref = refs[:8]
    biases = refs[8:]

    @pl.when(pl.program_id(0) == 0)
    def _():
        fill_bias(scalar_ref[0], *biases)

    for row in range(0, ROWS, QT):
        product = o_ref[row : row + QT, :].astype(full) * grad_ref[row : row + QT, :].astype(full)
        turned = jnp.transpose(product)
        delta_acc[0:1, row : row + QT] = jnp.sum(turned[:HEAD_DIM], axis=0, keepdims=True)
        delta_acc[1:2, row : row + QT] = jnp.sum(turned[HEAD_DIM:], axis=0, keepdims=True)

    def products(head, tile, noised, start, count):
        halves, plain = lane_masks(head, QT)
        row = tile * QT + (0 if noised else SEQ)
        zero = jnp.zeros((), low)
        query = jnp.where(halves, q_ref[row : row + QT, :], zero)
        grad = jnp.where(plain, grad_ref[row : row + QT, :], zero)
        scores = dot(k_ref[start : start + count, :], query, 1, 1)
        return scores, dot(v_ref[start : start + count, :], grad, 1, 1)

    def keep(head, tile, noised, start, count, kind, pair):
        row = tile * QT + (0 if noised else SEQ)
        scores, prob_grad = pair
        scores = masked(scores, kind, tile, start, count, biases)
        probs = jnp.exp(scores - log_ref[0, head : head + 1, row : row + QT])
        delta = delta_acc[head : head + 1, row : row + QT]
        score_grad = (probs * (prob_grad - delta)).astype(low)
        if kind == "same":
            own_prob_ref[start : start + count, :] = probs.astype(low)
            own_score_ref[start : start + count, :] = score_grad
        else:
            key = start - SEQ
            prob_ref[key : key + count, row : row + QT] = probs.astype(low)
            score_ref[key : key + count, row : row + QT] = score_grad

    def put(ref, row, mask, value):
        ref[row : row + QT, :] = jnp.where(mask, value, ref[row : row + QT, :])

    def sums(head, tile):
        halves, plain = lane_masks(head, QT)
        row = tile * QT
        rows, clean_rows = slice(row, row + QT), slice(SEQ + row, SEQ + row + QT)
        seen = (slice(row, SEQ), slice(SEQ + row, ROWS))
        put(v_acc, row, plain, dot(own_prob_ref[rows, :], grad_ref[rows, :]))
        put(k_acc, row, halves, dot(own_score_ref[rows, :], q_ref[rows, :]))
        put(
            v_acc, SEQ + row, plain,
            dot(prob_ref[rows, seen[0]], grad_ref[seen[0], :])
            + dot(prob_ref[rows, seen[1]], grad_ref[seen[1], :]),
        )
        put(
            k_acc, SEQ + row, halves,
            dot(score_ref[rows, seen[0]], q_ref[seen[0], :])
            + dot(score_ref[rows, seen[1]], q_ref[seen[1], :]),
        )
        keys = k_ref[SEQ : SEQ + row + QT, :]
        put(
            q_acc, row, halves,
            dot(score_ref[: row + QT, rows], keys, 0, 0)
            + dot(own_score_ref[rows, :], k_ref[rows, :], 0, 0),
        )
        put(q_acc, SEQ + row, halves, dot(score_ref[: row + QT, clean_rows], keys, 0, 0))

    items = []
    for head in range(2):
        for tile in reversed(range(TILES)):
            for noised in (True, False):
                for start, count, kind in segments(tile, noised):
                    items.append((head, tile, noised, start, count, kind))
    waiting = []
    pair = products(*items[0][:5])
    for index, item in enumerate(items):
        following = None
        if index + 1 < len(items):
            following = products(*items[index + 1][:5])
        keep(*item, pair)
        pair = following
        if index + 1 == len(items) or items[index + 1][:2] != item[:2]:
            sums(*item[:2])
    for row in range(0, ROWS, QT):
        rows = slice(row, row + QT)
        cos = cos_ref[row % SEQ : row % SEQ + QT, :]
        sin = -sin_ref[row % SEQ : row % SEQ + QT, :]
        grad_out_ref[0, rows, :] = turn(q_acc[rows, :] * HEAD_DIM**-0.5, cos, sin).astype(low)
        grad_out_ref[1, rows, :] = turn(k_acc[rows, :], cos, sin).astype(low)
        grad_out_ref[2, rows, :] = v_acc[rows, :].astype(low)
    if weighted:
        parts = jnp.concatenate([grad_out_ref[part] for part in range(3)], axis=1)
        result = dot(a_ref[...], parts, 0, 0) * row_scale
        planes, narrow, _, rows, _ = weight_ref.shape
        for place in range(narrow):
            for plane in range(planes):
                start = (place * planes + plane) * rows
                for part in range(3):
                    block = result[start : start + rows, part * PAIR : (part + 1) * PAIR]
                    weight_ref[plane, place, part] = block.astype(low)


def attend_back(scalars, qkv, attended, grad, logs, cos, sin, attn_in=None, blocks=None):
    pairs = qkv.shape[1] // (3 * PAIR)
    table = whole((SEQ, PAIR))
    weighted = attn_in is not None
    out_specs = [pl.BlockSpec((3, ROWS, PAIR), lambda g, *_: (0, 0, g))]
    out_shape = [jax.ShapeDtypeStruct((3, ROWS, pairs * PAIR), low)]
    if weighted:
        shape = (*blocks, 3, D // (blocks[0] * blocks[1]))
        out_specs.append(pl.BlockSpec((*shape, PAIR), lambda g, *_: (0, 0, 0, 0, g)))
        out_shape.append(jax.ShapeDtypeStruct((*shape, pairs * PAIR), low))
    return pl.pallas_call(
        partial(attend_back_kernel, weighted),
        grid_spec=pltpu.PrefetchScalarGridSpec(
            num_scalar_prefetch=1,
            grid=(pairs,),
            in_specs=[
                column_spec(0), column_spec(pairs), column_spec(2 * pairs),
                pair_spec, pair_spec, log_spec, table, table,
                *([whole((ROWS, D))] if weighted else []),
            ],
            out_specs=out_specs,
            scratch_shapes=[
                pltpu.VMEM((ROWS, PAIR), full),
                pltpu.VMEM((ROWS, PAIR), full),
                pltpu.VMEM((ROWS, PAIR), full),
                pltpu.VMEM((8, ROWS), full),
                pltpu.VMEM((SEQ, ROWS), low),
                pltpu.VMEM((SEQ, ROWS), low),
                pltpu.VMEM((SEQ, QT), low),
                pltpu.VMEM((SEQ, QT), low),
                *bias_scratch,
            ],
        ),
        out_shape=out_shape,
        cost_estimate=pl.CostEstimate(
            flops=40 * PAIRS_SEEN * PAIR * pairs,
            bytes_accessed=16 * ROWS * PAIR * pairs,
            transcendentals=0,
        ),
        compiler_params=params(),
        name="attend_back",
    )(
        scalars, qkv, qkv, qkv, attended, grad, logs, cos, sin,
        *([attn_in] if weighted else []),
    )


root_two_pi = 0.7978845608028654
cubic = 0.044715


HALF = D // 2
FF_HALF = FF // 2


FEED_TILE = 512
SUB = 256


def feed_kernel(
    levels_ref, side_ref, tokens_ref, o_ref, dy_ref, vec_ref, bias_ref,
    wide_mine_hbm, wide_other_hbm, down_mine_hbm, down_other_hbm,
    y_ref, b_ref, gl_ref, du_ref, dr_ref, drb_ref, do_ref, sums_ref, upsum_ref,
    wide_mine, wide_other, down_mine, down_other, semaphores
):
    copies = all_copies(
        [wide_mine_hbm, wide_other_hbm, down_mine_hbm, down_other_hbm],
        [wide_mine, wide_other, down_mine, down_other],
        side_ref[1],
        semaphores,
    )

    @pl.when(pl.program_id(0) == 0)
    def _():
        for copy in copies:
            copy.start()
        sums_ref[...] = jnp.zeros_like(sums_ref)
        upsum_ref[...] = jnp.zeros_like(upsum_ref)
        for copy in copies[: len(copies) // 2]:
            copy.wait()

    swapped = side_ref[0] == 1
    gain = vec_ref[1:2, :]
    subs = FEED_TILE // SUB

    def in_order(mine, other):
        return jnp.concatenate(
            [jnp.where(swapped, other, mine), jnp.where(swapped, mine, other)], axis=1
        )

    def weights(part):
        wide_ref, down_ref = (wide_mine, down_mine) if part < 2 else (wide_other, down_other)
        inner = part % 2
        up = side_by_side(wide_ref, (inner * 2, inner * 2 + 1))
        return up, down_ref[0, inner * D : (inner + 1) * D, :]

    def head(sub):
        rows = slice(sub * SUB, (sub + 1) * SUB)
        attended = o_ref[rows, :]
        hidden = hidden_tile(levels_ref, tokens_ref[rows, :], vec_ref, sub, subs)
        resid = hidden + in_order(
            dot(attended, wide_mine[UP_ROWS]), dot(attended, wide_other[UP_ROWS])
        )
        normed, scaling = normalised(resid)
        mlp_in = (normed * gain).astype(low)
        b_ref[rows, :] = mlp_in
        return normed, scaling, mlp_in, resid + vec_ref[2:3, :]

    def products(sub, part, mlp_in):
        up, down = weights(part)
        rows = slice(sub * SUB, (sub + 1) * SUB)
        columns = slice(part * D, (part + 1) * D)
        return dot(mlp_in, up) + bias_ref[:, columns], dot(dy_ref[rows, :], down, 1, 1)

    def bend(sub, part, pre, act_grad):
        rows = slice(sub * SUB, (sub + 1) * SUB)
        columns = slice(part * D, (part + 1) * D)
        square = pre * pre
        bent = jnp.tanh(pre * (root_two_pi + (cubic * root_two_pi) * square))
        half = 0.5 + 0.5 * bent
        act = (pre * half).astype(low)
        slope = half + (0.5 * pre) * (1.0 - bent * bent) * (
            root_two_pi + (3.0 * cubic * root_two_pi) * square
        )
        pre_grad = act_grad * slope
        pre_low = pre_grad.astype(low)
        gl_ref[rows, columns] = act
        du_ref[rows, columns] = pre_low
        upsum_ref[:, columns] += eight_rows(pre_grad)
        return act, pre_low

    def main(sub, mlp_in, result):
        back = None
        ahead = products(sub, 0, mlp_in)
        for part in range(UP_ROWS):
            pair = ahead
            if part + 1 < UP_ROWS:
                ahead = products(sub, part + 1, mlp_in)
            act, pre_low = bend(sub, part, *pair)
            up, down = weights(part)
            result = result + dot(act, down)
            term = dot(pre_low, up, 1, 1)
            back = term if back is None else back + term
        return result, back

    def tail(sub, normed, scaling, result, back):
        rows = slice(sub * SUB, (sub + 1) * SUB)
        y_ref[rows, :] = result.astype(low)
        dy_full = dy_ref[rows, :].astype(full)
        sums_ref[0:8, :] += eight_rows(back * normed)
        sums_ref[8:16, :] += eight_rows(dy_full)
        resid_grad = dy_full + norm_back(normed, scaling, gain, back)
        dr_ref[rows, :] = resid_grad
        drb_ref[rows, :] = resid_grad.astype(low)
        first, second = resid_grad[:, :HALF], resid_grad[:, HALF:]
        mine = jnp.where(swapped, second, first).astype(low)
        other = jnp.where(swapped, first, second).astype(low)
        do_ref[rows, :] = (
            dot(mine, wide_mine[UP_ROWS], 1, 1) + dot(other, wide_other[UP_ROWS], 1, 1)
        ).astype(low)

    state = head(0)

    @pl.when(pl.program_id(0) == 0)
    def _():
        for copy in copies[len(copies) // 2 :]:
            copy.wait()

    for sub in range(subs):
        normed, scaling, mlp_in, result = state
        result, back = main(sub, mlp_in, result)
        if sub + 1 < subs:
            state = head(sub + 1)
        tail(sub, normed, scaling, result, back)


def feed(levels, side, tokens, attended, cotangent, vec_master, bias, weights):
    def out(width, kind=low):
        return jax.ShapeDtypeStruct((ROWS, width), kind)

    def rows(width):
        return rows_of(width, FEED_TILE)

    return pl.pallas_call(
        feed_kernel,
        grid_spec=pltpu.PrefetchScalarGridSpec(
            num_scalar_prefetch=2,
            grid=(ROWS // FEED_TILE,),
            in_specs=[
                rows(D), rows(D), rows(D), whole((VROWS, D)), whole((1, FF)), *[anywhere] * 4
            ],
            out_specs=[
                rows(D), rows(D), rows(FF), rows(FF), rows(D), rows(D), rows(D),
                pl.BlockSpec((16, D), lambda i, *_: (0, 0)),
                pl.BlockSpec((8, FF), lambda i, *_: (0, 0)),
            ],
            scratch_shapes=ordered_scratch(weights),
        ),
        out_shape=[
            out(D), out(D), out(FF), out(FF), out(D, full), out(D), out(D),
            jax.ShapeDtypeStruct((16, D), full), jax.ShapeDtypeStruct((8, FF), full),
        ],
        cost_estimate=pl.CostEstimate(
            flops=ROWS * D * (4 * D + 8 * FF), bytes_accessed=30 * ROWS * D, transcendentals=0
        ),
        compiler_params=params(),
        name="feed",
    )(levels, side, tokens, attended, cotangent, vec_master, bias, *weights)


def weight_kernel(added, scalar_ref, x_ref, y_ref, *refs):
    out_ref = refs[-1]
    result = dot(x_ref[...], y_ref[...], 0, 0) * row_scale
    planes, narrow, _, rows, _ = out_ref.shape
    for place in range(narrow):
        for plane in range(planes):
            start = (place * planes + plane) * rows
            block = result[start : start + rows]
            if added:
                block = block + refs[0][plane, place, 0].astype(full)
            out_ref[plane, place, 0] = block.astype(low)


def weight_call(name, count, x_spec, y_spec, out_spec, shape, first, x, y, added):
    return pl.pallas_call(
        partial(weight_kernel, added is not None),
        grid_spec=pltpu.PrefetchScalarGridSpec(
            num_scalar_prefetch=1,
            grid=(count,),
            in_specs=[x_spec, y_spec, *([out_spec] if added is not None else [])],
            out_specs=out_spec,
        ),
        out_shape=jax.ShapeDtypeStruct(shape, low),
        cost_estimate=pl.CostEstimate(
            flops=4 * ROWS * count * D * HALF, bytes_accessed=8 * ROWS * D, transcendentals=0
        ),
        compiler_params=params(),
        name=name,
    )(jnp.asarray(first, jnp.int32).reshape(1), x, y, *([added] if added is not None else []))


def grad_of_columns(blocks, x, y, first, count, added=None):
    planes, narrow = blocks
    rows = D // (planes * narrow)
    if y.ndim == 3:
        y_spec = pl.BlockSpec((None, ROWS, HALF), lambda j, s: (s[0] + j, 0, 0))
    else:
        y_spec = pl.BlockSpec((ROWS, HALF), lambda j, s: (0, s[0] + j))
    return weight_call(
        "grad_of_columns",
        count,
        pl.BlockSpec((ROWS, D), lambda j, s: (0, 0)),
        y_spec,
        pl.BlockSpec((planes, narrow, 1, rows, HALF), lambda j, s: (0, 0, j, 0, 0)),
        (planes, narrow, count, rows, HALF),
        first, x, y, added,
    )


def wide_kernel(added, side_ref, x_ref, y_ref, o_hbm, dr_hbm, *refs):
    out_ref, o_ref, dr_ref, semaphores = refs[-4:]
    step = pl.program_id(0)
    column = pl.multiple_of(side_ref[1] * HALF, HALF)
    copies = [
        pltpu.make_async_copy(o_hbm, o_ref, semaphores.at[0]),
        pltpu.make_async_copy(dr_hbm.at[:, pl.ds(column, HALF)], dr_ref, semaphores.at[1]),
    ]

    def store(result):
        planes, narrow, _, rows, _ = out_ref.shape
        for place in range(narrow):
            for plane in range(planes):
                start = (place * planes + plane) * rows
                block = result[start : start + rows] * row_scale
                if added:
                    block = block + refs[0][plane, place, 0].astype(full)
                out_ref[plane, place, 0] = block.astype(low)

    @pl.when(step == 0)
    def _():
        for copy in copies:
            copy.start()

    @pl.when(step < UP_ROWS)
    def _():
        store(dot(x_ref[...], y_ref[...], 0, 0))

    @pl.when(step == UP_ROWS)
    def _():
        for copy in copies:
            copy.wait()
        store(dot(o_ref[...], dr_ref[...], 0, 0))


def grad_of_wide(blocks, x, y, first, attended, resid_low, side, added=None):
    planes, narrow = blocks
    rows = D // (planes * narrow)
    count = UP_ROWS + 1
    out_spec = pl.BlockSpec((planes, narrow, 1, rows, HALF), lambda j, s: (0, 0, j, 0, 0))
    return pl.pallas_call(
        partial(wide_kernel, added is not None),
        grid_spec=pltpu.PrefetchScalarGridSpec(
            num_scalar_prefetch=1,
            grid=(count,),
            in_specs=[
                whole((ROWS, D)),
                pl.BlockSpec(
                    (ROWS, HALF), lambda j, s: (0, s[0] + jnp.minimum(j, UP_ROWS - 1))
                ),
                anywhere,
                anywhere,
                *([out_spec] if added is not None else []),
            ],
            out_specs=out_spec,
            scratch_shapes=[
                pltpu.VMEM((ROWS, D), low),
                pltpu.VMEM((ROWS, HALF), low),
                pltpu.SemaphoreType.DMA((2,)),
            ],
        ),
        out_shape=jax.ShapeDtypeStruct((planes, narrow, count, rows, HALF), low),
        cost_estimate=pl.CostEstimate(
            flops=4 * ROWS * count * D * HALF, bytes_accessed=8 * ROWS * D, transcendentals=0
        ),
        compiler_params=params(),
        name="grad_of_wide",
    )(
        jnp.stack([jnp.int32(first), side]), x, y, attended, resid_low,
        *([added] if added is not None else []),
    )


def grad_of_rows(blocks, x, y, first, count, added=None):
    planes, narrow = blocks
    if planes == 1:
        rows = HALF
        out_spec = pl.BlockSpec((1, 1, 1, rows, D), lambda i, s: (0, 0, 0, i, 0))
        shape = (1, 1, 1, count * HALF, D)
    else:
        rows = HALF // planes
        out_spec = pl.BlockSpec((planes, 1, 1, rows, D), lambda i, s: (0, i, 0, 0, 0))
        shape = (planes, count, 1, rows, D)
    return weight_call(
        "grad_of_rows",
        count,
        pl.BlockSpec((ROWS, HALF), lambda i, s: (0, s[0] + i)),
        pl.BlockSpec((ROWS, D), lambda i, s: (0, 0)),
        out_spec,
        shape,
        first, x, y, added,
    )


ENTRY_TILE = 512


def entry_kernel(count, levels_ref, place_ref, tokens_ref, dr_ref, vec_ref, *refs):
    step = pl.program_id(0)
    grads, sources = refs[:count], refs[count : 2 * count]
    grad_ref, gain_ref, table_ref = refs[2 * count : 2 * count + 3]
    weights, semaphores = refs[2 * count + 3 : -1], refs[-1]

    @pl.when(step == 0)
    def _():
        gain_ref[...] = jnp.zeros_like(gain_ref)
        table_ref[...] = jnp.zeros_like(table_ref)
        bring(sources, weights, place_ref[1], semaphores)

    matrices = [side_by_side(weight, range(3)) for weight in weights]
    per_tile = TILE // BLOCK
    subs = ENTRY_TILE // TILE
    for sub in range(subs):
        rows = slice(sub * TILE, (sub + 1) * TILE)
        back = None
        for grad, matrix in zip(grads, matrices):
            parts = jnp.concatenate([grad[part, rows, :] for part in range(3)], axis=1)
            term = dot(parts, matrix, 1, 1)
            back = term if back is None else back + term
        hidden = hidden_tile(levels_ref, tokens_ref[rows, :], vec_ref, sub, subs)
        normed, scaling = normalised(hidden)
        gain_ref[...] += eight_rows(back * normed)
        result = dr_ref[rows, :] + norm_back(normed, scaling, vec_ref[0:1, :], back)
        grad_ref[rows, :] = result

    @pl.when(step < SEQ // ENTRY_TILE)
    def _():
        for sub in range(subs):
            sums = grad_ref[sub * TILE : (sub + 1) * TILE, :]
            sums = sums.reshape(per_tile, BLOCK, D).sum(axis=1)
            for block in range(per_tile):
                level = levels_ref[(step * subs + sub) * per_tile + block]
                table_ref[pl.ds(level, 1), :] += sums[block : block + 1, :]


def entry(levels, places, tokens, resid_grad, vec_master, grads, weights):
    count = len(weights)
    return pl.pallas_call(
        partial(entry_kernel, count),
        grid_spec=pltpu.PrefetchScalarGridSpec(
            num_scalar_prefetch=2,
            grid=(ROWS // ENTRY_TILE,),
            in_specs=[rows_of(D, ENTRY_TILE), rows_of(D, ENTRY_TILE), whole((VROWS, D))]
            + [
                pl.BlockSpec((3, ENTRY_TILE, grad.shape[2]), lambda i, *_: (0, i, 0))
                for grad in grads
            ]
            + [anywhere] * count,
            out_specs=[
                rows_of(D, ENTRY_TILE),
                pl.BlockSpec((8, D), lambda i, *_: (0, 0)),
                pl.BlockSpec((LEVELS, D), lambda i, *_: (0, 0)),
            ],
            scratch_shapes=ordered_scratch(weights),
        ),
        out_shape=[
            jax.ShapeDtypeStruct((ROWS, D), full),
            jax.ShapeDtypeStruct((8, D), full),
            jax.ShapeDtypeStruct((LEVELS, D), full),
        ],
        cost_estimate=pl.CostEstimate(
            flops=6 * ROWS * D * D, bytes_accessed=20 * ROWS * D, transcendentals=0
        ),
        compiler_params=params(),
        name="entry",
    )(levels, places, tokens, resid_grad, vec_master, *grads, *weights)


PARTS = (3, 1, 4)


def swapped_halves(entries):
    lane = lax.broadcasted_iota(jnp.int32, entries.shape, 1) % PAIR
    quarter = HEAD_DIM // 2
    width = entries.shape[1]
    ahead = pltpu.roll(entries, width - quarter, 1)
    behind = pltpu.roll(entries, quarter, 1)
    second = (lane >= quarter) & (lane < 2 * quarter)
    third = (lane >= 2 * quarter) & (lane < 3 * quarter)
    return jnp.where(second, ahead, jnp.where(third, behind, entries))


def slot_pieces(kind, wide):
    planes = wide // 2
    found = []
    for plane in range(planes):
        for half in range(2):
            place = 2 * plane + half
            if kind < 3:
                parts, rows = PARTS[kind], D // 4 // planes
                for part in range(parts):
                    where = pl.ds(plane * rows * parts + part, rows, stride=parts)
                    found.append((place, part, part * rows, rows, where, half * HALF))
            else:
                rows = HALF // planes
                for column in range(2):
                    where = pl.ds(half * HALF + plane * rows, rows)
                    found.append((place, 2, column * rows, rows, where, column * HALF))
    return found


LANES = 128


def pack_kernel(owners_ref, slot_ref, out_ref, stage_ref):
    place = lax.axis_index("wide")
    wide = out_ref.shape[0]
    for index in range(D // LANES):
        stage_ref[index] = slot_ref[:, index * LANES : (index + 1) * LANES]
    for kind in range(4):

        @pl.when(owners_ref[kind] == place)
        def _(kind=kind):
            for target, part, start, rows, where, column in slot_pieces(kind, wide):
                for index in range(HALF // LANES):
                    block = stage_ref[column // LANES + index, where, :]
                    if kind == 0 and part < 2:
                        block = swapped_halves(block)
                    columns = slice(index * LANES, (index + 1) * LANES)
                    out_ref[target, start : start + rows, columns] = block.astype(low)


def pack(owners, slot):
    wide = lax.axis_size("wide")
    shape = (wide, 2 * D // wide, HALF)
    return pl.pallas_call(
        pack_kernel,
        grid_spec=pltpu.PrefetchScalarGridSpec(
            num_scalar_prefetch=1,
            grid=(1,),
            in_specs=[whole(slot.shape)],
            out_specs=whole(shape),
            scratch_shapes=[pltpu.VMEM((D // LANES, slot.shape[0], LANES), full)],
        ),
        out_shape=jax.ShapeDtypeStruct(shape, low),
        cost_estimate=pl.CostEstimate(
            flops=D * D, bytes_accessed=6 * D * D, transcendentals=0
        ),
        compiler_params=params(16),
        name="pack",
    )(owners, slot)


def settle_kernel(owners_ref, qkv_ref, wide_ref, down_ref, out_ref):
    squares = jnp.zeros((8, HALF), full)

    def summed(ref, part):
        result = ref[0, part].astype(full)
        for index in range(1, ref.shape[0]):
            result = result + ref[index, part].astype(full)
        return result.astype(low)

    out_ref[...] = jnp.zeros_like(out_ref)
    for kind in range(4):
        target = owners_ref[kind]
        for part in range((3, 1, 4, 1)[kind]):
            if kind == 0:
                share = summed(qkv_ref, part)
            elif kind < 3:
                share = summed(wide_ref, UP_ROWS if kind == 1 else part)
            else:
                share = summed(down_ref, 0)
            rows = share.shape[0]
            for column in range(share.shape[1] // HALF):
                block = share[:, column * HALF : (column + 1) * HALF]
                start = (part + column) * rows
                out_ref[target, start : start + rows, :] = block
                entries = block.astype(full)
                squares = squares + eight_rows(entries * entries)
    rest = jnp.sum(squares, keepdims=True)
    rows = out_ref.shape[1] - 16
    for index in range(3):
        term = rest.astype(low)
        rest = rest - term.astype(full)
        terms = jnp.broadcast_to(term, (16, LANES))
        columns = slice(index * LANES, (index + 1) * LANES)
        for target in range(out_ref.shape[0]):
            out_ref[target, rows:, columns] = terms


def square_sums_kernel(came_ref, vec_ref, out_ref):
    total = jnp.zeros((1, LANES), full)
    for source in range(came_ref.shape[0]):
        for index in reversed(range(3)):
            columns = slice(index * LANES, (index + 1) * LANES)
            total = total + came_ref[source, :, columns].astype(full)[0:1]
    out_ref[0:VROWS, :] = vec_ref[...]
    out_ref[VROWS:, :] = jnp.concatenate([total] * (D // LANES), axis=1)


def square_sums(came, vec_wide):
    wide, rows, _ = came.shape
    return pl.pallas_call(
        square_sums_kernel,
        grid=(1,),
        in_specs=[
            pl.BlockSpec((wide, 16, HALF), lambda i: (0, rows // 16 - 1, 0)),
            whole((VROWS, D)),
        ],
        out_specs=whole((VROWS + 1, D)),
        out_shape=jax.ShapeDtypeStruct((VROWS + 1, D), full),
        compiler_params=params(16),
        name="square_sums",
    )(came, vec_wide)


def settle(owners, qkv, wide_parts, down):
    wide = lax.axis_size("wide")
    shape = (wide, 2 * D // wide + 16, HALF)
    return pl.pallas_call(
        settle_kernel,
        grid_spec=pltpu.PrefetchScalarGridSpec(
            num_scalar_prefetch=1,
            grid=(1,),
            in_specs=[whole(qkv.shape), whole(wide_parts.shape), whole(down.shape)],
            out_specs=whole(shape),
        ),
        out_shape=jax.ShapeDtypeStruct(shape, low),
        cost_estimate=pl.CostEstimate(
            flops=4 * D * D, bytes_accessed=6 * D * D, transcendentals=0
        ),
        compiler_params=params(16),
        name="settle",
    )(owners, qkv, wide_parts, down)


FINISH_ROWS = 192
held = pl.BlockSpec(memory_space=pltpu.VMEM)


def unpack_kernel(owners_ref, came_ref, out_ref, grad_ref):
    place = lax.axis_index("wide")
    wide = came_ref.shape[0]
    for kind in range(4):

        @pl.when(owners_ref[kind] == place)
        def _(kind=kind):
            for source, part, start, rows, where, column in slot_pieces(kind, wide):
                block = came_ref[source, start : start + rows, :].astype(full)
                for index in range(HALF // LANES):
                    piece = block[:, index * LANES : (index + 1) * LANES]
                    if kind == 0 and part < 2:
                        piece = swapped_halves(piece)
                    grad_ref[column // LANES + index, where, :] = piece

    for index in range(D // LANES):
        out_ref[:, index * LANES : (index + 1) * LANES] = grad_ref[index]


def unpack(owners, slot_rows, came):
    return pl.pallas_call(
        unpack_kernel,
        grid_spec=pltpu.PrefetchScalarGridSpec(
            num_scalar_prefetch=1,
            grid=(1,),
            in_specs=[whole(came.shape)],
            out_specs=held,
            scratch_shapes=[pltpu.VMEM((D // LANES, slot_rows, LANES), full)],
        ),
        out_shape=jax.ShapeDtypeStruct((slot_rows, D), full),
        cost_estimate=pl.CostEstimate(
            flops=2 * D * D, bytes_accessed=6 * D * D, transcendentals=0
        ),
        compiler_params=params(16),
        name="unpack",
    )(owners, came)


def finish_kernel(
    owners_ref, grad_ref, sums_ref, vec_moment_ref, vec_square_ref, vec_master_ref,
    moment_ref, square_ref, master_ref,
    master_out, moment_out, square_out, vec_grad_out, vec_moment_out, vec_square_out,
    vec_master_out, norm_out
):
    step = pl.program_id(0)
    place = lax.axis_index("wide")
    here = lax.axis_index("narrow")
    narrow = sums_ref.shape[0]
    total = sums_ref[here]
    for index in range(1, narrow):
        total = total + sums_ref[lax.rem(here - index + narrow, narrow)]
    vec, total = total[:VROWS], total[VROWS:, 0:1]
    norm = jnp.sqrt(total + jnp.sum(vec * vec, keepdims=True))
    clip = jnp.minimum(1.0, 1.0 / (norm + 1e-06))

    @pl.when(step == 0)
    def _():
        norm_out[...] = norm
        vec_clipped = vec * clip
        vec_grad_out[...] = vec_clipped
        vec_moment_out[...], vec_square_out[...], vec_master_out[...] = adam(
            vec_clipped, vec_moment_ref[...], vec_square_ref[...], vec_master_ref[...],
            0.0, vector_rate,
        )

    used = jnp.int32(0)
    for kind in range(4):
        rows = D // 4 * (PARTS[kind] if kind < 3 else 4)
        used = jnp.where(owners_ref[kind] == place, rows, used)
    row = step * FINISH_ROWS + lax.broadcasted_iota(jnp.int32, (FINISH_ROWS, D), 0)
    rows = pl.ds(pl.multiple_of(step * FINISH_ROWS, FINISH_ROWS), FINISH_ROWS)
    kept = row < used
    moment_new, square_new, master_new = adam(
        jnp.where(kept, grad_ref[rows, :] * clip, 0.0),
        moment_ref[rows, :], square_ref[rows, :], master_ref[rows, :], decay_rate, learn_rate,
    )
    master_out[...] = jnp.where(kept, master_new, 0.0)
    moment_out[...] = jnp.where(kept, moment_new, 0.0)
    square_out[...] = jnp.where(kept, square_new, 0.0)


def finish(owners, grad, sums, vec_states, states):
    rows = states[0].shape[0]
    state_spec = pl.BlockSpec((FINISH_ROWS, D), lambda i, *_: (i, 0))
    vec_spec = whole((VROWS, D))
    state = jax.ShapeDtypeStruct((rows, D), full)
    vec = jax.ShapeDtypeStruct((VROWS, D), full)
    return pl.pallas_call(
        finish_kernel,
        grid_spec=pltpu.PrefetchScalarGridSpec(
            num_scalar_prefetch=1,
            grid=(rows // FINISH_ROWS,),
            in_specs=[held, held, *[vec_spec] * 3, *[held] * 3],
            out_specs=[*[state_spec] * 3, *[vec_spec] * 4, whole((1, 1))],
        ),
        out_shape=[state] * 3 + [vec] * 4 + [jax.ShapeDtypeStruct((1, 1), full)],
        cost_estimate=pl.CostEstimate(
            flops=20 * D * D, bytes_accessed=26 * D * D, transcendentals=0
        ),
        compiler_params=params(24),
        name="finish",
    )(owners, grad, sums, *vec_states, *states)


def turn_tables():
    positions = jnp.arange(SEQ, dtype=jnp.int32).astype(full)
    exponents = jnp.arange(HEAD_DIM // 2, dtype=full) * (2.0 / HEAD_DIM)
    angles = positions[:, None] * (rope_base ** (-exponents))[None, :]
    cos = jnp.cos(angles)
    sin = jnp.sin(angles)
    return (
        jnp.concatenate([cos, cos, cos, cos], axis=1),
        jnp.concatenate([-sin, -sin, sin, sin], axis=1),
    )


def adam(grad, moment, square, master, decay, rate):
    moment_new = moment_decay * moment + (1.0 - moment_decay) * grad
    square_new = moment_decay * square + (1.0 - moment_decay) * grad * grad
    correction = 1.0 - moment_decay**STEP
    master_new = master * (1.0 - rate * decay) - rate * (moment_new / correction) / (
        jnp.sqrt(square_new / correction) + adam_eps
    )
    return (moment_new, square_new, master_new)


def flip(value, axis, bits):
    count = lax.axis_size(axis)
    return lax.ppermute(value, axis, [(i, i ^ bits) for i in range(count)])


def planes_groups():
    count = lax.axis_size("wide")
    return [list(range(start, count, 2)) for start in range(2)]


def shift(value, step):
    count = lax.axis_size("narrow")
    return lax.ppermute(value, "narrow", [(i, (i + step) % count) for i in range(count)])


def swap_planes(blocks):
    return lax.all_to_all(blocks, "wide", 0, 0, axis_index_groups=planes_groups())


def copies(value, count):
    return jnp.broadcast_to(value[None], (count, *value.shape))


def after(value, *others):
    return lax.optimization_barrier((value, *others))[0]


def gather_narrow(share):
    return [share] + [shift(share, step) for step in range(1, lax.axis_size("narrow"))]


def gather_planes(held):
    held = swap_planes(copies(jnp.stack(held), lax.axis_size("wide") // 2))
    if held.shape[3] % 16 == 0:
        return held
    narrow, parts, columns = held.shape[1], held.shape[2], held.shape[4]
    order = (lax.axis_index("narrow") - jnp.arange(narrow)) % narrow
    held = jnp.take(held, order, axis=1)
    return held.transpose(2, 1, 0, 3, 4).reshape(1, 1, parts, -1, columns)


def total(blocks):
    return jnp.sum(blocks.astype(full), axis=0).astype(low)


def reduce_planes(matrix):
    planes, narrow = lax.axis_size("wide") // 2, lax.axis_size("narrow")
    if matrix.shape[0] != planes:
        parts, columns = matrix.shape[2], matrix.shape[4]
        matrix = matrix.reshape(parts, narrow, planes, -1, columns)
        matrix = matrix.transpose(2, 1, 0, 3, 4)
    return total(swap_planes(matrix))


def narrow_pieces(held):
    count = lax.axis_size("narrow")
    place = lax.axis_index("narrow")

    def part(step):
        return lax.dynamic_index_in_dim(held, (place + step) % count, 0, keepdims=False)

    return [part(0)] + [shift(part(step), step) for step in range(1, count)]


def swap_halves(matrix):
    pairs = matrix.reshape(*matrix.shape[:-1], -1, 2, 2, HEAD_DIM // 2)
    return jnp.swapaxes(pairs, -3, -2).reshape(matrix.shape)


def plain_layouts(slot_rows):
    wide = lax.axis_size("wide")
    planes, most = wide // 2, 2 * D // wide
    rows, deep = D // 4 // planes, HALF // planes

    def pack_columns(kind, slot):
        parts = PARTS[kind]
        blocks = slot[: rows * planes * parts].reshape(planes, rows, parts, 2, HALF)
        blocks = blocks.transpose(0, 3, 2, 1, 4)
        if kind == 0:
            blocks = jnp.concatenate([swap_halves(blocks[:, :, :2]), blocks[:, :, 2:]], axis=2)
        blocks = blocks.reshape(wide, parts * rows, HALF)
        return jnp.pad(blocks, ((0, 0), (0, most - parts * rows), (0, 0)))

    def unpack_columns(kind, blocks):
        parts = PARTS[kind]
        blocks = blocks[:, : parts * rows].reshape(planes, 2, parts, rows, HALF)
        if kind == 0:
            blocks = jnp.concatenate([swap_halves(blocks[:, :, :2]), blocks[:, :, 2:]], axis=2)
        flat = blocks.transpose(0, 3, 2, 1, 4).reshape(planes * rows * parts, D)
        return jnp.pad(flat, ((0, slot_rows - flat.shape[0]), (0, 0)))

    def pack_down(slot):
        blocks = slot.reshape(2, planes, deep, 2, HALF)
        return blocks.transpose(1, 0, 3, 2, 4).reshape(wide, 2 * deep, HALF)

    def unpack_down(blocks):
        blocks = blocks.reshape(planes, 2, 2, deep, HALF)
        return blocks.transpose(1, 0, 3, 2, 4).reshape(slot_rows, D)

    packs = [partial(pack_columns, kind) for kind in range(3)] + [pack_down]
    unpacks = [partial(unpack_columns, kind) for kind in range(3)] + [unpack_down]
    packs.append(lambda slot: jnp.zeros((wide, most, HALF), slot.dtype))
    unpacks.append(lambda blocks: jnp.zeros((slot_rows, D), blocks.dtype))
    return packs, unpacks


def plain_pack(kind, slot):
    return lax.switch(kind, plain_layouts(slot.shape[0])[0], slot.astype(low))


def plain_settle(owners, qkv, wide_parts, down):
    wide = lax.axis_size("wide")
    qkv, wide_parts, down = total(qkv), total(wide_parts), total(down)
    down = jnp.stack([down[0, :, :HALF], down[0, :, HALF:]])
    places = jnp.arange(wide, dtype=jnp.int32)[:, None, None]
    sent = jnp.zeros((wide, 2 * D // wide, HALF), low)
    squares = jnp.zeros((), full)
    shares = (qkv, wide_parts[UP_ROWS:], wide_parts[:UP_ROWS], down)
    for kind, share in enumerate(shares):
        share = share.reshape(-1, HALF)
        squares = squares + jnp.sum(jnp.square(share.astype(full)))
        block = jnp.pad(share, ((0, sent.shape[1] - share.shape[0]), (0, 0)))[None]
        sent = jnp.where(places == owners[kind], block, sent)
    return sent, jnp.broadcast_to(squares, (1, D))


def plain_unpack(kind, slot_rows, came):
    return lax.switch(kind, plain_layouts(slot_rows)[1], came).astype(full)


def sum_over_wide(value):
    wide = lax.axis_size("wide")
    bit = 1
    while bit < wide:
        value = value + flip(value, "wide", bit)
        bit *= 2
    return value


def local(
    tokens,
    cotangent,
    lengths,
    levels,
    owners,
    master_slots,
    moment_slots,
    square_slots,
    vec_master,
    vec_moment,
    vec_square,
):
    narrow = lax.axis_size("narrow")
    wide = lax.axis_size("wide")
    side = lax.axis_index("wide") & 1
    planes = wide // 2
    rows = D // (narrow * planes)
    deep = FF // 2 // (narrow * planes)

    plain = rows % 16 != 0
    owned = owners == lax.axis_index("wide")
    kind = jnp.where(jnp.any(owned), jnp.argmax(owned), 4).astype(jnp.int32)
    if plain:
        packed = plain_pack(kind, master_slots[0])
    else:
        packed = pack(owners, master_slots[0])
    came = lax.all_to_all(packed, "wide", 0, 0)

    def share(came, kind, count):
        return lax.dynamic_index_in_dim(came, owners[kind], 0, keepdims=False)[:count]

    qkv_share = share(came, 0, 3 * rows).reshape(3, rows, HALF)

    tokens = tokens.reshape(ROWS, D)
    cotangent = cotangent.reshape(ROWS, D)
    levels = levels.reshape(-1)
    here = jnp.stack([side, lax.axis_index("narrow")]).astype(jnp.int32)
    cos, sin = turn_tables()
    bias = vec_master[3 : 3 + UP_ROWS].reshape(UP_ROWS, 2, HALF)
    bias = jnp.stack([bias[:, 0], bias[:, 1]])
    bias = jnp.where(side == 1, bias[::-1], bias).reshape(1, FF)
    half_pairs = GROUPS // 2
    scalars = [
        jnp.stack([lengths[0], half_pairs * half]) for half in (side, 1 - side)
    ]
    attn_in = norm_one(levels, tokens, vec_master)

    qkv_plane = gather_narrow(after(qkv_share, attn_in, cos, sin, bias, *scalars))
    qkv_mine = gather_planes(qkv_plane)
    came = after(came, *qkv_plane)
    down_share = share(came, 3, 2 * deep)
    down_share = jnp.concatenate([down_share[:deep], down_share[deep:]], axis=1)[None]
    down_plane = gather_narrow(down_share)
    wide_share = jnp.concatenate([share(came, 2, 4 * rows), share(came, 1, rows)])
    wide_share = wide_share.reshape(UP_ROWS + 1, rows, HALF)
    wide_plane = gather_narrow(after(wide_share, *down_plane))
    qkv_other = flip(qkv_mine, "wide", 1)
    heads_mine = project(here, attn_in, qkv_mine, cos, sin)
    down_mine = gather_planes(after(down_plane, qkv_mine))
    before = attend(scalars[0], heads_mine, None, 0, 1)
    wide_mine = gather_planes(after(wide_plane, before[0], down_mine))
    before = attend(scalars[0], heads_mine, before, 1, 2)
    down_other = flip(after(down_mine, before[0]), "wide", 1)
    heads_other = project(here, after(attn_in, before[0]), qkv_other, cos, sin)
    before = attend(scalars[1], heads_other, before, 0, 2)
    wide_other = flip(after(wide_mine, before[0]), "wide", 1)
    attended, logs = attend(scalars[1], heads_other, before, 2, 1)
    output, mlp_in, act, pre_grad, resid_grad, resid_low, attended_grad, sums, up_sums = feed(
        levels,
        here,
        tokens,
        attended,
        cotangent,
        vec_master,
        bias,
        (wide_mine, wide_other, down_mine, down_other),
    )

    blocks = (1, 1) if plain else (planes, narrow)
    down_theirs = flip(grad_of_rows(blocks, act, cotangent, 4, 4), "wide", 1)
    wide_theirs = grad_of_wide(
        blocks, mlp_in, pre_grad, 4, attended, resid_low, 1 - side
    )
    wide_came = flip(wide_theirs, "wide", 1)
    down_grad = grad_of_rows(blocks, act, after(cotangent, wide_theirs), 0, 4, down_theirs)
    down_planes = reduce_planes(down_grad)
    wide_grad = grad_of_wide(
        blocks, mlp_in, after(pre_grad, down_grad), 0, attended, resid_low, side, wide_came
    )
    grad_other, qkv_theirs = attend_back(
        scalars[1], heads_other, attended, after(attended_grad, wide_grad), logs, cos, sin,
        attn_in, blocks,
    )
    wide_planes = reduce_planes(after(wide_grad, down_planes))
    down_pieces = narrow_pieces(down_planes)
    (grad_mine,) = attend_back(
        scalars[0], heads_mine, attended, after(attended_grad, qkv_theirs, down_planes), logs, cos, sin
    )
    qkv_grad = grad_of_columns(
        blocks, attn_in, after(grad_mine, wide_planes, *down_pieces), 0, 3,
        flip(qkv_theirs, "wide", 1),
    )
    wide_pieces = narrow_pieces(after(wide_planes, *down_pieces))
    qkv_planes = reduce_planes(after(qkv_grad, wide_planes))
    input_grad, gain_sums, table_grad = entry(
        levels, here, tokens, resid_grad, vec_master,
        (after(grad_mine, qkv_grad, *wide_pieces), grad_other),
        (qkv_mine, qkv_other),
    )
    qkv_pieces = narrow_pieces(after(qkv_planes, input_grad, *wide_pieces))
    up_sums = up_sums.sum(axis=0).reshape(2, UP_ROWS, HALF)
    up_sums = jnp.where(side == 1, up_sums[::-1], up_sums)
    up_sums = jnp.swapaxes(up_sums, 0, 1).reshape(UP_ROWS, D)
    vec_local = (
        jnp.concatenate(
            [
                gain_sums.sum(axis=0)[None],
                sums[:8].sum(axis=0)[None],
                sums[8:].sum(axis=0)[None],
                up_sums,
                table_grad,
            ],
            axis=0,
        )
        * row_scale
    )
    pieces = [jnp.stack(part) for part in (qkv_pieces, wide_pieces, down_pieces)]
    if plain:
        sent, squares = plain_settle(owners, *pieces)
        came = lax.all_to_all(sent, "wide", 0, 0)
        slot_grad = plain_unpack(kind, master_slots.shape[1], came)
        vec_sums = sum_over_wide(jnp.concatenate([vec_local, squares]))
        all_sums = gather_narrow(vec_sums)
    else:
        vec_wide = sum_over_wide(vec_local)
        sent = settle(owners, *pieces)
        came = lax.all_to_all(after(sent, vec_wide), "wide", 0, 0)
        all_sums = gather_narrow(square_sums(came, vec_wide))
        slot_grad = unpack(owners, master_slots.shape[1], came)
    all_sums = jnp.stack(all_sums)
    (
        master_new, moment_new, square_new,
        vec_grad, vec_moment_new, vec_square_new, vec_master_new, norm_value,
    ) = finish(
        owners, slot_grad, all_sums, (vec_moment, vec_square, vec_master),
        (moment_slots[0], square_slots[0], master_slots[0]),
    )
    return (
        output[None],
        input_grad[None],
        master_new[None],
        moment_new[None],
        square_new[None],
        vec_grad,
        vec_moment_new,
        vec_square_new,
        vec_master_new,
        norm_value.reshape(1),
    )


def solution(mesh):
    placed = (
        P(("wide", "narrow"), None, None),
        P(("wide", "narrow"), None, None),
        P(("wide", "narrow")),
        P(("wide", "narrow"), None),
        P(),
        P("wide", "narrow", None),
        P("wide", "narrow", None),
        P("wide", "narrow", None),
        P(),
        P(),
        P(),
    )
    return jax.shard_map(
        local,
        mesh=mesh,
        in_specs=placed,
        out_specs=(
            P(("wide", "narrow"), None, None),
            P(("wide", "narrow"), None, None),
            P("wide", "narrow", None),
            P("wide", "narrow", None),
            P("wide", "narrow", None),
            P(),
            P(),
            P(),
            P(),
            P(),
        ),
        check_vma=False,
    )
```

```python
from functools import partial

import jax
import jax.numpy as jnp
from jax import lax
from jax.experimental import pallas as pl
from jax.experimental.pallas import tpu as pltpu
from jax.sharding import PartitionSpec as P

D = 768
HEADS = 12
HEAD_DIM = 64
FF = 3072
BLOCK = 16
SEQ = 1024
LEVELS = 8
STEP = 10
ROWS = 2 * SEQ

ln_eps = 1e-05
learn_rate = 0.05
vector_rate = 0.5
decay_rate = 0.1
moment_decay = 0.5
adam_eps = 1e-08
masked_score = -1e30
rope_base = 10000.0
row_scale = 1.0 / (2 * SEQ)

TILE = 256
PAIR = 2 * HEAD_DIM
GROUPS = HEADS // 2
UP_ROWS = FF // D
VROWS = 3 + UP_ROWS + LEVELS
low = jnp.bfloat16
full = jnp.float32


def dot(a, b, dim_a=1, dim_b=0):
    return lax.dot_general(
        a, b, (((dim_a,), (dim_b,)), ((), ())), preferred_element_type=full
    )


def came_from(here, place, narrow):
    return lax.rem(here - place + narrow, narrow) if narrow > 1 else 0


anywhere = pl.BlockSpec(memory_space=pltpu.HBM)


def copies_in_order(source, target, here, semaphores):
    planes, narrow, _, rows, _ = source.shape
    found = []
    for place in range(narrow):
        for plane in range(planes):
            found.append(
                pltpu.make_async_copy(
                    source.at[plane, came_from(here, place, narrow)],
                    target.at[:, pl.ds((place * planes + plane) * rows, rows), :],
                    semaphores.at[place * planes + plane],
                )
            )
    return found


def all_copies(sources, targets, here, semaphores):
    found = []
    for index, (source, target) in enumerate(zip(sources, targets)):
        found += copies_in_order(source, target, here, semaphores.at[index])
    return found


def bring(sources, targets, here, semaphores):
    found = all_copies(sources, targets, here, semaphores)
    for copy in found:
        copy.start()
    for copy in found:
        copy.wait()


def ordered_shape(weight):
    planes, narrow, parts, rows, columns = weight.shape
    return (parts, planes * narrow * rows, columns)


def ordered_scratch(weights):
    return [pltpu.VMEM(ordered_shape(weight), low) for weight in weights] + [
        pltpu.SemaphoreType.DMA((len(weights), 16))
    ]


def side_by_side(ref, parts):
    return jnp.concatenate([ref[part] for part in parts], axis=1)


def params(limit=62):
    return pltpu.CompilerParams(vmem_limit_bytes=limit * 2**20)


def whole(shape):
    zeros = (0,) * len(shape)
    return pl.BlockSpec(shape, lambda *_: zeros, pipeline_mode=pl.Buffered(1))


def rows_of(width, rows=TILE):
    return pl.BlockSpec((rows, width), lambda i, *_: (i, 0))


def hidden_tile(levels_ref, tokens, vec_ref, sub=0, subs=1):
    count = tokens.shape[0]
    step = pl.program_id(0) * subs + sub
    per_tile = count // BLOCK
    first = lax.rem(step, SEQ // count) * per_tile
    rows = []
    for block in range(per_tile):
        level = levels_ref[first + block]
        row = vec_ref[pl.ds(3 + UP_ROWS + level, 1), :]
        rows.append(jnp.broadcast_to(row, (BLOCK, D)))
    embedding = jnp.concatenate(rows, axis=0)
    noised = step < SEQ // count
    return tokens.astype(full) + jnp.where(noised, embedding, 0.0)


def normalised(entries):
    centred = entries - jnp.mean(entries, axis=-1, keepdims=True)
    scaling = lax.rsqrt(jnp.mean(centred * centred, axis=-1, keepdims=True) + ln_eps)
    return centred * scaling, scaling


def norm_back(normed, scaling, gain, grad):
    inner = grad * gain
    return (
        inner
        - jnp.mean(inner, axis=-1, keepdims=True)
        - normed * jnp.mean(inner * normed, axis=-1, keepdims=True)
    ) * scaling


def eight_rows(entries):
    return entries.reshape(-1, 8, entries.shape[-1]).sum(axis=0)


def norm_one_kernel(levels_ref, tokens_ref, vec_ref, out_ref):
    normed, _ = normalised(hidden_tile(levels_ref, tokens_ref[...], vec_ref))
    out_ref[...] = (normed * vec_ref[0:1, :]).astype(low)


def norm_one(levels, tokens, vec_master):
    return pl.pallas_call(
        norm_one_kernel,
        grid_spec=pltpu.PrefetchScalarGridSpec(
            num_scalar_prefetch=1,
            grid=(ROWS // TILE,),
            in_specs=[rows_of(D), whole((VROWS, D))],
            out_specs=rows_of(D),
        ),
        out_shape=jax.ShapeDtypeStruct((ROWS, D), low),
        cost_estimate=pl.CostEstimate(
            flops=10 * ROWS * D, bytes_accessed=4 * ROWS * D, transcendentals=0
        ),
        compiler_params=params(),
        name="norm_one",
    )(levels, tokens, vec_master)


def turn(entries, cos, sin):
    return entries * cos + pltpu.roll(entries, HEAD_DIM, 1) * sin


PROJECT_TILE = 512


def project_kernel(pairs, place_ref, a_ref, w_hbm, cos_ref, sin_ref, out_ref, w_ref, semaphores):
    @pl.when(pl.program_id(0) == 0)
    def _():
        bring([w_hbm], [w_ref], place_ref[1], semaphores)

    weights = side_by_side(w_ref, range(3))
    for sub in range(PROJECT_TILE // TILE):
        rows = slice(sub * TILE, (sub + 1) * TILE)
        cos = cos_ref[rows, :]
        sin = sin_ref[rows, :]
        projected = dot(a_ref[rows, :], weights)
        for part in range(3):
            for pair in range(pairs):
                start = (part * pairs + pair) * PAIR
                columns = slice(start, start + PAIR)
                result = projected[:, columns]
                if part < 2:
                    result = turn(result, cos, sin)
                if part == 0:
                    result = result * HEAD_DIM**-0.5
                out_ref[rows, columns] = result.astype(low)


def project(places, attn_in, w_part, cos, sin):
    width = 3 * w_part.shape[4]
    table = pl.BlockSpec(
        (PROJECT_TILE, PAIR), lambda i, *_: (lax.rem(i, SEQ // PROJECT_TILE), 0)
    )
    return pl.pallas_call(
        partial(project_kernel, width // (3 * PAIR)),
        grid_spec=pltpu.PrefetchScalarGridSpec(
            num_scalar_prefetch=1,
            grid=(ROWS // PROJECT_TILE,),
            in_specs=[rows_of(D, PROJECT_TILE), anywhere, table, table],
            out_specs=rows_of(width, PROJECT_TILE),
            scratch_shapes=ordered_scratch([w_part]),
        ),
        out_shape=jax.ShapeDtypeStruct((ROWS, width), low),
        cost_estimate=pl.CostEstimate(
            flops=2 * ROWS * D * width, bytes_accessed=8 * ROWS * D, transcendentals=0
        ),
        compiler_params=params(),
        name="project",
    )(places, attn_in, w_part, cos, sin)


QT = 256
TILES = SEQ // QT
SHORTEST = 256


OWN = 128


def by_parts(left, right, dim_left, dim_right, joined):
    parts = []
    for start in range(0, QT, OWN):
        here = slice(start, start + OWN)
        chosen = left[here, :] if left.shape[0] == QT else left[:, here]
        parts.append(dot(chosen, right[here, :], dim_left, dim_right))
    return jnp.concatenate(parts, axis=joined)


def fill_bias(length, same_ref, earlier_ref, causal_ref, length_ref):
    key = lax.broadcasted_iota(jnp.int32, (QT, QT), 0)
    query = lax.broadcasted_iota(jnp.int32, (QT, QT), 1)
    key_block = key // BLOCK
    query_block = query // BLOCK
    for tile in range(TILES):
        kept = key + tile * QT < length
        own = kept | (key == query)
        own_key = (query // OWN) * OWN + lax.broadcasted_iota(jnp.int32, (QT, QT), 0) % OWN
        own_kept = (own_key + tile * QT < length) | (own_key == query)
        same = (own_key // BLOCK == query_block) & own_kept
        same_ref[tile] = jnp.where(same, 0.0, masked_score)[:OWN]
        earlier_ref[tile] = jnp.where((key_block < query_block) & kept, 0.0, masked_score)
        causal_ref[tile] = jnp.where((key_block <= query_block) & own, 0.0, masked_score)
    position = lax.broadcasted_iota(jnp.int32, (SEQ, QT), 0)
    length_ref[...] = jnp.where(position < length, 0.0, masked_score)


bias_scratch = [
    pltpu.VMEM((TILES, OWN, QT), full),
    pltpu.VMEM((TILES, QT, QT), full),
    pltpu.VMEM((TILES, QT, QT), full),
    pltpu.VMEM((SEQ, QT), full),
]


def segments(tile, noised):
    found = []
    if noised:
        found.append((tile * QT, QT, "same"))
        found.append((SEQ + tile * QT, QT, "earlier"))
    else:
        found.append((SEQ + tile * QT, QT, "causal"))
    before = tile * QT
    free = min(before, SHORTEST)
    if before > free:
        found.append((SEQ + free, before - free, "length"))
    if free > 0:
        found.append((SEQ, free, None))
    return found


def masked(scores, kind, tile, start, count, biases):
    same_ref, earlier_ref, causal_ref, length_ref = biases
    if kind == "same":
        return scores + same_ref[tile]
    if kind == "earlier":
        return scores + earlier_ref[tile]
    if kind == "causal":
        return scores + causal_ref[tile]
    if kind == "length":
        return scores + length_ref[start - SEQ : start - SEQ + count, :]
    return scores


def lane_masks(head, rows):
    lane = lax.broadcasted_iota(jnp.int32, (rows, PAIR), 1)
    halves = (lane // (HEAD_DIM // 2)) % 2 == head
    plain = lane // HEAD_DIM == head
    return halves, plain


def attend_kernel(aliased, scalar_ref, q_ref, k_ref, v_ref, *refs):
    o_ref, log_ref, *biases = refs[2:] if aliased else refs

    @pl.when(pl.program_id(0) == 0)
    def _():
        fill_bias(scalar_ref[0], *biases)

    units = [
        (head, tile, noised)
        for head in range(2)
        for tile in range(TILES)
        for noised in (True, False)
    ]

    def score(head, tile, noised):
        halves, _ = lane_masks(head, QT)
        row = tile * QT + (0 if noised else SEQ)
        query = jnp.where(halves, q_ref[row : row + QT, :], jnp.zeros((), low))
        parts = []
        for start, count, kind in segments(tile, noised):
            keys = k_ref[start : start + count, :]
            if kind == "same":
                scores = by_parts(keys, query, 1, 1, 1)
            else:
                scores = dot(keys, query, 1, 1)
            parts.append((start, count, masked(scores, kind, tile, start, count, biases)))
        return parts

    def weigh(head, tile, noised, parts):
        row = tile * QT + (0 if noised else SEQ)
        row_max = None
        for start, count, scores in parts:
            top = jnp.max(scores, axis=0, keepdims=True)
            row_max = top if row_max is None else jnp.maximum(row_max, top)
        total = None
        weights = []
        for start, count, scores in parts:
            expo = jnp.exp(scores - row_max)
            part_total = jnp.sum(expo, axis=0, keepdims=True)
            total = part_total if total is None else total + part_total
            weights.append((start, count, expo.astype(low)))
        log_ref[0, head : head + 1, row : row + QT] = row_max + jnp.log(total)
        return weights, total

    def finish(head, tile, noised, weights, total):
        _, plain = lane_masks(head, QT)
        row = tile * QT + (0 if noised else SEQ)
        attended = None
        for start, count, expo in weights:
            values = v_ref[start : start + count, :]
            if start < SEQ:
                product = by_parts(expo, values, 0, 0, 0)
            else:
                product = dot(expo, values, 0, 0)
            attended = product if attended is None else attended + product
        inverse = jnp.transpose(jnp.broadcast_to(1.0 / total, (PAIR, QT)))
        result = (attended * inverse).astype(low)
        o_ref[row : row + QT, :] = jnp.where(plain, result, o_ref[row : row + QT, :])

    parts = score(*units[0])
    held = None
    for index, unit in enumerate(units):
        following = score(*units[index + 1]) if index + 1 < len(units) else None
        weights = weigh(*unit, parts)
        if held is not None:
            finish(*held)
        held = (*unit, *weights)
        parts = following
    finish(*held)


def column_spec(offset):
    return pl.BlockSpec((ROWS, PAIR), lambda g, *_: (0, offset + g))


def pair_spec_from(first):
    return pl.BlockSpec((ROWS, PAIR), lambda g, scalars: (0, scalars[1] + first + g))


def log_spec_from(first):
    return pl.BlockSpec((1, 2, ROWS), lambda g, scalars: (scalars[1] + first + g, 0, 0))


pair_spec = pair_spec_from(0)
log_spec = log_spec_from(0)
PAIRS_SEEN = 1572864


def attend(scalars, qkv, before, first=0, count=None):
    pairs = qkv.shape[1] // (3 * PAIR)
    count = count or pairs
    aliased = before is not None
    kept = [pl.BlockSpec(memory_space=pl.ANY)] * 2 if aliased else []
    return pl.pallas_call(
        partial(attend_kernel, aliased),
        grid_spec=pltpu.PrefetchScalarGridSpec(
            num_scalar_prefetch=1,
            grid=(count,),
            in_specs=[
                column_spec(first), column_spec(pairs + first), column_spec(2 * pairs + first), *kept
            ],
            out_specs=[pair_spec_from(first), log_spec_from(first)],
            scratch_shapes=bias_scratch,
        ),
        out_shape=[
            jax.ShapeDtypeStruct((ROWS, D), low),
            jax.ShapeDtypeStruct((GROUPS, 2, ROWS), full),
        ],
        input_output_aliases={4: 0, 5: 1} if aliased else {},
        cost_estimate=pl.CostEstimate(
            flops=16 * PAIRS_SEEN * PAIR * count,
            bytes_accessed=8 * ROWS * PAIR * count,
            transcendentals=0,
        ),
        compiler_params=params(),
        name="attend",
    )(scalars, qkv, qkv, qkv, *(before or ()))


def attend_back_kernel(
    weighted, scalar_ref, q_ref, k_ref, v_ref, o_ref, grad_ref, log_ref, cos_ref, sin_ref, *refs
):
    a_ref, weight_ref = None, None
    if weighted:
        a_ref, grad_out_ref, weight_ref, *refs = refs
    else:
        grad_out_ref, *refs = refs
    q_acc, k_acc, v_acc, delta_acc, prob_ref, score_ref, own_prob_ref, own_score_ref = refs[:8]
    biases = refs[8:]

    @pl.when(pl.program_id(0) == 0)
    def _():
        fill_bias(scalar_ref[0], *biases)

    for row in range(0, ROWS, QT):
        product = o_ref[row : row + QT, :].astype(full) * grad_ref[row : row + QT, :].astype(full)
        turned = jnp.transpose(product)
        delta_acc[0:1, row : row + QT] = jnp.sum(turned[:HEAD_DIM], axis=0, keepdims=True)
        delta_acc[1:2, row : row + QT] = jnp.sum(turned[HEAD_DIM:], axis=0, keepdims=True)

    def products(head, tile, noised, start, count):
        halves, plain = lane_masks(head, QT)
        row = tile * QT + (0 if noised else SEQ)
        zero = jnp.zeros((), low)
        query = jnp.where(halves, q_ref[row : row + QT, :], zero)
        grad = jnp.where(plain, grad_ref[row : row + QT, :], zero)
        keys, values = k_ref[start : start + count, :], v_ref[start : start + count, :]
        if start < SEQ:
            return by_parts(keys, query, 1, 1, 1), by_parts(values, grad, 1, 1, 1)
        return dot(keys, query, 1, 1), dot(values, grad, 1, 1)

    def keep(head, tile, noised, start, count, kind, pair):
        row = tile * QT + (0 if noised else SEQ)
        scores, prob_grad = pair
        scores = masked(scores, kind, tile, start, count, biases)
        probs = jnp.exp(scores - log_ref[0, head : head + 1, row : row + QT])
        delta = delta_acc[head : head + 1, row : row + QT]
        score_grad = (probs * (prob_grad - delta)).astype(low)
        if kind == "same":
            own = slice(tile * OWN, (tile + 1) * OWN)
            own_prob_ref[own, :] = probs.astype(low)
            own_score_ref[own, :] = score_grad
        else:
            key = start - SEQ
            prob_ref[key : key + count, row : row + QT] = probs.astype(low)
            score_ref[key : key + count, row : row + QT] = score_grad

    def put(ref, row, mask, value):
        ref[row : row + QT, :] = jnp.where(mask, value, ref[row : row + QT, :])

    def sums(head, tile):
        halves, plain = lane_masks(head, QT)
        row = tile * QT
        rows, clean_rows = slice(row, row + QT), slice(SEQ + row, SEQ + row + QT)
        seen = (slice(row, SEQ), slice(SEQ + row, ROWS))
        own = slice(tile * OWN, (tile + 1) * OWN)
        own_prob, own_score = own_prob_ref[own, :], own_score_ref[own, :]
        put(v_acc, row, plain, by_parts(own_prob, grad_ref[rows, :], 1, 0, 0))
        put(k_acc, row, halves, by_parts(own_score, q_ref[rows, :], 1, 0, 0))
        put(
            v_acc, SEQ + row, plain,
            dot(prob_ref[rows, seen[0]], grad_ref[seen[0], :])
            + dot(prob_ref[rows, seen[1]], grad_ref[seen[1], :]),
        )
        put(
            k_acc, SEQ + row, halves,
            dot(score_ref[rows, seen[0]], q_ref[seen[0], :])
            + dot(score_ref[rows, seen[1]], q_ref[seen[1], :]),
        )
        keys = k_ref[SEQ : SEQ + row + QT, :]
        put(
            q_acc, row, halves,
            dot(score_ref[: row + QT, rows], keys, 0, 0)
            + by_parts(own_score, k_ref[rows, :], 0, 0, 0),
        )
        put(q_acc, SEQ + row, halves, dot(score_ref[: row + QT, clean_rows], keys, 0, 0))

    items = []
    for head in range(2):
        for tile in reversed(range(TILES)):
            for noised in (True, False):
                for start, count, kind in segments(tile, noised):
                    items.append((head, tile, noised, start, count, kind))
    waiting = []
    pair = products(*items[0][:5])
    for index, item in enumerate(items):
        following = None
        if index + 1 < len(items):
            following = products(*items[index + 1][:5])
        keep(*item, pair)
        pair = following
        if index + 1 == len(items) or items[index + 1][:2] != item[:2]:
            sums(*item[:2])
    for row in range(0, ROWS, QT):
        rows = slice(row, row + QT)
        cos = cos_ref[row % SEQ : row % SEQ + QT, :]
        sin = -sin_ref[row % SEQ : row % SEQ + QT, :]
        grad_out_ref[0, rows, :] = turn(q_acc[rows, :] * HEAD_DIM**-0.5, cos, sin).astype(low)
        grad_out_ref[1, rows, :] = turn(k_acc[rows, :], cos, sin).astype(low)
        grad_out_ref[2, rows, :] = v_acc[rows, :].astype(low)
    if weighted:
        parts = jnp.concatenate([grad_out_ref[part] for part in range(3)], axis=1)
        result = dot(a_ref[...], parts, 0, 0) * row_scale
        planes, narrow, _, rows, _ = weight_ref.shape
        for place in range(narrow):
            for plane in range(planes):
                start = (place * planes + plane) * rows
                for part in range(3):
                    block = result[start : start + rows, part * PAIR : (part + 1) * PAIR]
                    weight_ref[plane, place, part] = block.astype(low)


def attend_back(scalars, qkv, attended, grad, logs, cos, sin, attn_in=None, blocks=None):
    pairs = qkv.shape[1] // (3 * PAIR)
    table = whole((SEQ, PAIR))
    weighted = attn_in is not None
    out_specs = [pl.BlockSpec((3, ROWS, PAIR), lambda g, *_: (0, 0, g))]
    out_shape = [jax.ShapeDtypeStruct((3, ROWS, pairs * PAIR), low)]
    if weighted:
        shape = (*blocks, 3, D // (blocks[0] * blocks[1]))
        out_specs.append(pl.BlockSpec((*shape, PAIR), lambda g, *_: (0, 0, 0, 0, g)))
        out_shape.append(jax.ShapeDtypeStruct((*shape, pairs * PAIR), low))
    return pl.pallas_call(
        partial(attend_back_kernel, weighted),
        grid_spec=pltpu.PrefetchScalarGridSpec(
            num_scalar_prefetch=1,
            grid=(pairs,),
            in_specs=[
                column_spec(0), column_spec(pairs), column_spec(2 * pairs),
                pair_spec, pair_spec, log_spec, table, table,
                *([whole((ROWS, D))] if weighted else []),
            ],
            out_specs=out_specs,
            scratch_shapes=[
                pltpu.VMEM((ROWS, PAIR), full),
                pltpu.VMEM((ROWS, PAIR), full),
                pltpu.VMEM((ROWS, PAIR), full),
                pltpu.VMEM((8, ROWS), full),
                pltpu.VMEM((SEQ, ROWS), low),
                pltpu.VMEM((SEQ, ROWS), low),
                pltpu.VMEM((TILES * OWN, QT), low),
                pltpu.VMEM((TILES * OWN, QT), low),
                *bias_scratch,
            ],
        ),
        out_shape=out_shape,
        cost_estimate=pl.CostEstimate(
            flops=40 * PAIRS_SEEN * PAIR * pairs,
            bytes_accessed=16 * ROWS * PAIR * pairs,
            transcendentals=0,
        ),
        compiler_params=params(),
        name="attend_back",
    )(
        scalars, qkv, qkv, qkv, attended, grad, logs, cos, sin,
        *([attn_in] if weighted else []),
    )


root_two_pi = 0.7978845608028654
cubic = 0.044715


HALF = D // 2
FF_HALF = FF // 2


FEED_TILE = 512
SUB = 256


def feed_kernel(
    levels_ref, side_ref, tokens_ref, o_ref, dy_ref, vec_ref, bias_ref,
    wide_mine_hbm, wide_other_hbm, down_mine_hbm, down_other_hbm,
    y_ref, b_ref, gl_ref, du_ref, dr_ref, drb_ref, do_ref, sums_ref, upsum_ref,
    wide_mine, wide_other, down_mine, down_other, semaphores
):
    copies = all_copies(
        [wide_mine_hbm, wide_other_hbm, down_mine_hbm, down_other_hbm],
        [wide_mine, wide_other, down_mine, down_other],
        side_ref[1],
        semaphores,
    )

    @pl.when(pl.program_id(0) == 0)
    def _():
        for copy in copies:
            copy.start()
        sums_ref[...] = jnp.zeros_like(sums_ref)
        upsum_ref[...] = jnp.zeros_like(upsum_ref)
        for copy in copies[: len(copies) // 2]:
            copy.wait()

    swapped = side_ref[0] == 1
    gain = vec_ref[1:2, :]
    subs = FEED_TILE // SUB

    def in_order(mine, other):
        return jnp.concatenate(
            [jnp.where(swapped, other, mine), jnp.where(swapped, mine, other)], axis=1
        )

    def weights(part):
        wide_ref, down_ref = (wide_mine, down_mine) if part < 2 else (wide_other, down_other)
        inner = part % 2
        up = side_by_side(wide_ref, (inner * 2, inner * 2 + 1))
        return up, down_ref[0, inner * D : (inner + 1) * D, :]

    def head(sub):
        rows = slice(sub * SUB, (sub + 1) * SUB)
        attended = o_ref[rows, :]
        hidden = hidden_tile(levels_ref, tokens_ref[rows, :], vec_ref, sub, subs)
        resid = hidden + in_order(
            dot(attended, wide_mine[UP_ROWS]), dot(attended, wide_other[UP_ROWS])
        )
        normed, scaling = normalised(resid)
        mlp_in = (normed * gain).astype(low)
        b_ref[rows, :] = mlp_in
        return normed, scaling, mlp_in, resid + vec_ref[2:3, :]

    def products(sub, part, mlp_in):
        up, down = weights(part)
        rows = slice(sub * SUB, (sub + 1) * SUB)
        columns = slice(part * D, (part + 1) * D)
        return dot(mlp_in, up) + bias_ref[:, columns], dot(dy_ref[rows, :], down, 1, 1)

    def bend(sub, part, pre, act_grad):
        rows = slice(sub * SUB, (sub + 1) * SUB)
        columns = slice(part * D, (part + 1) * D)
        square = pre * pre
        bent = jnp.tanh(pre * (root_two_pi + (cubic * root_two_pi) * square))
        half = 0.5 + 0.5 * bent
        act = (pre * half).astype(low)
        slope = half + (0.5 * pre) * (1.0 - bent * bent) * (
            root_two_pi + (3.0 * cubic * root_two_pi) * square
        )
        pre_grad = act_grad * slope
        pre_low = pre_grad.astype(low)
        gl_ref[rows, columns] = act
        du_ref[rows, columns] = pre_low
        upsum_ref[:, columns] += eight_rows(pre_grad)
        return act, pre_low

    def main(sub, mlp_in, result):
        back = None
        ahead = products(sub, 0, mlp_in)
        for part in range(UP_ROWS):
            pair = ahead
            if part + 1 < UP_ROWS:
                ahead = products(sub, part + 1, mlp_in)
            act, pre_low = bend(sub, part, *pair)
            up, down = weights(part)
            result = result + dot(act, down)
            term = dot(pre_low, up, 1, 1)
            back = term if back is None else back + term
        return result, back

    def tail(sub, normed, scaling, result, back):
        rows = slice(sub * SUB, (sub + 1) * SUB)
        y_ref[rows, :] = result.astype(low)
        dy_full = dy_ref[rows, :].astype(full)
        sums_ref[0:8, :] += eight_rows(back * normed)
        sums_ref[8:16, :] += eight_rows(dy_full)
        resid_grad = dy_full + norm_back(normed, scaling, gain, back)
        dr_ref[rows, :] = resid_grad
        drb_ref[rows, :] = resid_grad.astype(low)
        first, second = resid_grad[:, :HALF], resid_grad[:, HALF:]
        mine = jnp.where(swapped, second, first).astype(low)
        other = jnp.where(swapped, first, second).astype(low)
        do_ref[rows, :] = (
            dot(mine, wide_mine[UP_ROWS], 1, 1) + dot(other, wide_other[UP_ROWS], 1, 1)
        ).astype(low)

    state = head(0)

    @pl.when(pl.program_id(0) == 0)
    def _():
        for copy in copies[len(copies) // 2 :]:
            copy.wait()

    for sub in range(subs):
        normed, scaling, mlp_in, result = state
        result, back = main(sub, mlp_in, result)
        if sub + 1 < subs:
            state = head(sub + 1)
        tail(sub, normed, scaling, result, back)


def feed(levels, side, tokens, attended, cotangent, vec_master, bias, weights):
    def out(width, kind=low):
        return jax.ShapeDtypeStruct((ROWS, width), kind)

    def rows(width):
        return rows_of(width, FEED_TILE)

    return pl.pallas_call(
        feed_kernel,
        grid_spec=pltpu.PrefetchScalarGridSpec(
            num_scalar_prefetch=2,
            grid=(ROWS // FEED_TILE,),
            in_specs=[
                rows(D), rows(D), rows(D), whole((VROWS, D)), whole((1, FF)), *[anywhere] * 4
            ],
            out_specs=[
                rows(D), rows(D), rows(FF), rows(FF), rows(D), rows(D), rows(D),
                pl.BlockSpec((16, D), lambda i, *_: (0, 0)),
                pl.BlockSpec((8, FF), lambda i, *_: (0, 0)),
            ],
            scratch_shapes=ordered_scratch(weights),
        ),
        out_shape=[
            out(D), out(D), out(FF), out(FF), out(D, full), out(D), out(D),
            jax.ShapeDtypeStruct((16, D), full), jax.ShapeDtypeStruct((8, FF), full),
        ],
        cost_estimate=pl.CostEstimate(
            flops=ROWS * D * (4 * D + 8 * FF), bytes_accessed=30 * ROWS * D, transcendentals=0
        ),
        compiler_params=params(),
        name="feed",
    )(levels, side, tokens, attended, cotangent, vec_master, bias, *weights)


def weight_kernel(added, scalar_ref, x_ref, y_ref, *refs):
    out_ref = refs[-1]
    result = dot(x_ref[...], y_ref[...], 0, 0) * row_scale
    planes, narrow, _, rows, _ = out_ref.shape
    for place in range(narrow):
        for plane in range(planes):
            start = (place * planes + plane) * rows
            block = result[start : start + rows]
            if added:
                block = block + refs[0][plane, place, 0].astype(full)
            out_ref[plane, place, 0] = block.astype(low)


def weight_call(name, count, x_spec, y_spec, out_spec, shape, first, x, y, added):
    return pl.pallas_call(
        partial(weight_kernel, added is not None),
        grid_spec=pltpu.PrefetchScalarGridSpec(
            num_scalar_prefetch=1,
            grid=(count,),
            in_specs=[x_spec, y_spec, *([out_spec] if added is not None else [])],
            out_specs=out_spec,
        ),
        out_shape=jax.ShapeDtypeStruct(shape, low),
        cost_estimate=pl.CostEstimate(
            flops=4 * ROWS * count * D * HALF, bytes_accessed=8 * ROWS * D, transcendentals=0
        ),
        compiler_params=params(),
        name=name,
    )(jnp.asarray(first, jnp.int32).reshape(1), x, y, *([added] if added is not None else []))


def grad_of_columns(blocks, x, y, first, count, added=None):
    planes, narrow = blocks
    rows = D // (planes * narrow)
    if y.ndim == 3:
        y_spec = pl.BlockSpec((None, ROWS, HALF), lambda j, s: (s[0] + j, 0, 0))
    else:
        y_spec = pl.BlockSpec((ROWS, HALF), lambda j, s: (0, s[0] + j))
    return weight_call(
        "grad_of_columns",
        count,
        pl.BlockSpec((ROWS, D), lambda j, s: (0, 0)),
        y_spec,
        pl.BlockSpec((planes, narrow, 1, rows, HALF), lambda j, s: (0, 0, j, 0, 0)),
        (planes, narrow, count, rows, HALF),
        first, x, y, added,
    )


def wide_kernel(added, side_ref, x_ref, y_ref, o_hbm, dr_hbm, *refs):
    out_ref, o_ref, dr_ref, semaphores = refs[-4:]
    step = pl.program_id(0)
    column = pl.multiple_of(side_ref[1] * HALF, HALF)
    copies = [
        pltpu.make_async_copy(o_hbm, o_ref, semaphores.at[0]),
        pltpu.make_async_copy(dr_hbm.at[:, pl.ds(column, HALF)], dr_ref, semaphores.at[1]),
    ]

    def store(result):
        planes, narrow, _, rows, _ = out_ref.shape
        for place in range(narrow):
            for plane in range(planes):
                start = (place * planes + plane) * rows
                block = result[start : start + rows] * row_scale
                if added:
                    block = block + refs[0][plane, place, 0].astype(full)
                out_ref[plane, place, 0] = block.astype(low)

    @pl.when(step == 0)
    def _():
        for copy in copies:
            copy.start()

    @pl.when(step < UP_ROWS)
    def _():
        store(dot(x_ref[...], y_ref[...], 0, 0))

    @pl.when(step == UP_ROWS)
    def _():
        for copy in copies:
            copy.wait()
        store(dot(o_ref[...], dr_ref[...], 0, 0))


def grad_of_wide(blocks, x, y, first, attended, resid_low, side, added=None):
    planes, narrow = blocks
    rows = D // (planes * narrow)
    count = UP_ROWS + 1
    out_spec = pl.BlockSpec((planes, narrow, 1, rows, HALF), lambda j, s: (0, 0, j, 0, 0))
    return pl.pallas_call(
        partial(wide_kernel, added is not None),
        grid_spec=pltpu.PrefetchScalarGridSpec(
            num_scalar_prefetch=1,
            grid=(count,),
            in_specs=[
                whole((ROWS, D)),
                pl.BlockSpec(
                    (ROWS, HALF), lambda j, s: (0, s[0] + jnp.minimum(j, UP_ROWS - 1))
                ),
                anywhere,
                anywhere,
                *([out_spec] if added is not None else []),
            ],
            out_specs=out_spec,
            scratch_shapes=[
                pltpu.VMEM((ROWS, D), low),
                pltpu.VMEM((ROWS, HALF), low),
                pltpu.SemaphoreType.DMA((2,)),
            ],
        ),
        out_shape=jax.ShapeDtypeStruct((planes, narrow, count, rows, HALF), low),
        cost_estimate=pl.CostEstimate(
            flops=4 * ROWS * count * D * HALF, bytes_accessed=8 * ROWS * D, transcendentals=0
        ),
        compiler_params=params(),
        name="grad_of_wide",
    )(
        jnp.stack([jnp.int32(first), side]), x, y, attended, resid_low,
        *([added] if added is not None else []),
    )


def grad_of_rows(blocks, x, y, first, count, added=None):
    planes, narrow = blocks
    if planes == 1:
        rows = HALF
        out_spec = pl.BlockSpec((1, 1, 1, rows, D), lambda i, s: (0, 0, 0, i, 0))
        shape = (1, 1, 1, count * HALF, D)
    else:
        rows = HALF // planes
        out_spec = pl.BlockSpec((planes, 1, 1, rows, D), lambda i, s: (0, i, 0, 0, 0))
        shape = (planes, count, 1, rows, D)
    return weight_call(
        "grad_of_rows",
        count,
        pl.BlockSpec((ROWS, HALF), lambda i, s: (0, s[0] + i)),
        pl.BlockSpec((ROWS, D), lambda i, s: (0, 0)),
        out_spec,
        shape,
        first, x, y, added,
    )


ENTRY_TILE = 512


def entry_kernel(count, levels_ref, place_ref, tokens_ref, dr_ref, vec_ref, *refs):
    step = pl.program_id(0)
    grads, sources = refs[:count], refs[count : 2 * count]
    grad_ref, gain_ref, table_ref = refs[2 * count : 2 * count + 3]
    weights, semaphores = refs[2 * count + 3 : -1], refs[-1]

    @pl.when(step == 0)
    def _():
        gain_ref[...] = jnp.zeros_like(gain_ref)
        table_ref[...] = jnp.zeros_like(table_ref)
        bring(sources, weights, place_ref[1], semaphores)

    matrices = [side_by_side(weight, range(3)) for weight in weights]
    per_tile = TILE // BLOCK
    subs = ENTRY_TILE // TILE
    for sub in range(subs):
        rows = slice(sub * TILE, (sub + 1) * TILE)
        back = None
        for grad, matrix in zip(grads, matrices):
            parts = jnp.concatenate([grad[part, rows, :] for part in range(3)], axis=1)
            term = dot(parts, matrix, 1, 1)
            back = term if back is None else back + term
        hidden = hidden_tile(levels_ref, tokens_ref[rows, :], vec_ref, sub, subs)
        normed, scaling = normalised(hidden)
        gain_ref[...] += eight_rows(back * normed)
        result = dr_ref[rows, :] + norm_back(normed, scaling, vec_ref[0:1, :], back)
        grad_ref[rows, :] = result

    @pl.when(step < SEQ // ENTRY_TILE)
    def _():
        for sub in range(subs):
            sums = grad_ref[sub * TILE : (sub + 1) * TILE, :]
            sums = sums.reshape(per_tile, BLOCK, D).sum(axis=1)
            for block in range(per_tile):
                level = levels_ref[(step * subs + sub) * per_tile + block]
                table_ref[pl.ds(level, 1), :] += sums[block : block + 1, :]


def entry(levels, places, tokens, resid_grad, vec_master, grads, weights):
    count = len(weights)
    return pl.pallas_call(
        partial(entry_kernel, count),
        grid_spec=pltpu.PrefetchScalarGridSpec(
            num_scalar_prefetch=2,
            grid=(ROWS // ENTRY_TILE,),
            in_specs=[rows_of(D, ENTRY_TILE), rows_of(D, ENTRY_TILE), whole((VROWS, D))]
            + [
                pl.BlockSpec((3, ENTRY_TILE, grad.shape[2]), lambda i, *_: (0, i, 0))
                for grad in grads
            ]
            + [anywhere] * count,
            out_specs=[
                rows_of(D, ENTRY_TILE),
                pl.BlockSpec((8, D), lambda i, *_: (0, 0)),
                pl.BlockSpec((LEVELS, D), lambda i, *_: (0, 0)),
            ],
            scratch_shapes=ordered_scratch(weights),
        ),
        out_shape=[
            jax.ShapeDtypeStruct((ROWS, D), full),
            jax.ShapeDtypeStruct((8, D), full),
            jax.ShapeDtypeStruct((LEVELS, D), full),
        ],
        cost_estimate=pl.CostEstimate(
            flops=6 * ROWS * D * D, bytes_accessed=20 * ROWS * D, transcendentals=0
        ),
        compiler_params=params(),
        name="entry",
    )(levels, places, tokens, resid_grad, vec_master, *grads, *weights)


PARTS = (3, 1, 4)


def swapped_halves(entries):
    lane = lax.broadcasted_iota(jnp.int32, entries.shape, 1) % PAIR
    quarter = HEAD_DIM // 2
    width = entries.shape[1]
    ahead = pltpu.roll(entries, width - quarter, 1)
    behind = pltpu.roll(entries, quarter, 1)
    second = (lane >= quarter) & (lane < 2 * quarter)
    third = (lane >= 2 * quarter) & (lane < 3 * quarter)
    return jnp.where(second, ahead, jnp.where(third, behind, entries))


def slot_pieces(kind, wide):
    planes = wide // 2
    found = []
    for plane in range(planes):
        for half in range(2):
            place = 2 * plane + half
            if kind < 3:
                parts, rows = PARTS[kind], D // 4 // planes
                for part in range(parts):
                    where = pl.ds(plane * rows * parts + part, rows, stride=parts)
                    found.append((place, part, part * rows, rows, where, half * HALF))
            else:
                rows = HALF // planes
                for column in range(2):
                    where = pl.ds(half * HALF + plane * rows, rows)
                    found.append((place, 2, column * rows, rows, where, column * HALF))
    return found


LANES = 128


def pack_kernel(owners_ref, slot_ref, out_ref, stage_ref):
    place = lax.axis_index("wide")
    wide = out_ref.shape[0]
    for index in range(D // LANES):
        stage_ref[index] = slot_ref[:, index * LANES : (index + 1) * LANES]
    for kind in range(4):

        @pl.when(owners_ref[kind] == place)
        def _(kind=kind):
            for target, part, start, rows, where, column in slot_pieces(kind, wide):
                for index in range(HALF // LANES):
                    block = stage_ref[column // LANES + index, where, :]
                    if kind == 0 and part < 2:
                        block = swapped_halves(block)
                    columns = slice(index * LANES, (index + 1) * LANES)
                    out_ref[target, start : start + rows, columns] = block.astype(low)


def pack(owners, slot):
    wide = lax.axis_size("wide")
    shape = (wide, 2 * D // wide, HALF)
    return pl.pallas_call(
        pack_kernel,
        grid_spec=pltpu.PrefetchScalarGridSpec(
            num_scalar_prefetch=1,
            grid=(1,),
            in_specs=[whole(slot.shape)],
            out_specs=whole(shape),
            scratch_shapes=[pltpu.VMEM((D // LANES, slot.shape[0], LANES), full)],
        ),
        out_shape=jax.ShapeDtypeStruct(shape, low),
        cost_estimate=pl.CostEstimate(
            flops=D * D, bytes_accessed=6 * D * D, transcendentals=0
        ),
        compiler_params=params(16),
        name="pack",
    )(owners, slot)


def settle_kernel(owners_ref, qkv_ref, wide_ref, down_ref, out_ref):
    squares = jnp.zeros((8, HALF), full)

    def summed(ref, part):
        result = ref[0, part].astype(full)
        for index in range(1, ref.shape[0]):
            result = result + ref[index, part].astype(full)
        return result.astype(low)

    out_ref[...] = jnp.zeros_like(out_ref)
    for kind in range(4):
        target = owners_ref[kind]
        for part in range((3, 1, 4, 1)[kind]):
            if kind == 0:
                share = summed(qkv_ref, part)
            elif kind < 3:
                share = summed(wide_ref, UP_ROWS if kind == 1 else part)
            else:
                share = summed(down_ref, 0)
            rows = share.shape[0]
            for column in range(share.shape[1] // HALF):
                block = share[:, column * HALF : (column + 1) * HALF]
                start = (part + column) * rows
                out_ref[target, start : start + rows, :] = block
                entries = block.astype(full)
                squares = squares + eight_rows(entries * entries)
    rest = jnp.sum(squares, keepdims=True)
    rows = out_ref.shape[1] - 16
    for index in range(3):
        term = rest.astype(low)
        rest = rest - term.astype(full)
        terms = jnp.broadcast_to(term, (16, LANES))
        columns = slice(index * LANES, (index + 1) * LANES)
        for target in range(out_ref.shape[0]):
            out_ref[target, rows:, columns] = terms


def square_sums_kernel(came_ref, vec_ref, out_ref):
    total = jnp.zeros((1, LANES), full)
    for source in range(came_ref.shape[0]):
        for index in reversed(range(3)):
            columns = slice(index * LANES, (index + 1) * LANES)
            total = total + came_ref[source, :, columns].astype(full)[0:1]
    out_ref[0:VROWS, :] = vec_ref[...]
    out_ref[VROWS:, :] = jnp.concatenate([total] * (D // LANES), axis=1)


def square_sums(came, vec_wide):
    wide, rows, _ = came.shape
    return pl.pallas_call(
        square_sums_kernel,
        grid=(1,),
        in_specs=[
            pl.BlockSpec((wide, 16, HALF), lambda i: (0, rows // 16 - 1, 0)),
            whole((VROWS, D)),
        ],
        out_specs=whole((VROWS + 1, D)),
        out_shape=jax.ShapeDtypeStruct((VROWS + 1, D), full),
        compiler_params=params(16),
        name="square_sums",
    )(came, vec_wide)


def settle(owners, qkv, wide_parts, down):
    wide = lax.axis_size("wide")
    shape = (wide, 2 * D // wide + 16, HALF)
    return pl.pallas_call(
        settle_kernel,
        grid_spec=pltpu.PrefetchScalarGridSpec(
            num_scalar_prefetch=1,
            grid=(1,),
            in_specs=[whole(qkv.shape), whole(wide_parts.shape), whole(down.shape)],
            out_specs=whole(shape),
        ),
        out_shape=jax.ShapeDtypeStruct(shape, low),
        cost_estimate=pl.CostEstimate(
            flops=4 * D * D, bytes_accessed=6 * D * D, transcendentals=0
        ),
        compiler_params=params(16),
        name="settle",
    )(owners, qkv, wide_parts, down)


FINISH_ROWS = 192
held = pl.BlockSpec(memory_space=pltpu.VMEM)


def unpack_kernel(owners_ref, came_ref, out_ref, grad_ref):
    place = lax.axis_index("wide")
    wide = came_ref.shape[0]
    for kind in range(4):

        @pl.when(owners_ref[kind] == place)
        def _(kind=kind):
            for source, part, start, rows, where, column in slot_pieces(kind, wide):
                block = came_ref[source, start : start + rows, :].astype(full)
                for index in range(HALF // LANES):
                    piece = block[:, index * LANES : (index + 1) * LANES]
                    if kind == 0 and part < 2:
                        piece = swapped_halves(piece)
                    grad_ref[column // LANES + index, where, :] = piece

    for index in range(D // LANES):
        out_ref[:, index * LANES : (index + 1) * LANES] = grad_ref[index]


def unpack(owners, slot_rows, came):
    return pl.pallas_call(
        unpack_kernel,
        grid_spec=pltpu.PrefetchScalarGridSpec(
            num_scalar_prefetch=1,
            grid=(1,),
            in_specs=[whole(came.shape)],
            out_specs=held,
            scratch_shapes=[pltpu.VMEM((D // LANES, slot_rows, LANES), full)],
        ),
        out_shape=jax.ShapeDtypeStruct((slot_rows, D), full),
        cost_estimate=pl.CostEstimate(
            flops=2 * D * D, bytes_accessed=6 * D * D, transcendentals=0
        ),
        compiler_params=params(16),
        name="unpack",
    )(owners, came)


def finish_kernel(
    owners_ref, grad_ref, sums_ref, vec_moment_ref, vec_square_ref, vec_master_ref,
    moment_ref, square_ref, master_ref,
    master_out, moment_out, square_out, vec_grad_out, vec_moment_out, vec_square_out,
    vec_master_out, norm_out
):
    step = pl.program_id(0)
    place = lax.axis_index("wide")
    here = lax.axis_index("narrow")
    narrow = sums_ref.shape[0]
    total = sums_ref[here]
    for index in range(1, narrow):
        total = total + sums_ref[lax.rem(here - index + narrow, narrow)]
    vec, total = total[:VROWS], total[VROWS:, 0:1]
    norm = jnp.sqrt(total + jnp.sum(vec * vec, keepdims=True))
    clip = jnp.minimum(1.0, 1.0 / (norm + 1e-06))

    @pl.when(step == 0)
    def _():
        norm_out[...] = norm
        vec_clipped = vec * clip
        vec_grad_out[...] = vec_clipped
        vec_moment_out[...], vec_square_out[...], vec_master_out[...] = adam(
            vec_clipped, vec_moment_ref[...], vec_square_ref[...], vec_master_ref[...],
            0.0, vector_rate,
        )

    used = jnp.int32(0)
    for kind in range(4):
        rows = D // 4 * (PARTS[kind] if kind < 3 else 4)
        used = jnp.where(owners_ref[kind] == place, rows, used)
    row = step * FINISH_ROWS + lax.broadcasted_iota(jnp.int32, (FINISH_ROWS, D), 0)
    rows = pl.ds(pl.multiple_of(step * FINISH_ROWS, FINISH_ROWS), FINISH_ROWS)
    kept = row < used
    moment_new, square_new, master_new = adam(
        jnp.where(kept, grad_ref[rows, :] * clip, 0.0),
        moment_ref[rows, :], square_ref[rows, :], master_ref[rows, :], decay_rate, learn_rate,
    )
    master_out[...] = jnp.where(kept, master_new, 0.0)
    moment_out[...] = jnp.where(kept, moment_new, 0.0)
    square_out[...] = jnp.where(kept, square_new, 0.0)


def finish(owners, grad, sums, vec_states, states):
    rows = states[0].shape[0]
    state_spec = pl.BlockSpec((FINISH_ROWS, D), lambda i, *_: (i, 0))
    vec_spec = whole((VROWS, D))
    state = jax.ShapeDtypeStruct((rows, D), full)
    vec = jax.ShapeDtypeStruct((VROWS, D), full)
    return pl.pallas_call(
        finish_kernel,
        grid_spec=pltpu.PrefetchScalarGridSpec(
            num_scalar_prefetch=1,
            grid=(rows // FINISH_ROWS,),
            in_specs=[held, held, *[vec_spec] * 3, *[held] * 3],
            out_specs=[*[state_spec] * 3, *[vec_spec] * 4, whole((1, 1))],
        ),
        out_shape=[state] * 3 + [vec] * 4 + [jax.ShapeDtypeStruct((1, 1), full)],
        cost_estimate=pl.CostEstimate(
            flops=20 * D * D, bytes_accessed=26 * D * D, transcendentals=0
        ),
        compiler_params=params(24),
        name="finish",
    )(owners, grad, sums, *vec_states, *states)


def turn_tables():
    positions = jnp.arange(SEQ, dtype=jnp.int32).astype(full)
    exponents = jnp.arange(HEAD_DIM // 2, dtype=full) * (2.0 / HEAD_DIM)
    angles = positions[:, None] * (rope_base ** (-exponents))[None, :]
    cos = jnp.cos(angles)
    sin = jnp.sin(angles)
    return (
        jnp.concatenate([cos, cos, cos, cos], axis=1),
        jnp.concatenate([-sin, -sin, sin, sin], axis=1),
    )


def adam(grad, moment, square, master, decay, rate):
    moment_new = moment_decay * moment + (1.0 - moment_decay) * grad
    square_new = moment_decay * square + (1.0 - moment_decay) * grad * grad
    correction = 1.0 - moment_decay**STEP
    master_new = master * (1.0 - rate * decay) - rate * (moment_new / correction) / (
        jnp.sqrt(square_new / correction) + adam_eps
    )
    return (moment_new, square_new, master_new)


def flip(value, axis, bits):
    count = lax.axis_size(axis)
    return lax.ppermute(value, axis, [(i, i ^ bits) for i in range(count)])


def planes_groups():
    count = lax.axis_size("wide")
    return [list(range(start, count, 2)) for start in range(2)]


def shift(value, step):
    count = lax.axis_size("narrow")
    return lax.ppermute(value, "narrow", [(i, (i + step) % count) for i in range(count)])


def swap_planes(blocks):
    return lax.all_to_all(blocks, "wide", 0, 0, axis_index_groups=planes_groups())


def copies(value, count):
    return jnp.broadcast_to(value[None], (count, *value.shape))


def after(value, *others):
    return lax.optimization_barrier((value, *others))[0]


def gather_narrow(share):
    return [share] + [shift(share, step) for step in range(1, lax.axis_size("narrow"))]


def gather_planes(held):
    held = swap_planes(copies(jnp.stack(held), lax.axis_size("wide") // 2))
    if held.shape[3] % 16 == 0:
        return held
    narrow, parts, columns = held.shape[1], held.shape[2], held.shape[4]
    order = (lax.axis_index("narrow") - jnp.arange(narrow)) % narrow
    held = jnp.take(held, order, axis=1)
    return held.transpose(2, 1, 0, 3, 4).reshape(1, 1, parts, -1, columns)


def total(blocks):
    return jnp.sum(blocks.astype(full), axis=0).astype(low)


def reduce_planes(matrix):
    planes, narrow = lax.axis_size("wide") // 2, lax.axis_size("narrow")
    if matrix.shape[0] != planes:
        parts, columns = matrix.shape[2], matrix.shape[4]
        matrix = matrix.reshape(parts, narrow, planes, -1, columns)
        matrix = matrix.transpose(2, 1, 0, 3, 4)
    return total(swap_planes(matrix))


def narrow_pieces(held):
    count = lax.axis_size("narrow")
    place = lax.axis_index("narrow")

    def part(step):
        return lax.dynamic_index_in_dim(held, (place + step) % count, 0, keepdims=False)

    return [part(0)] + [shift(part(step), step) for step in range(1, count)]


def swap_halves(matrix):
    pairs = matrix.reshape(*matrix.shape[:-1], -1, 2, 2, HEAD_DIM // 2)
    return jnp.swapaxes(pairs, -3, -2).reshape(matrix.shape)


def plain_layouts(slot_rows):
    wide = lax.axis_size("wide")
    planes, most = wide // 2, 2 * D // wide
    rows, deep = D // 4 // planes, HALF // planes

    def pack_columns(kind, slot):
        parts = PARTS[kind]
        blocks = slot[: rows * planes * parts].reshape(planes, rows, parts, 2, HALF)
        blocks = blocks.transpose(0, 3, 2, 1, 4)
        if kind == 0:
            blocks = jnp.concatenate([swap_halves(blocks[:, :, :2]), blocks[:, :, 2:]], axis=2)
        blocks = blocks.reshape(wide, parts * rows, HALF)
        return jnp.pad(blocks, ((0, 0), (0, most - parts * rows), (0, 0)))

    def unpack_columns(kind, blocks):
        parts = PARTS[kind]
        blocks = blocks[:, : parts * rows].reshape(planes, 2, parts, rows, HALF)
        if kind == 0:
            blocks = jnp.concatenate([swap_halves(blocks[:, :, :2]), blocks[:, :, 2:]], axis=2)
        flat = blocks.transpose(0, 3, 2, 1, 4).reshape(planes * rows * parts, D)
        return jnp.pad(flat, ((0, slot_rows - flat.shape[0]), (0, 0)))

    def pack_down(slot):
        blocks = slot.reshape(2, planes, deep, 2, HALF)
        return blocks.transpose(1, 0, 3, 2, 4).reshape(wide, 2 * deep, HALF)

    def unpack_down(blocks):
        blocks = blocks.reshape(planes, 2, 2, deep, HALF)
        return blocks.transpose(1, 0, 3, 2, 4).reshape(slot_rows, D)

    packs = [partial(pack_columns, kind) for kind in range(3)] + [pack_down]
    unpacks = [partial(unpack_columns, kind) for kind in range(3)] + [unpack_down]
    packs.append(lambda slot: jnp.zeros((wide, most, HALF), slot.dtype))
    unpacks.append(lambda blocks: jnp.zeros((slot_rows, D), blocks.dtype))
    return packs, unpacks


def plain_pack(kind, slot):
    return lax.switch(kind, plain_layouts(slot.shape[0])[0], slot.astype(low))


def plain_settle(owners, qkv, wide_parts, down):
    wide = lax.axis_size("wide")
    qkv, wide_parts, down = total(qkv), total(wide_parts), total(down)
    down = jnp.stack([down[0, :, :HALF], down[0, :, HALF:]])
    places = jnp.arange(wide, dtype=jnp.int32)[:, None, None]
    sent = jnp.zeros((wide, 2 * D // wide, HALF), low)
    squares = jnp.zeros((), full)
    shares = (qkv, wide_parts[UP_ROWS:], wide_parts[:UP_ROWS], down)
    for kind, share in enumerate(shares):
        share = share.reshape(-1, HALF)
        squares = squares + jnp.sum(jnp.square(share.astype(full)))
        block = jnp.pad(share, ((0, sent.shape[1] - share.shape[0]), (0, 0)))[None]
        sent = jnp.where(places == owners[kind], block, sent)
    return sent, jnp.broadcast_to(squares, (1, D))


def plain_unpack(kind, slot_rows, came):
    return lax.switch(kind, plain_layouts(slot_rows)[1], came).astype(full)


def sum_over_wide(value):
    wide = lax.axis_size("wide")
    bit = 1
    while bit < wide:
        value = value + flip(value, "wide", bit)
        bit *= 2
    return value


def local(
    tokens,
    cotangent,
    lengths,
    levels,
    owners,
    master_slots,
    moment_slots,
    square_slots,
    vec_master,
    vec_moment,
    vec_square,
):
    narrow = lax.axis_size("narrow")
    wide = lax.axis_size("wide")
    side = lax.axis_index("wide") & 1
    planes = wide // 2
    rows = D // (narrow * planes)
    deep = FF // 2 // (narrow * planes)

    plain = rows % 16 != 0
    owned = owners == lax.axis_index("wide")
    kind = jnp.where(jnp.any(owned), jnp.argmax(owned), 4).astype(jnp.int32)
    if plain:
        packed = plain_pack(kind, master_slots[0])
    else:
        packed = pack(owners, master_slots[0])
    came = lax.all_to_all(packed, "wide", 0, 0)

    def share(came, kind, count):
        return lax.dynamic_index_in_dim(came, owners[kind], 0, keepdims=False)[:count]

    qkv_share = share(came, 0, 3 * rows).reshape(3, rows, HALF)

    tokens = tokens.reshape(ROWS, D)
    cotangent = cotangent.reshape(ROWS, D)
    levels = levels.reshape(-1)
    here = jnp.stack([side, lax.axis_index("narrow")]).astype(jnp.int32)
    cos, sin = turn_tables()
    bias = vec_master[3 : 3 + UP_ROWS].reshape(UP_ROWS, 2, HALF)
    bias = jnp.stack([bias[:, 0], bias[:, 1]])
    bias = jnp.where(side == 1, bias[::-1], bias).reshape(1, FF)
    half_pairs = GROUPS // 2
    scalars = [
        jnp.stack([lengths[0], half_pairs * half]) for half in (side, 1 - side)
    ]
    attn_in = norm_one(levels, tokens, vec_master)

    qkv_plane = gather_narrow(after(qkv_share, attn_in, cos, sin, bias, *scalars))
    qkv_mine = gather_planes(qkv_plane)
    came = after(came, *qkv_plane)
    down_share = share(came, 3, 2 * deep)
    down_share = jnp.concatenate([down_share[:deep], down_share[deep:]], axis=1)[None]
    down_plane = gather_narrow(down_share)
    wide_share = jnp.concatenate([share(came, 2, 4 * rows), share(came, 1, rows)])
    wide_share = wide_share.reshape(UP_ROWS + 1, rows, HALF)
    wide_plane = gather_narrow(after(wide_share, *down_plane))
    qkv_other = flip(qkv_mine, "wide", 1)
    heads_mine = project(here, attn_in, qkv_mine, cos, sin)
    down_mine = gather_planes(after(down_plane, qkv_mine))
    before = attend(scalars[0], heads_mine, None, 0, 1)
    wide_mine = gather_planes(after(wide_plane, before[0], down_mine))
    before = attend(scalars[0], heads_mine, before, 1, 2)
    down_other = flip(after(down_mine, before[0]), "wide", 1)
    heads_other = project(here, after(attn_in, before[0]), qkv_other, cos, sin)
    before = attend(scalars[1], heads_other, before, 0, 2)
    wide_other = flip(after(wide_mine, before[0]), "wide", 1)
    attended, logs = attend(scalars[1], heads_other, before, 2, 1)
    output, mlp_in, act, pre_grad, resid_grad, resid_low, attended_grad, sums, up_sums = feed(
        levels,
        here,
        tokens,
        attended,
        cotangent,
        vec_master,
        bias,
        (wide_mine, wide_other, down_mine, down_other),
    )

    blocks = (1, 1) if plain else (planes, narrow)
    down_theirs = flip(grad_of_rows(blocks, act, cotangent, 4, 4), "wide", 1)
    wide_theirs = grad_of_wide(
        blocks, mlp_in, pre_grad, 4, attended, resid_low, 1 - side
    )
    wide_came = flip(wide_theirs, "wide", 1)
    down_grad = grad_of_rows(blocks, act, after(cotangent, wide_theirs), 0, 4, down_theirs)
    down_planes = reduce_planes(down_grad)
    wide_grad = grad_of_wide(
        blocks, mlp_in, after(pre_grad, down_grad), 0, attended, resid_low, side, wide_came
    )
    grad_other, qkv_theirs = attend_back(
        scalars[1], heads_other, attended, after(attended_grad, wide_grad), logs, cos, sin,
        attn_in, blocks,
    )
    wide_planes = reduce_planes(after(wide_grad, down_planes))
    down_pieces = narrow_pieces(down_planes)
    (grad_mine,) = attend_back(
        scalars[0], heads_mine, attended, after(attended_grad, qkv_theirs, down_planes), logs, cos, sin
    )
    qkv_grad = grad_of_columns(
        blocks, attn_in, after(grad_mine, wide_planes, *down_pieces), 0, 3,
        flip(qkv_theirs, "wide", 1),
    )
    wide_pieces = narrow_pieces(after(wide_planes, *down_pieces))
    qkv_planes = reduce_planes(after(qkv_grad, wide_planes))
    input_grad, gain_sums, table_grad = entry(
        levels, here, tokens, resid_grad, vec_master,
        (after(grad_mine, qkv_grad, *wide_pieces), grad_other),
        (qkv_mine, qkv_other),
    )
    qkv_pieces = narrow_pieces(after(qkv_planes, input_grad, *wide_pieces))
    up_sums = up_sums.sum(axis=0).reshape(2, UP_ROWS, HALF)
    up_sums = jnp.where(side == 1, up_sums[::-1], up_sums)
    up_sums = jnp.swapaxes(up_sums, 0, 1).reshape(UP_ROWS, D)
    vec_local = (
        jnp.concatenate(
            [
                gain_sums.sum(axis=0)[None],
                sums[:8].sum(axis=0)[None],
                sums[8:].sum(axis=0)[None],
                up_sums,
                table_grad,
            ],
            axis=0,
        )
        * row_scale
    )
    pieces = [jnp.stack(part) for part in (qkv_pieces, wide_pieces, down_pieces)]
    if plain:
        sent, squares = plain_settle(owners, *pieces)
        came = lax.all_to_all(sent, "wide", 0, 0)
        slot_grad = plain_unpack(kind, master_slots.shape[1], came)
        vec_sums = sum_over_wide(jnp.concatenate([vec_local, squares]))
        all_sums = gather_narrow(vec_sums)
    else:
        vec_wide = sum_over_wide(vec_local)
        sent = settle(owners, *pieces)
        came = lax.all_to_all(after(sent, vec_wide), "wide", 0, 0)
        all_sums = gather_narrow(square_sums(came, vec_wide))
        slot_grad = unpack(owners, master_slots.shape[1], came)
    all_sums = jnp.stack(all_sums)
    (
        master_new, moment_new, square_new,
        vec_grad, vec_moment_new, vec_square_new, vec_master_new, norm_value,
    ) = finish(
        owners, slot_grad, all_sums, (vec_moment, vec_square, vec_master),
        (moment_slots[0], square_slots[0], master_slots[0]),
    )
    return (
        output[None],
        input_grad[None],
        master_new[None],
        moment_new[None],
        square_new[None],
        vec_grad,
        vec_moment_new,
        vec_square_new,
        vec_master_new,
        norm_value.reshape(1),
    )


def solution(mesh):
    placed = (
        P(("wide", "narrow"), None, None),
        P(("wide", "narrow"), None, None),
        P(("wide", "narrow")),
        P(("wide", "narrow"), None),
        P(),
        P("wide", "narrow", None),
        P("wide", "narrow", None),
        P("wide", "narrow", None),
        P(),
        P(),
        P(),
    )
    return jax.shard_map(
        local,
        mesh=mesh,
        in_specs=placed,
        out_specs=(
            P(("wide", "narrow"), None, None),
            P(("wide", "narrow"), None, None),
            P("wide", "narrow", None),
            P("wide", "narrow", None),
            P("wide", "narrow", None),
            P(),
            P(),
            P(),
            P(),
            P(),
        ),
        check_vma=False,
    )
```
